32 devices in a mesh: ctx: 4 (over y, core), exp: 8 (over z, x).
Axes of the slice: x: 2, y: 2, z: 4, core: 2. Of those that a mesh axis runs over, the one named last changes fastest.
Arguments:
- layer_input: bfloat16 [8, 1024, 1536], P('exp', 'ctx'), may hold values from -6 to 6
- attn_gain: float32 [1536], replicated, may hold values from 0.1 to 1.9
- w_query: bfloat16 [1536, 1536], replicated, may hold values from -0.3125 to 0.3125
- w_key: bfloat16 [1536, 512], replicated, may hold values from -0.15625 to 0.15625
- w_value: bfloat16 [1536, 512], replicated, may hold values from -0.15625 to 0.15625
- w_out: bfloat16 [1536, 1536], replicated, may hold values from -1.25 to 1.25
- ffn_gain: float32 [1536], replicated, may hold values from 0.1 to 1.9
- shared_gate: bfloat16 [1536, 1024], replicated, may hold values from -0.15625 to 0.15625
- shared_up: bfloat16 [1536, 1024], replicated, may hold values from -0.15625 to 0.15625
- shared_down: bfloat16 [1024, 1536], replicated, may hold values from -0.1875 to 0.1875
- expert_gate: bfloat16 [16, 1536, 512], P('exp'), may hold values from -0.15625 to 0.15625
- expert_up: bfloat16 [16, 1536, 512], P('exp'), may hold values from -0.15625 to 0.15625
- expert_down: bfloat16 [16, 512, 1536], P('exp'), may hold values from -0.5 to 0.5
- routes: int32 [8, 1024, 6], P('exp', 'ctx'), may hold values from 0 to 15, all different within a row; in each aligned block of 256 rows (0 to 255, 256 to 511, ..., all dimensions but the last counted through in order) at most 192 rows name the same one
- gate_logits: float32 [8, 1024, 6], P('exp', 'ctx'), may hold values from -3 to 3
- span_order: int32 [8], replicated, may hold values from 0 to 7, each once
- cotangent: bfloat16 [8, 1024, 1536], P('exp', 'ctx'), may hold values from -6 to 6
Outputs:
- layer_output: bfloat16 [8, 1024, 1536], P('exp', 'ctx')
- input_grad: float32 [8, 1024, 1536], P('exp', 'ctx')
- attn_gain_grad: float32 [1536], P(('ctx', 'exp'))
- w_query_grad: float32 [1536, 1536], P(('ctx', 'exp'))
- w_key_grad: float32 [1536, 512], P(('ctx', 'exp'))
- w_value_grad: float32 [1536, 512], P(('ctx', 'exp'))
- w_out_grad: float32 [1536, 1536], P(('ctx', 'exp'))
- ffn_gain_grad: float32 [1536], P(('ctx', 'exp'))
- shared_gate_grad: float32 [1536, 1024], P(('ctx', 'exp'))
- shared_up_grad: float32 [1536, 1024], P(('ctx', 'exp'))
- shared_down_grad: float32 [1024, 1536], P(('ctx', 'exp'))
- expert_gate_grad: float32 [16, 1536, 512], P('exp', 'ctx')
- expert_up_grad: float32 [16, 1536, 512], P('exp', 'ctx')
- expert_down_grad: float32 [16, 512, 1536], P('exp', None, 'ctx')
The draws below stay inside these ranges and needn't reach their ends.
Inputs may be any that keep to these rules, and one draw needn't show every extreme that they name: `routes`: each row names 6 different experts. In each aligned block of 256 rows (the rows of one device) no expert is named by more than 192 rows, a bound that some block reaches. `span_order`: each number appears once; entry c gives which block of 128 consecutive positions the c-th block of stored rows holds.
All inputs are finite; a program needn't handle non-finite values.
Results may differ from the reference program's by a relative error of at most 0.02.
Values may be sent and summed in bfloat16 or wider, within the bound.
No kernel may reach another device: no remote copies, remote signals or barrier semaphores. Data moves between devices by JAX's collectives and lax.ppermute only.
A program may use at most 320 MiB of HBM per device.

```python
import math
import jax
import jax.numpy as jnp
import numpy as np
from jax import lax

D = 1536
H = 12
HD = 128
KVH = 4
FS = 1024
FE = 512
TOP = 6
TOK_DEV = 256
SEQ_LEN = 1024
SEQS = 8
EXPERTS = 16
CAP = 192
N_CTX = 4


def raised(drawn, rng, source, target, blocks, factor):
    def block_of(dim):
        return (jnp.arange(drawn.shape[dim]) // (drawn.shape[dim] // blocks)).reshape((-1,) + (1,) * (drawn.ndim - 1 - dim))

    near = jax.random.permutation(rng, blocks)[block_of(target)]
    other_side = (block_of(target) + blocks // 2) % blocks
    return jnp.where((block_of(source) == near) | (block_of(source) == other_side), factor * drawn, drawn)


def block_levels(own_key, dims, pieces, smallest, top_value):
    loudness = 1.0
    for axis_at, parts in pieces:
        draws = jax.random.uniform(jax.random.fold_in(jax.random.fold_in(own_key, 6), axis_at), (parts,), jnp.float32, smallest / len(pieces), top_value / len(pieces))
        loudness = loudness * jnp.repeat(jnp.exp(draws), dims[axis_at] // parts).reshape((-1,) + (1,) * (len(dims) - 1 - axis_at))
    return loudness


def routed_block(stream_key, own, number, rows, amount, top, bound, skew):
    sequence = jax.random.permutation(stream_key, amount)
    packed, ordinary = shares(amount, rows * top, bound, skew, True), shares(amount, rows * top, bound, skew, False)
    places = jnp.arange(amount)

    def named(sizes, offset_by):
        used = int((sizes > 0).sum())
        fixed = max(1, used // 4)
        passed = fixed + (places - fixed + offset_by * (used - fixed)) % max(1, amount - fixed)
        return jnp.zeros((amount,), jnp.int32).at[sequence[jnp.where(places < fixed, places, passed)]].set(jnp.asarray(sizes, jnp.int32))

    sizes = jnp.where(number % 4 == 0, named(packed, number // 4), named(ordinary, number - number // 4 - 1))
    mixed = jax.random.permutation(jax.random.fold_in(own, 3), amount)
    donor, receiver = mixed[0:amount // 2 * 2:2], mixed[1:amount // 2 * 2:2]
    slack = jnp.minimum(sizes[donor] - 1, bound - sizes[receiver]) // 2
    slack = jnp.where((donor == sequence[0]) | (receiver == sequence[0]) | (sizes[receiver] == 0), 0, jnp.maximum(slack, 0))
    passed = jax.random.randint(jax.random.fold_in(own, 4), (amount // 2,), 0, 1 << 20) % (slack + 1)
    sizes = sizes.at[donor].add(-passed).at[receiver].add(passed)
    items = jnp.searchsorted(jnp.cumsum(sizes), jnp.arange(rows * top), side="right").astype(jnp.int32)
    listing = items.reshape(top, rows).T
    listing = listing[jax.random.permutation(jax.random.fold_in(own, 1), rows)]
    offset_by = jax.random.randint(jax.random.fold_in(own, 2), (rows, 1), 0, top)
    return jnp.take_along_axis(listing, (jnp.arange(top)[None, :] + offset_by) % top, axis=1)


def shares(amount, total, most, skew, full):
    weights = [(1 << 20) // math.isqrt(standing ** skew) + 1 for standing in range(1, amount + 1)]
    largest = most if full else min(most, max(-(-total // amount), total * weights[0] // sum(weights)))
    least = 1 if total - largest >= amount - 1 else 0
    given, rest = [largest] + [least] * (amount - 1), total - largest - least * (amount - 1)
    while rest > 0:
        movable = [i for i in range(1, amount) if given[i] < largest] or [i for i in range(1, amount) if given[i] < most]
        whole, left = sum([weights[i] for i in movable]), rest
        for i in movable:
            more = min(most - given[i], max(1, left * weights[i] // whole), rest)
            given[i] = given[i] + more
            rest = rest - more
    return np.array(given)


def normal_values(rng, shape, width, reach, split=(), kind=jnp.bfloat16):
    array = width * jax.random.normal(rng, shape, jnp.float32)
    if split:
        array = array * block_levels(rng, shape, split, -0.22, 0.18)
    return jnp.clip(array, -reach, reach).astype(kind)


def bell_draw_with(stream_key, extent, spread, limit, pieces, heavy, kind=jnp.bfloat16):
    drawn = spread * jax.random.normal(stream_key, extent, jnp.float32)
    if pieces:
        drawn = drawn * block_levels(stream_key, extent, pieces, -0.22, 0.18)
    return jnp.clip(raised(drawn, jax.random.fold_in(stream_key, 3), *heavy), -limit, limit).astype(kind)


def setup_inputs(seed: int = 0) -> dict:
    arg_keys = jax.random.split(jax.random.key(seed), 18)
    layer_input = normal_values(arg_keys[0], (SEQS, SEQ_LEN, D), 1.0, 6.0, ((0, 8), (1, 4)))
    attn_gain = jnp.clip(1.0 + 0.18 * jax.random.normal(arg_keys[1], (D,), jnp.float32), 0.1, 1.9)
    w_query = normal_values(arg_keys[2], (D, H * HD), (D // 4) ** -0.5, 0.3125)
    w_key = normal_values(arg_keys[3], (D, KVH * HD), D ** -0.5, 0.15625)
    w_value = normal_values(arg_keys[4], (D, KVH * HD), D ** -0.5, 0.15625)
    w_out = normal_values(arg_keys[5], (H * HD, D), (D // 64) ** -0.5, 1.25)
    ffn_gain = jnp.clip(1.0 + 0.18 * jax.random.normal(arg_keys[6], (D,), jnp.float32), 0.1, 1.9)
    shared_gate = normal_values(arg_keys[7], (D, FS), D ** -0.5, 0.15625)
    shared_up = normal_values(arg_keys[8], (D, FS), D ** -0.5, 0.15625)
    shared_down = normal_values(arg_keys[9], (FS, D), FS ** -0.5, 0.1875)
    expert_gate = normal_values(arg_keys[10], (EXPERTS, D, FE), D ** -0.5, 0.15625, ((0, 8),))
    expert_up = normal_values(arg_keys[11], (EXPERTS, D, FE), D ** -0.5, 0.15625, ((0, 8),))
    expert_down = normal_values(arg_keys[12], (EXPERTS, FE, D), (FE // 4) ** -0.5, 0.5, ((0, 8),))
    routes_keys = jax.random.split(jax.random.fold_in(arg_keys[13], 1), SEQS * SEQ_LEN // TOK_DEV)
    routes_turns = jax.random.permutation(jax.random.fold_in(arg_keys[13], 3), SEQS * SEQ_LEN // TOK_DEV)
    routes = jax.vmap(lambda own, number: routed_block(jax.random.fold_in(arg_keys[13], 2), own, number, TOK_DEV, EXPERTS, TOP, CAP, 2))(routes_keys, routes_turns).reshape((SEQS, SEQ_LEN, TOP))
    gate_logits = normal_values(arg_keys[14], (SEQS, SEQ_LEN, TOP), 0.5, 3.0, ((0, 8), (1, 4)), jnp.float32)
    span_order = jax.random.permutation(arg_keys[15], 2 * N_CTX).astype(jnp.int32)
    cotangent = bell_draw_with(arg_keys[16], (SEQS, SEQ_LEN, D), 1.0, 6.0, ((0, 8), (1, 4)), (1, 2, 4, 2.0))
    return dict(layer_input=layer_input, attn_gain=attn_gain, w_query=w_query, w_key=w_key, w_value=w_value, w_out=w_out, ffn_gain=ffn_gain, shared_gate=shared_gate, shared_up=shared_up, shared_down=shared_down, expert_gate=expert_gate, expert_up=expert_up, expert_down=expert_down, routes=routes, gate_logits=gate_logits, span_order=span_order, cotangent=cotangent)


EPSILON = 1e-06
NEGATIVE = -1e+30
HIGHEST = lax.Precision.HIGHEST

@jax.custom_vjp
def low(v):
    return lax.optimization_barrier(v.astype(jnp.bfloat16)).astype(jnp.float32)

@jax.custom_vjp
def low_back(v):
    return v

def low_keep(v):
    return (low(v), None)

def low_pass(kept, grad):
    return (grad,)

def back_keep(v):
    return (v, None)

def back_low(kept, grad):
    return (low(grad),)
low.defvjp(low_keep, low_pass)
low_back.defvjp(back_keep, back_low)

def both_ways(value):
    return low_back(low(value))

def matmul(left_op, right_op):
    return jnp.matmul(left_op, right_op, precision=HIGHEST)

def rms_norm(values, gain_vec):
    return values * lax.rsqrt(lax.optimization_barrier(jnp.mean(values * values, axis=-1, keepdims=True)) + EPSILON) * gain_vec

def sequence_attention(queries, keys, values, places):
    length = queries.shape[0]
    block_rows = min(512, length)
    blocks = length // block_rows
    groups = H // KVH
    key_heads = keys.reshape(length, KVH, HD)
    value_heads = values.reshape(length, KVH, HD)
    query_blocks = queries.reshape(blocks, block_rows, KVH, groups, HD)
    place_blocks = places.reshape(blocks, block_rows)

    @jax.checkpoint
    def one_block(inputs):
        query_heads, query_places = inputs
        raw_scores = low_back(jnp.einsum('tgrd,jgd->tgrj', query_heads, key_heads, precision=HIGHEST))
        scores = raw_scores * HD ** (-0.5)
        visible = (places[None, :] <= query_places[:, None])[:, None, None, :]
        scores = jnp.where(visible, scores, NEGATIVE)
        log_total = jax.nn.logsumexp(scores, axis=-1, keepdims=True)
        weights = low(jnp.where(visible, jnp.exp(scores - log_total), 0.0))
        mixed = jnp.einsum('tgrj,jgd->tgrd', weights, value_heads, precision=HIGHEST)
        return mixed.reshape(block_rows, H * HD)
    return lax.map(one_block, (query_blocks, place_blocks)).reshape(length, H * HD)

def sequence_routed(rows_in, route_ids, gate_vals, gate_w, up_w, down_w):
    assigned = route_ids.shape[0] * TOP
    flat_route = route_ids.reshape(assigned)
    flat_gate = gate_vals.reshape(assigned)
    capacity = N_CTX * CAP

    def one_expert(summed, inputs):
        expert_id, gate_one, up_one, down_one = inputs
        chosen = jnp.nonzero(flat_route == expert_id, size=capacity, fill_value=assigned)[0].astype(jnp.int32)
        inside = chosen < assigned
        safe_ids = jnp.minimum(chosen, assigned - 1)
        owners = safe_ids // TOP
        weight = jnp.where(inside, flat_gate[safe_ids], 0.0)
        picked = low_back(rows_in[owners])
        gate_act = low_back(matmul(picked, gate_one))
        up_act = low_back(matmul(picked, up_one))
        hidden = low(jax.nn.silu(gate_act) * up_act)
        result = both_ways(matmul(hidden, down_one))
        return (summed.at[owners].add(weight[:, None] * result), None)
    summed, unused = lax.scan(jax.checkpoint(one_expert), jnp.zeros_like(rows_in), (jnp.arange(EXPERTS, dtype=jnp.int32), gate_w, up_w, down_w))
    return summed

def layer(inputs, attn_gain, w_query, w_key, w_value, w_out, ffn_gain, shared_gate, shared_up, shared_down, expert_gate, expert_up, expert_down, route_ids, gate_vals, places):
    normed = low(rms_norm(inputs, attn_gain))
    queries = both_ways(matmul(normed, w_query))
    keys = both_ways(matmul(normed, w_key))
    values = both_ways(matmul(normed, w_value))
    attended = lax.map(lambda triple: sequence_attention(triple[0], triple[1], triple[2], places), (queries, keys, values))
    attended = both_ways(attended)
    middle = inputs + low_back(matmul(attended, w_out))
    rows_in = low(rms_norm(middle, ffn_gain))
    shared_g = low_back(matmul(rows_in, shared_gate))
    shared_u = low_back(matmul(rows_in, shared_up))
    shared_hidden = low(jax.nn.silu(shared_g) * shared_u)
    shared_out = matmul(shared_hidden, shared_down)
    routed = lax.map(lambda triple: sequence_routed(triple[0], triple[1], triple[2], expert_gate, expert_up, expert_down), (rows_in, route_ids, gate_vals))
    return middle + shared_out + routed

def reference(layer_input, attn_gain, w_query, w_key, w_value, w_out, ffn_gain, shared_gate, shared_up, shared_down, expert_gate, expert_up, expert_down, routes, gate_logits, span_order, cotangent):
    span_rows = TOK_DEV // 2
    stored = jnp.arange(SEQ_LEN, dtype=jnp.int32)
    places = (span_order[stored // span_rows] * span_rows + stored % span_rows).astype(jnp.int32)
    gate_vals = jax.nn.softmax(gate_logits.astype(jnp.float32), axis=-1)

    def forward(inputs, gain_one, query_w, key_w, value_w, out_w, gain_two, sg_w, su_w, sd_w, eg_w, eu_w, ed_w):
        return layer(inputs, gain_one, query_w, key_w, value_w, out_w, gain_two, sg_w, su_w, sd_w, eg_w, eu_w, ed_w, routes, gate_vals, places)
    output, pullback = jax.vjp(forward, layer_input.astype(jnp.float32), attn_gain.astype(jnp.float32), w_query.astype(jnp.float32), w_key.astype(jnp.float32), w_value.astype(jnp.float32), w_out.astype(jnp.float32), ffn_gain.astype(jnp.float32), shared_gate.astype(jnp.float32), shared_up.astype(jnp.float32), shared_down.astype(jnp.float32), expert_gate.astype(jnp.float32), expert_up.astype(jnp.float32), expert_down.astype(jnp.float32))
    grads = pullback(cotangent.astype(jnp.float32))
    return (output.astype(jnp.bfloat16), grads[0], grads[1], grads[2], grads[3], grads[4], grads[5], grads[6], grads[7], grads[8], grads[9], grads[10], grads[11], grads[12])
```

```python
import functools

import jax
import jax.numpy as jnp
from jax import lax
from jax.experimental import pallas as pl
from jax.experimental.pallas import tpu as pltpu
from jax.sharding import PartitionSpec as P

H = 12
HD = 128
KVH = 4
GROUPS = H // KVH
EPSILON = 1e-06
NEGATIVE = -1e30
SCALE = HD ** (-0.5)
BOTH = ("ctx", "exp")
GATE_LANES = 128
LOW_LANE = 64
VMEM_LIMIT = 60 * 2**20
bf16 = jnp.bfloat16
f32 = jnp.float32


def dot(left_op, right_op):
    return jnp.dot(left_op, right_op, preferred_element_type=f32)


def dot_nt(left_op, right_op):
    return lax.dot_general(left_op, right_op, (((1,), (1,)), ((), ())), preferred_element_type=f32)


def dot_tn(left_op, right_op):
    return lax.dot_general(left_op, right_op, (((0,), (0,)), ((), ())), preferred_element_type=f32)


def whole(shape):
    return pl.BlockSpec(shape, lambda *_: (0,) * len(shape))


def params():
    return pltpu.CompilerParams(vmem_limit_bytes=VMEM_LIMIT)


def cost(flops, nbytes):
    return pl.CostEstimate(flops=flops, bytes_accessed=nbytes, transcendentals=0)


def keyvalue_kernel(x_ref, gain_ref, wk_ref, wv_ref, normed_ref, kv_ref):
    @pl.when(pl.program_id(0) == 0)
    def _():
        x = x_ref[...].astype(f32)
        factor = lax.rsqrt(jnp.mean(x * x, axis=-1, keepdims=True) + EPSILON)
        normed_ref[...] = (x * factor * gain_ref[...]).astype(bf16)

    both = jnp.concatenate([wk_ref[...], wv_ref[...]], axis=1)
    kv_ref[...] = dot(normed_ref[...], both).astype(bf16)


def keyvalue(x, gain, wk, wv):
    rows, width = x.shape
    return pl.pallas_call(
        keyvalue_kernel,
        grid=(KVH,),
        in_specs=[
            whole((rows, width)),
            whole((1, width)),
            pl.BlockSpec((width, HD), lambda g: (0, g)),
            pl.BlockSpec((width, HD), lambda g: (0, g)),
        ],
        out_specs=[whole((rows, width)), pl.BlockSpec((rows, 2 * HD), lambda g: (0, g))],
        out_shape=[
            jax.ShapeDtypeStruct((rows, width), bf16),
            jax.ShapeDtypeStruct((rows, 2 * KVH * HD), bf16),
        ],
        compiler_params=params(),
        cost_estimate=cost(4 * rows * width * KVH * HD, 5 * 2**20),
    )(x, gain.reshape(1, width), wk, wv)


def stack_heads(ref):
    return jnp.concatenate([ref[:, r * HD : (r + 1) * HD] for r in range(GROUPS)], axis=0)


def place_column(bases, at, rows):
    row = lax.broadcasted_iota(jnp.int32, (rows, 1), 0)
    half = rows // 2
    return jnp.where(row < half, bases[at] + row, bases[at + 1] + row - half)


def place_row(bases, rows):
    row = lax.broadcasted_iota(jnp.int32, (1, GROUPS * rows), 1) % rows
    half = rows // 2
    return jnp.where(row < half, bases[0] + row, bases[1] + row - half)


def attend_kernel(blocks, bases, q_ref, *refs):
    kv_refs = refs[:blocks]
    out_ref, lse_ref, score_ref = refs[blocks:]
    rows = q_ref.shape[0]
    queries = stack_heads(q_ref)
    wanted = place_row(bases, rows)
    peak = jnp.full((1, GROUPS * rows), NEGATIVE, f32)
    for b in range(blocks):
        scores = dot_nt(kv_refs[b][:, :HD], queries) * SCALE
        visible = place_column(bases, 2 + 2 * b, rows) <= wanted
        scores = jnp.where(visible, scores, NEGATIVE)
        score_ref[b * rows : (b + 1) * rows, :] = scores
        peak = jnp.maximum(peak, jnp.max(scores, axis=0, keepdims=True))
    total = jnp.zeros_like(peak)
    mixed = jnp.zeros((HD, GROUPS * rows), f32)
    for b in range(blocks):
        weights = jnp.exp(score_ref[b * rows : (b + 1) * rows, :] - peak)
        total = total + jnp.sum(weights, axis=0, keepdims=True)
        mixed = mixed + dot_tn(kv_refs[b][:, HD:], weights.astype(bf16))
    lse_ref[0] = peak + jnp.log(total)
    mixed = jnp.transpose(mixed / total)
    for r in range(GROUPS):
        out_ref[:, r * HD : (r + 1) * HD] = mixed[r * rows : (r + 1) * rows].astype(bf16)


def attend(bases, queries, kv_blocks):
    rows = queries.shape[0]
    blocks = len(kv_blocks)
    wide = GROUPS * HD
    return pl.pallas_call(
        functools.partial(attend_kernel, blocks),
        grid_spec=pltpu.PrefetchScalarGridSpec(
            num_scalar_prefetch=1,
            grid=(KVH,),
            in_specs=[pl.BlockSpec((rows, wide), lambda g, _: (0, g))]
            + [pl.BlockSpec((rows, 2 * HD), lambda g, _: (0, g))] * blocks,
            out_specs=[
                pl.BlockSpec((rows, wide), lambda g, _: (0, g)),
                pl.BlockSpec((1, 1, GROUPS * rows), lambda g, _: (g, 0, 0)),
            ],
            scratch_shapes=[pltpu.VMEM((blocks * rows, GROUPS * rows), f32)],
        ),
        out_shape=[
            jax.ShapeDtypeStruct((rows, H * HD), bf16),
            jax.ShapeDtypeStruct((KVH, 1, GROUPS * rows), f32),
        ],
        compiler_params=params(),
        cost_estimate=cost(8 * rows * rows * blocks * H * HD, 4 * 2**20),
    )(bases, queries, *kv_blocks)


def attend_back_kernel(blocks, bases, q_ref, grad_ref, lse_ref, *refs):
    kv_refs = refs[:blocks]
    dq_ref = refs[blocks]
    dkv_refs = refs[blocks + 1 : 2 * blocks + 1]
    prob_ref, slope_ref = refs[2 * blocks + 1 :]
    rows = q_ref.shape[0]
    queries = stack_heads(q_ref)
    grads = stack_heads(grad_ref)
    wanted = place_row(bases, rows)
    lse = lse_ref[0]
    delta = jnp.zeros((1, GROUPS * rows), f32)
    for b in range(blocks):
        part = slice(b * rows, (b + 1) * rows)
        scores = dot_nt(kv_refs[b][:, :HD], queries) * SCALE - lse
        visible = place_column(bases, 2 + 2 * b, rows) <= wanted
        prob = jnp.exp(jnp.where(visible, scores, NEGATIVE))
        slope = dot_nt(kv_refs[b][:, HD:], grads)
        delta = delta + jnp.sum(prob * slope, axis=0, keepdims=True)
        prob_ref[part, :] = prob
        slope_ref[part, :] = slope
        dkv_refs[b][:, HD:] = dot(prob.astype(bf16), grads).astype(bf16)
    query_grad = jnp.zeros((HD, GROUPS * rows), f32)
    for b in range(blocks):
        part = slice(b * rows, (b + 1) * rows)
        dscore = (prob_ref[part, :] * (slope_ref[part, :] - delta) * SCALE).astype(bf16)
        dkv_refs[b][:, :HD] = dot(dscore, queries).astype(bf16)
        query_grad = query_grad + dot_tn(kv_refs[b][:, :HD], dscore)
    query_grad = jnp.transpose(query_grad)
    for r in range(GROUPS):
        dq_ref[:, r * HD : (r + 1) * HD] = query_grad[r * rows : (r + 1) * rows].astype(bf16)


def attend_back(bases, queries, grads, lse, kv_blocks):
    rows = queries.shape[0]
    blocks = len(kv_blocks)
    wide = GROUPS * HD
    by_group = pl.BlockSpec((rows, wide), lambda g, _: (0, g))
    kv_spec = pl.BlockSpec((rows, 2 * HD), lambda g, _: (0, g))
    return pl.pallas_call(
        functools.partial(attend_back_kernel, blocks),
        grid_spec=pltpu.PrefetchScalarGridSpec(
            num_scalar_prefetch=1,
            grid=(KVH,),
            in_specs=[
                by_group,
                by_group,
                pl.BlockSpec((1, 1, GROUPS * rows), lambda g, _: (g, 0, 0)),
            ]
            + [kv_spec] * blocks,
            out_specs=[by_group] + [kv_spec] * blocks,
            scratch_shapes=[pltpu.VMEM((blocks * rows, GROUPS * rows), f32)] * 2,
        ),
        out_shape=[jax.ShapeDtypeStruct((rows, H * HD), bf16)]
        + [jax.ShapeDtypeStruct((rows, 2 * KVH * HD), bf16)] * blocks,
        compiler_params=params(),
        cost_estimate=cost(20 * rows * rows * blocks * H * HD, 8 * 2**20),
    )(bases, queries, grads, lse, *kv_blocks)


def middle_kernel(x_ref, att_ref, w_ref, gain_ref, middle_ref, rows_ref):
    step = pl.program_id(0)
    tile = w_ref.shape[1]
    columns = pl.ds(pl.multiple_of(step * tile, tile), tile)
    middle_ref[:, columns] = x_ref[...].astype(f32) + dot(att_ref[...], w_ref[...])

    @pl.when(step == pl.num_programs(0) - 1)
    def _():
        middle = middle_ref[...]
        factor = lax.rsqrt(jnp.mean(middle * middle, axis=-1, keepdims=True) + EPSILON)
        rows_ref[...] = (middle * factor * gain_ref[...]).astype(bf16)


def middle_forward(x, attended, w_out, gain, tile=512):
    rows, width = x.shape
    return pl.pallas_call(
        middle_kernel,
        grid=(width // tile,),
        in_specs=[
            pl.BlockSpec((rows, tile), lambda n: (0, n)),
            whole(attended.shape),
            pl.BlockSpec((w_out.shape[0], tile), lambda n: (0, n)),
            whole((1, width)),
        ],
        out_specs=[whole((rows, width))] * 2,
        out_shape=[
            jax.ShapeDtypeStruct((rows, width), f32),
            jax.ShapeDtypeStruct((rows, width), bf16),
        ],
        compiler_params=params(),
        cost_estimate=cost(2 * rows * width * width, 8 * 2**20),
    )(x, attended, w_out, gain.reshape(1, width))


def middle_back_kernel(parts, *refs):
    grad_refs = refs[:parts]
    middle_ref, cot_ref, gain_ref, w_ref = refs[parts : parts + 4]
    mgrad_ref, low_ref, dgain_ref, out_ref = refs[parts + 4 :]

    @pl.when(pl.program_id(0) == 0)
    def _():
        upstream = grad_refs[0][...].astype(f32)
        for ref in grad_refs[1:]:
            upstream = upstream + ref[...].astype(f32)
        middle = middle_ref[...]
        factor = lax.rsqrt(jnp.mean(middle * middle, axis=-1, keepdims=True) + EPSILON)
        scaled = upstream * gain_ref[...]
        inner = jnp.mean(scaled * middle, axis=-1, keepdims=True)
        grad = factor * scaled - middle * (factor * factor * factor * inner)
        grad = cot_ref[...].astype(f32) + grad
        mgrad_ref[...] = grad
        low_ref[...] = grad.astype(bf16)
        dgain_ref[...] = jnp.sum(upstream * middle * factor, axis=0, keepdims=True)

    out_ref[...] = dot_nt(low_ref[...], w_ref[...]).astype(bf16)


def middle_back(grads, middle, cotangent, gain, w_out, tile=512):
    rows, width = middle.shape
    inner = w_out.shape[0]
    return pl.pallas_call(
        functools.partial(middle_back_kernel, len(grads)),
        grid=(inner // tile,),
        in_specs=[whole((rows, width))] * (len(grads) + 2)
        + [whole((1, width)), pl.BlockSpec((tile, width), lambda n: (n, 0))],
        out_specs=[
            whole((rows, width)),
            whole((rows, width)),
            whole((1, width)),
            pl.BlockSpec((rows, tile), lambda n: (0, n)),
        ],
        out_shape=[
            jax.ShapeDtypeStruct((rows, width), f32),
            jax.ShapeDtypeStruct((rows, width), bf16),
            jax.ShapeDtypeStruct((1, width), f32),
            jax.ShapeDtypeStruct((rows, inner), bf16),
        ],
        compiler_params=params(),
        cost_estimate=cost(2 * rows * width * inner, 16 * 2**20),
    )(*grads, middle, cotangent, gain.reshape(1, width), w_out)


def input_back_kernel(dq_ref, dkv_ref, wq_ref, wk_ref, wv_ref, x_ref, gain_ref, mgrad_ref, out_ref, dgain_ref):
    step = pl.program_id(0)
    term = dot_nt(dq_ref[...], wq_ref[...])
    term = term + dot_nt(dkv_ref[:, :HD], wk_ref[...]) + dot_nt(dkv_ref[:, HD:], wv_ref[...])

    @pl.when(step == 0)
    def _():
        out_ref[...] = term

    @pl.when(step > 0)
    def _():
        out_ref[...] += term

    @pl.when(step == pl.num_programs(0) - 1)
    def _():
        upstream = out_ref[...]
        x = x_ref[...].astype(f32)
        factor = lax.rsqrt(jnp.mean(x * x, axis=-1, keepdims=True) + EPSILON)
        scaled = upstream * gain_ref[...]
        inner = jnp.mean(scaled * x, axis=-1, keepdims=True)
        out_ref[...] = mgrad_ref[...] + factor * scaled - x * (factor * factor * factor * inner)
        dgain_ref[...] = jnp.sum(upstream * x * factor, axis=0, keepdims=True)


def input_back(dq, dkv, wq, wk, wv, x, gain, mgrad):
    rows, width = x.shape
    wide = GROUPS * HD
    return pl.pallas_call(
        input_back_kernel,
        grid=(KVH,),
        in_specs=[
            pl.BlockSpec((rows, wide), lambda g: (0, g)),
            pl.BlockSpec((rows, 2 * HD), lambda g: (0, g)),
            pl.BlockSpec((width, wide), lambda g: (0, g)),
            pl.BlockSpec((width, HD), lambda g: (0, g)),
            pl.BlockSpec((width, HD), lambda g: (0, g)),
            whole((rows, width)),
            whole((1, width)),
            whole((rows, width)),
        ],
        out_specs=[whole((rows, width)), whole((1, width))],
        out_shape=[
            jax.ShapeDtypeStruct((rows, width), f32),
            jax.ShapeDtypeStruct((1, width), f32),
        ],
        compiler_params=params(),
        cost_estimate=cost(2 * rows * width * (H + 2 * KVH) * HD, 14 * 2**20),
    )(dq, dkv, wq, wk, wv, x, gain.reshape(1, width), mgrad)


def experts_kernel(count, per, weighted, ids_ref, *refs):
    x_refs, c_refs = refs[:count], refs[count : 2 * count]
    wg_ref, wu_ref, wd_ref = refs[2 * count : 2 * count + 3]
    outs = refs[-(2 * count + 6) :]
    o_refs, g_refs = outs[:count], outs[count : 2 * count]
    x_all, c_all, hid_ref, dgu_ref, acc_o, acc_g = outs[2 * count :]
    step = pl.program_id(0)
    rows, width = x_refs[0].shape
    chunk = wg_ref.shape[2]

    @pl.when(step == 0)
    def _():
        for i in range(count):
            x_all[i * rows : (i + 1) * rows, :] = x_refs[i][...]
            c_all[i * rows : (i + 1) * rows, :] = c_refs[i][:, :width]

    x = x_all[...]
    gate = dot(x, wg_ref[0])
    up = dot(x, wu_ref[0])
    slope = dot_nt(c_all[...], wd_ref[0])
    sigmoid = 1.0 / (1.0 + jnp.exp(-gate))
    act = gate * sigmoid
    hidden = act * up
    if weighted:
        lane = ids_ref[0] + step // per
        lanes = lax.broadcasted_iota(jnp.int32, (rows, GATE_LANES), 1)
        chosen = (lanes == lane) | (lanes == lane + LOW_LANE)
        weight = jnp.concatenate(
            [
                jnp.sum(
                    jnp.where(chosen, c_refs[i][:, width:].astype(f32), 0.0),
                    axis=1,
                    keepdims=True,
                )
                for i in range(count)
            ],
            axis=0,
        )
        hidden = hidden * weight
        slope = slope * weight
    hidden = hidden.astype(bf16)
    dg = (slope * up * (sigmoid * (1.0 + gate * (1.0 - sigmoid)))).astype(bf16)
    du = (slope * act).astype(bf16)
    hid_ref[...] = hidden
    dgu_ref[:, :chunk] = dg
    dgu_ref[:, chunk:] = du
    out_term = dot(hidden, wd_ref[0])
    grad_term = dot_nt(dg, wg_ref[0]) + dot_nt(du, wu_ref[0])

    @pl.when(step == 0)
    def _():
        acc_o[...] = out_term
        acc_g[...] = grad_term

    @pl.when((step > 0) & (step < pl.num_programs(0) - 1))
    def _():
        acc_o[...] += out_term
        acc_g[...] += grad_term

    @pl.when(step == pl.num_programs(0) - 1)
    def _():
        out = acc_o[...] + out_term
        grad = acc_g[...] + grad_term
        for i in range(count):
            o_refs[i][...] = out[i * rows : (i + 1) * rows].astype(o_refs[i].dtype)
            g_refs[i][...] = grad[i * rows : (i + 1) * rows].astype(g_refs[i].dtype)


def experts(lane, xs, cs, wg, wu, wd, part, parts, kept, weighted, kind, chunk=256):
    count = len(xs)
    rows, width = xs[0].shape
    held, _, inner = wg.shape
    per = inner // chunk
    steps = held * per
    taken = count * rows
    collected = [
        jax.ShapeDtypeStruct((parts * taken, width), bf16),
        jax.ShapeDtypeStruct((parts * taken, width), bf16),
        jax.ShapeDtypeStruct((parts * taken, held * inner), bf16),
        jax.ShapeDtypeStruct((parts * taken, 2 * held * inner), bf16),
    ]
    in_specs = [whole((rows, width))] * count + [whole(cs[0].shape)] * count
    in_specs += [
        pl.BlockSpec((1, width, chunk), lambda i, _: (i // per, 0, i % per)),
        pl.BlockSpec((1, width, chunk), lambda i, _: (i // per, 0, i % per)),
        pl.BlockSpec((1, chunk, width), lambda i, _: (i // per, i % per, 0)),
    ]
    operands = [lane, *xs, *cs, wg, wu, wd]
    aliases = {}
    if kept is not None:
        aliases = {len(operands) + j: 2 * count + j for j in range(4)}
        operands += list(kept)
        in_specs += [pl.BlockSpec(memory_space=pl.ANY)] * 4
    result = pl.pallas_call(
        functools.partial(experts_kernel, count, per, weighted),
        grid_spec=pltpu.PrefetchScalarGridSpec(
            num_scalar_prefetch=1,
            grid=(steps,),
            in_specs=in_specs,
            out_specs=[whole((rows, width))] * (2 * count)
            + [
                pl.BlockSpec((taken, width), lambda i, _: (part, 0)),
                pl.BlockSpec((taken, width), lambda i, _: (part, 0)),
                pl.BlockSpec((taken, chunk), lambda i, _: (part, i)),
                pl.BlockSpec((taken, 2 * chunk), lambda i, _: (part, i)),
            ],
            scratch_shapes=[pltpu.VMEM((taken, width), f32)] * 2,
        ),
        out_shape=[jax.ShapeDtypeStruct((rows, width), kind)] * (2 * count) + collected,
        input_output_aliases=aliases,
        compiler_params=params(),
        cost_estimate=cost(12 * taken * width * held * inner, 24 * 2**20),
    )(*operands)
    return result[:count], result[count : 2 * count], result[2 * count :]


def swap_inner(value, axis):
    size = lax.axis_size(axis)
    return lax.ppermute(value, axis, [(i, i ^ 1) for i in range(size)])


def shift_outer(value, axis, by):
    outer = lax.axis_size(axis) // 2
    perm = [(o * 2 + i, ((o + by) % outer) * 2 + i) for o in range(outer) for i in range(2)]
    return lax.ppermute(value, axis, perm)


def ring_step(value, by):
    n_ctx, n_exp = lax.axis_size("ctx"), lax.axis_size("exp")
    outer = n_exp // 2
    perm = []
    for c in range(n_ctx):
        way = by if c % 2 == 0 else -by
        for o in range(outer):
            for i in range(2):
                perm.append((c * n_exp + o * 2 + i, c * n_exp + ((o + way) % outer) * 2 + i))
    return lax.ppermute(value, BOTH, perm)


def ring_gather(block):
    own = [block]
    for _ in range(lax.axis_size("exp") // 2 - 1):
        own.append(ring_step(own[-1], 1))
    return [(b, swap_inner(b, "exp")) for b in own]


def ring_reduce(pieces):
    pairs = [(a, swap_inner(b, "exp")) for a, b in pieces]
    moved = None
    for a, b in reversed(pairs[1:]):
        total = a.astype(f32) + b.astype(f32)
        if moved is not None:
            total = total + moved.astype(f32)
        moved = ring_step(total.astype(bf16), -1)
    return [pairs[0][0], pairs[0][1], moved]


def pick(value, index, dim):
    return lax.dynamic_index_in_dim(value, index, dim, keepdims=False)


def stages(total, dims, order, kind):
    c, e = lax.axis_index("ctx"), lax.axis_index("exp")
    at = {"y": c // 2, "core": c % 2, "z": e // 2, "x": e % 2}
    axis = {"y": "ctx", "core": "ctx", "z": "exp", "x": "exp"}
    dims = list(dims)
    for name in order:
        dim = dims.index(name)
        dims.remove(name)
        size = total.shape[dim]
        kept = pick(total, at[name], dim).astype(f32)
        for d in range(1, size):
            sent = pick(total, (at[name] + d) % size, dim).astype(kind)
            if name in ("core", "x"):
                got = swap_inner(sent, axis[name])
            else:
                got = shift_outer(sent, axis[name], d)
            kept = kept + got.astype(f32)
        total = kept
    return total


def weight_sum(left_op, right_op, order):
    n_ctx, n_exp = lax.axis_size("ctx"), lax.axis_size("exp")
    core = lax.axis_index("ctx") % 2
    tokens, height = left_op.shape
    outer = n_ctx // 2
    rows = height // (n_ctx * n_exp)
    split = left_op.reshape(tokens, outer, 2, height // n_ctx)
    halves = []
    for side in (1 - core, core):
        mine = pick(split, side, 2).reshape(tokens, height // 2)
        halves.append(dot_tn(mine, right_op).astype(bf16))
    total = halves[1].astype(f32) + swap_inner(halves[0], "ctx").astype(f32)
    total = total.reshape(outer, n_exp // 2, 2, rows, right_op.shape[1])
    return stages(total, ("y", "z", "x"), order, bf16)


def shards(
    layer_input,
    attn_gain,
    w_query,
    w_key,
    w_value,
    w_out,
    ffn_gain,
    shared_gate,
    shared_up,
    shared_down,
    expert_gate,
    expert_up,
    expert_down,
    routes,
    gate_logits,
    span_order,
    cotangent,
):
    x = layer_input[0]
    cot = cotangent[0]
    tokens, width = x.shape
    span_rows = tokens // 2
    n_ctx, n_exp = lax.axis_size("ctx"), lax.axis_size("exp")
    ctx_id, exp_id = lax.axis_index("ctx"), lax.axis_index("exp")
    local_experts, _, inner = expert_gate.shape
    expert_count = local_experts * n_exp

    normed, kv = keyvalue(x, attn_gain, w_key, w_value)
    kv_blocks, kv_ids = [], []
    moved = kv
    for k in range(n_ctx // 2):
        if k:
            moved = shift_outer(moved, "ctx", 1)
        source = ((ctx_id // 2 - k) % (n_ctx // 2)) * 2 + ctx_id % 2
        kv_blocks += [moved, swap_inner(moved, "ctx")]
        kv_ids += [source, source ^ 1]
    queries = dot(normed, w_query).astype(bf16)
    spans = jnp.stack([2 * i + s for i in [ctx_id] + kv_ids for s in range(2)])
    bases = span_order[spans] * span_rows

    gate_vals = jax.nn.softmax(gate_logits[0], axis=-1)
    named = routes[0][:, None, :] == jnp.arange(expert_count, dtype=jnp.int32)[None, :, None]
    row_gates = jnp.sum(jnp.where(named, gate_vals[:, None, :], 0.0), axis=-1)
    high = row_gates.astype(bf16)
    low = (row_gates - high.astype(f32)).astype(bf16)
    fill = ((0, 0), (0, LOW_LANE - expert_count))
    cot_ext = jnp.concatenate([cot, jnp.pad(high, fill), jnp.pad(low, fill)], axis=1)
    cot_blocks = ring_gather(cot_ext)

    attended, lse = attend(bases, queries, kv_blocks)
    middle, rows_low = middle_forward(x, attended, w_out, ffn_gain)

    row_blocks = ring_gather(rows_low)
    lane = (exp_id * local_experts).astype(jnp.int32).reshape(1)
    (shared_out,), (shared_grad,), (_, _, shared_hidden, shared_dgu) = experts(
        lane,
        [rows_low],
        [cot],
        shared_gate[None],
        shared_up[None],
        shared_down[None],
        0,
        1,
        None,
        False,
        f32,
    )
    levels = n_exp // 2
    out_terms, grad_terms, kept = [], [], None
    for k in range(levels):
        out_k, grad_k, kept = experts(
            lane,
            list(row_blocks[k]),
            list(cot_blocks[k]),
            expert_gate,
            expert_up,
            expert_down,
            k,
            levels,
            kept,
            True,
            bf16,
        )
        out_terms.append(out_k)
        grad_terms.append(grad_k)
    row_grads = ring_reduce(grad_terms)
    routed = ring_reduce(out_terms)
    rows_all, cot_all, hid_all, dgu_all = kept

    sum_gate_up = weight_sum(rows_low, shared_dgu, ("y", "x", "z"))
    sum_down = weight_sum(shared_hidden, cot, ("y", "x", "z"))
    grad_gate_up = dot_tn(rows_all, dgu_all).astype(bf16)
    grad_down = dot_tn(cot_all, hid_all).astype(bf16)
    expert_gate_up = lax.psum_scatter(grad_gate_up, "ctx", scatter_dimension=0, tiled=True)
    expert_down_t = lax.psum_scatter(grad_down, "ctx", scatter_dimension=0, tiled=True)

    mgrad, mgrad_low, ffn_gain_grad, att_grad = middle_back(
        [shared_grad] + row_grads, middle, cot, ffn_gain, w_out
    )
    dq, *dkv_blocks = attend_back(bases, queries, att_grad, lse, kv_blocks)
    kv_grad = None
    for k in reversed(range(n_ctx // 2)):
        term = dkv_blocks[2 * k].astype(f32) + swap_inner(dkv_blocks[2 * k + 1], "ctx").astype(f32)
        if kv_grad is not None:
            term = term + shift_outer(kv_grad.astype(bf16), "ctx", -1).astype(f32)
        kv_grad = term
    dkv = kv_grad.astype(bf16)
    sum_out = weight_sum(attended, mgrad_low, ("y", "x", "z"))
    middle_column = w_query.shape[1] // 2
    sum_query_a = weight_sum(normed, dq[:, :middle_column], ("x", "z", "y"))
    sum_query_b = weight_sum(normed, dq[:, middle_column:], ("z", "x", "y"))
    sum_kv = weight_sum(normed, dkv, ("y", "x", "z"))
    input_grad, attn_gain_grad = input_back(
        dq, dkv, w_query, w_key, w_value, x, attn_gain, mgrad
    )
    gains = jnp.stack(
        [
            attn_gain_grad.reshape(n_ctx // 2, 2, n_exp // 2, 2, -1),
            ffn_gain_grad.reshape(n_ctx // 2, 2, n_exp // 2, 2, -1),
        ],
        axis=4,
    )
    gains = stages(gains, ("y", "core", "z", "x"), ("core", "y", "x", "z"), f32)

    layer_out = middle + shared_out + sum(r.astype(f32) for r in routed)
    out_rows = width // n_ctx
    per = inner // 256
    expert_gate_up = expert_gate_up.reshape(out_rows, local_experts, per, 2, 256).astype(f32)
    expert_grads = [
        jnp.moveaxis(expert_gate_up[:, :, :, i], 1, 0).reshape(local_experts, out_rows, inner)
        for i in range(2)
    ]
    expert_down_grad = jnp.transpose(
        expert_down_t.reshape(out_rows, local_experts, inner), (1, 2, 0)
    ).astype(f32)
    shared_rows = sum_gate_up.reshape(sum_gate_up.shape[0], -1, 2, 256)
    kv_rows = sum_kv.reshape(sum_kv.shape[0], KVH, 2, HD)
    return (
        layer_out.astype(bf16)[None],
        input_grad[None],
        gains[0],
        jnp.concatenate([sum_query_a, sum_query_b], axis=1),
        kv_rows[:, :, 0].reshape(sum_kv.shape[0], -1),
        kv_rows[:, :, 1].reshape(sum_kv.shape[0], -1),
        sum_out,
        gains[1],
        shared_rows[:, :, 0].reshape(sum_gate_up.shape[0], -1),
        shared_rows[:, :, 1].reshape(sum_gate_up.shape[0], -1),
        sum_down,
        expert_grads[0],
        expert_grads[1],
        expert_down_grad,
    )


def solution(mesh):
    return jax.shard_map(
        shards,
        mesh=mesh,
        in_specs=(
            P("exp", "ctx", None),
            P(),
            P(),
            P(),
            P(),
            P(),
            P(),
            P(),
            P(),
            P(),
            P("exp", None, None),
            P("exp", None, None),
            P("exp", None, None),
            P("exp", "ctx", None),
            P("exp", "ctx", None),
            P(),
            P("exp", "ctx", None),
        ),
        out_specs=(
            P("exp", "ctx", None),
            P("exp", "ctx", None),
            P(("ctx", "exp")),
            P(("ctx", "exp"), None),
            P(("ctx", "exp"), None),
            P(("ctx", "exp"), None),
            P(("ctx", "exp"), None),
            P(("ctx", "exp")),
            P(("ctx", "exp"), None),
            P(("ctx", "exp"), None),
            P(("ctx", "exp"), None),
            P("exp", "ctx", None),
            P("exp", "ctx", None),
            P("exp", None, "ctx"),
        ),
        check_vma=False,
    )
```

```python
import functools

import jax
import jax.numpy as jnp
from jax import lax
from jax.experimental import pallas as pl
from jax.experimental.pallas import tpu as pltpu
from jax.sharding import PartitionSpec as P

H = 12
HD = 128
KVH = 4
GROUPS = H // KVH
EPSILON = 1e-06
GATE_LANES = 128
LOW_LANE = 64
NEGATIVE = -1e30
SCALE = HD ** (-0.5)
BOTH = ("ctx", "exp")
VMEM_LIMIT = 60 * 2**20
bf16 = jnp.bfloat16
f32 = jnp.float32


def dot(left_op, right_op):
    return jnp.dot(left_op, right_op, preferred_element_type=f32)


def dot_nt(left_op, right_op):
    return lax.dot_general(left_op, right_op, (((1,), (1,)), ((), ())), preferred_element_type=f32)


def dot_tn(left_op, right_op):
    return lax.dot_general(left_op, right_op, (((0,), (0,)), ((), ())), preferred_element_type=f32)


def whole(shape):
    return pl.BlockSpec(shape, lambda *_: (0,) * len(shape))


def params():
    return pltpu.CompilerParams(vmem_limit_bytes=VMEM_LIMIT)


def anywhere(count):
    return [pl.BlockSpec(memory_space=pl.ANY)] * count


def cost(flops, nbytes):
    return pl.CostEstimate(flops=flops // 4, bytes_accessed=nbytes // 4, transcendentals=0)


def keyvalue_kernel(x_ref, gain_ref, wk_ref, wv_ref, normed_ref, kv_ref):
    @pl.when(pl.program_id(0) == 0)
    def _():
        x = x_ref[...].astype(f32)
        factor = lax.rsqrt(jnp.mean(x * x, axis=-1, keepdims=True) + EPSILON)
        normed_ref[...] = (x * factor * gain_ref[...]).astype(bf16)

    both = jnp.concatenate([wk_ref[...], wv_ref[...]], axis=1)
    kv_ref[...] = dot(normed_ref[...], both).astype(bf16)


def keyvalue(x, gain, wk, wv):
    rows, width = x.shape
    return pl.pallas_call(
        keyvalue_kernel,
        grid=(KVH,),
        in_specs=[
            whole((rows, width)),
            whole((1, width)),
            pl.BlockSpec((width, HD), lambda g: (0, g)),
            pl.BlockSpec((width, HD), lambda g: (0, g)),
        ],
        out_specs=[whole((rows, width)), pl.BlockSpec((rows, 2 * HD), lambda g: (0, g))],
        out_shape=[
            jax.ShapeDtypeStruct((rows, width), bf16),
            jax.ShapeDtypeStruct((rows, 2 * KVH * HD), bf16),
        ],
        compiler_params=params(),
        cost_estimate=cost(4 * rows * width * KVH * HD, 5 * 2**20),
    )(x, gain.reshape(1, width), wk, wv)


def stack_heads(ref):
    return jnp.concatenate([ref[:, r * HD : (r + 1) * HD] for r in range(GROUPS)], axis=0)


def places(pos, spans, block, shape, dim, rows):
    outer, side = (0, 0) if block is None else (block // 2, block % 2)
    ring = spans.shape[0] // 4
    owner = 2 * lax.rem(pos[0] + ring - outer, ring) + lax.rem(pos[1] + side, 2)
    row = lax.broadcasted_iota(jnp.int32, shape, dim) % rows
    half = rows // 2
    first, second = spans[2 * owner] * half, spans[2 * owner + 1] * half
    return jnp.where(row < half, first + row, second + row - half)


def attend_kernel(blocks, extra, pos, spans, q_ref, *refs):
    kv_refs = refs[:blocks]
    out_ref, lse_ref, score_ref = refs[blocks + extra :]
    rows = q_ref.shape[0]
    queries = stack_heads(q_ref)
    wanted = places(pos, spans, None, (1, GROUPS * rows), 1, rows)
    peak = jnp.full((1, GROUPS * rows), NEGATIVE, f32)
    for b in range(blocks):
        scores = dot_nt(kv_refs[b][:, :HD], queries) * SCALE
        visible = places(pos, spans, b, (rows, 1), 0, rows) <= wanted
        scores = jnp.where(visible, scores, NEGATIVE)
        score_ref[b * rows : (b + 1) * rows, :] = scores
        peak = jnp.maximum(peak, jnp.max(scores, axis=0, keepdims=True))
    total = jnp.zeros_like(peak)
    mixed = jnp.zeros((HD, GROUPS * rows), f32)
    for b in range(blocks):
        weights = jnp.exp(score_ref[b * rows : (b + 1) * rows, :] - peak)
        total = total + jnp.sum(weights, axis=0, keepdims=True)
        mixed = mixed + dot_tn(kv_refs[b][:, HD:], weights.astype(bf16))
    lse_ref[0] = peak + jnp.log(total)
    mixed = jnp.transpose(mixed / total)
    for r in range(GROUPS):
        out_ref[:, r * HD : (r + 1) * HD] = mixed[r * rows : (r + 1) * rows].astype(bf16)


def attend(pos, spans, queries, kv_blocks, after=()):
    rows = queries.shape[0]
    blocks = len(kv_blocks)
    wide = GROUPS * HD
    return pl.pallas_call(
        functools.partial(attend_kernel, blocks, len(after)),
        grid_spec=pltpu.PrefetchScalarGridSpec(
            num_scalar_prefetch=2,
            grid=(KVH,),
            in_specs=[pl.BlockSpec((rows, wide), lambda g, *_: (0, g))]
            + [pl.BlockSpec((rows, 2 * HD), lambda g, *_: (0, g))] * blocks
            + anywhere(len(after)),
            out_specs=[
                pl.BlockSpec((rows, wide), lambda g, *_: (0, g)),
                pl.BlockSpec((1, 1, GROUPS * rows), lambda g, *_: (g, 0, 0)),
            ],
            scratch_shapes=[pltpu.VMEM((blocks * rows, GROUPS * rows), f32)],
        ),
        out_shape=[
            jax.ShapeDtypeStruct((rows, H * HD), bf16),
            jax.ShapeDtypeStruct((KVH, 1, GROUPS * rows), f32),
        ],
        compiler_params=params(),
        cost_estimate=cost(8 * rows * rows * blocks * H * HD, 4 * 2**20),
    )(pos, spans, queries, *kv_blocks, *after)


def attend_back_kernel(blocks, extra, pos, spans, q_ref, grad_ref, lse_ref, *refs):
    kv_refs = refs[:blocks]
    dq_ref, same_ref, other_ref = refs[blocks + extra : -2]
    prob_ref, slope_ref = refs[-2:]
    rows = q_ref.shape[0]
    queries = stack_heads(q_ref)
    grads = stack_heads(grad_ref)
    wanted = places(pos, spans, None, (1, GROUPS * rows), 1, rows)
    lse = lse_ref[0]
    delta = jnp.zeros((1, GROUPS * rows), f32)
    for b in range(blocks):
        part = slice(b * rows, (b + 1) * rows)
        scores = dot_nt(kv_refs[b][:, :HD], queries) * SCALE - lse
        visible = places(pos, spans, b, (rows, 1), 0, rows) <= wanted
        prob = jnp.exp(jnp.where(visible, scores, NEGATIVE))
        slope = dot_nt(kv_refs[b][:, HD:], grads)
        delta = delta + jnp.sum(prob * slope, axis=0, keepdims=True)
        prob_ref[part, :] = prob
        slope_ref[part, :] = slope
        dkv_ref = other_ref if b % 2 else same_ref
        dkv_ref[rows * (b // 2) : rows * (b // 2 + 1), HD:] = dot(prob.astype(bf16), grads).astype(bf16)
    query_grad = jnp.zeros((HD, GROUPS * rows), f32)
    for b in range(blocks):
        part = slice(b * rows, (b + 1) * rows)
        dscore = (prob_ref[part, :] * (slope_ref[part, :] - delta) * SCALE).astype(bf16)
        dkv_ref = other_ref if b % 2 else same_ref
        dkv_ref[rows * (b // 2) : rows * (b // 2 + 1), :HD] = dot(dscore, queries).astype(bf16)
        query_grad = query_grad + dot_tn(kv_refs[b][:, :HD], dscore)
    query_grad = jnp.transpose(query_grad)
    for r in range(GROUPS):
        dq_ref[:, r * HD : (r + 1) * HD] = query_grad[r * rows : (r + 1) * rows].astype(bf16)


def attend_back(pos, spans, queries, grads, lse, kv_blocks, after=()):
    rows = queries.shape[0]
    blocks = len(kv_blocks)
    wide = GROUPS * HD
    by_group = pl.BlockSpec((rows, wide), lambda g, *_: (0, g))
    kv_spec = pl.BlockSpec((rows, 2 * HD), lambda g, *_: (0, g))
    return pl.pallas_call(
        functools.partial(attend_back_kernel, blocks, len(after)),
        grid_spec=pltpu.PrefetchScalarGridSpec(
            num_scalar_prefetch=2,
            grid=(KVH,),
            in_specs=[
                by_group,
                by_group,
                pl.BlockSpec((1, 1, GROUPS * rows), lambda g, *_: (g, 0, 0)),
            ]
            + [kv_spec] * blocks
            + anywhere(len(after)),
            out_specs=[by_group]
            + [pl.BlockSpec((blocks // 2 * rows, 2 * HD), lambda g, *_: (0, g))] * 2,
            scratch_shapes=[pltpu.VMEM((blocks * rows, GROUPS * rows), f32)] * 2,
        ),
        out_shape=[jax.ShapeDtypeStruct((rows, H * HD), bf16)]
        + [jax.ShapeDtypeStruct((blocks // 2 * rows, 2 * KVH * HD), bf16)] * 2,
        compiler_params=params(),
        cost_estimate=cost(20 * rows * rows * blocks * H * HD, 8 * 2**20),
    )(pos, spans, queries, grads, lse, *kv_blocks, *after)


def middle_kernel(x_ref, att_ref, w_ref, gain_ref, middle_ref, rows_ref):
    step = pl.program_id(0)
    tile = w_ref.shape[1]
    columns = pl.ds(pl.multiple_of(step * tile, tile), tile)
    middle_ref[:, columns] = x_ref[...].astype(f32) + dot(att_ref[...], w_ref[...])

    @pl.when(step == pl.num_programs(0) - 1)
    def _():
        middle = middle_ref[...]
        factor = lax.rsqrt(jnp.mean(middle * middle, axis=-1, keepdims=True) + EPSILON)
        rows_ref[...] = (middle * factor * gain_ref[...]).astype(bf16)


def middle_forward(x, attended, w_out, gain, tile=512):
    rows, width = x.shape
    return pl.pallas_call(
        middle_kernel,
        grid=(width // tile,),
        in_specs=[
            pl.BlockSpec((rows, tile), lambda n: (0, n)),
            whole(attended.shape),
            pl.BlockSpec((w_out.shape[0], tile), lambda n: (0, n)),
            whole((1, width)),
        ],
        out_specs=[whole((rows, width))] * 2,
        out_shape=[
            jax.ShapeDtypeStruct((rows, width), f32),
            jax.ShapeDtypeStruct((rows, width), bf16),
        ],
        compiler_params=params(),
        cost_estimate=cost(2 * rows * width * width, 8 * 2**20),
    )(x, attended, w_out, gain.reshape(1, width))


def middle_back_kernel(parts, *refs):
    grad_refs = refs[:parts]
    middle_ref, cot_ref, gain_ref, w_ref = refs[parts : parts + 4]
    mgrad_ref, low_ref, dgain_ref, out_ref = refs[-4:]

    @pl.when(pl.program_id(0) == 0)
    def _():
        upstream = grad_refs[0][...].astype(f32)
        for ref in grad_refs[1:]:
            upstream = upstream + ref[...].astype(f32)
        middle = middle_ref[...]
        factor = lax.rsqrt(jnp.mean(middle * middle, axis=-1, keepdims=True) + EPSILON)
        scaled = upstream * gain_ref[...]
        inner = jnp.mean(scaled * middle, axis=-1, keepdims=True)
        grad = factor * scaled - middle * (factor * factor * factor * inner)
        grad = cot_ref[...].astype(f32) + grad
        mgrad_ref[...] = grad
        low_ref[...] = grad.astype(bf16)
        dgain_ref[...] = jnp.sum(upstream * middle * factor, axis=0, keepdims=True)

    out_ref[...] = dot_nt(low_ref[...], w_ref[...]).astype(bf16)


def middle_back(grads, middle, cotangent, gain, w_out, after=(), tile=512):
    rows, width = middle.shape
    inner = w_out.shape[0]
    return pl.pallas_call(
        functools.partial(middle_back_kernel, len(grads)),
        grid=(inner // tile,),
        in_specs=[whole((rows, width))] * (len(grads) + 2)
        + [whole((1, width)), pl.BlockSpec((tile, width), lambda n: (n, 0))]
        + anywhere(len(after)),
        out_specs=[
            whole((rows, width)),
            whole((rows, width)),
            whole((1, width)),
            pl.BlockSpec((rows, tile), lambda n: (0, n)),
        ],
        out_shape=[
            jax.ShapeDtypeStruct((rows, width), f32),
            jax.ShapeDtypeStruct((rows, width), bf16),
            jax.ShapeDtypeStruct((1, width), f32),
            jax.ShapeDtypeStruct((rows, inner), bf16),
        ],
        compiler_params=params(),
        cost_estimate=cost(2 * rows * width * inner, 16 * 2**20),
    )(*grads, middle, cotangent, gain.reshape(1, width), w_out, *after)


def input_back_kernel(dq_ref, dkv_ref, wq_ref, wk_ref, wv_ref, x_ref, gain_ref, mgrad_ref, *refs):
    out_ref, dgain_ref = refs[-2:]
    step = pl.program_id(0)
    term = dot_nt(dq_ref[...], wq_ref[...])
    term = term + dot_nt(dkv_ref[:, :HD], wk_ref[...]) + dot_nt(dkv_ref[:, HD:], wv_ref[...])

    @pl.when(step == 0)
    def _():
        out_ref[...] = term

    @pl.when(step > 0)
    def _():
        out_ref[...] += term

    @pl.when(step == pl.num_programs(0) - 1)
    def _():
        upstream = out_ref[...]
        x = x_ref[...].astype(f32)
        factor = lax.rsqrt(jnp.mean(x * x, axis=-1, keepdims=True) + EPSILON)
        scaled = upstream * gain_ref[...]
        inner = jnp.mean(scaled * x, axis=-1, keepdims=True)
        out_ref[...] = mgrad_ref[...] + factor * scaled - x * (factor * factor * factor * inner)
        dgain_ref[...] = jnp.sum(upstream * x * factor, axis=0, keepdims=True)


def input_back(dq, dkv, wq, wk, wv, x, gain, mgrad, after=()):
    rows, width = x.shape
    wide = GROUPS * HD
    return pl.pallas_call(
        input_back_kernel,
        grid=(KVH,),
        in_specs=[
            pl.BlockSpec((rows, wide), lambda g: (0, g)),
            pl.BlockSpec((rows, 2 * HD), lambda g: (0, g)),
            pl.BlockSpec((width, wide), lambda g: (0, g)),
            pl.BlockSpec((width, HD), lambda g: (0, g)),
            pl.BlockSpec((width, HD), lambda g: (0, g)),
            whole((rows, width)),
            whole((1, width)),
            whole((rows, width)),
        ]
        + anywhere(len(after)),
        out_specs=[whole((rows, width)), whole((1, width))],
        out_shape=[
            jax.ShapeDtypeStruct((rows, width), f32),
            jax.ShapeDtypeStruct((1, width), f32),
        ],
        compiler_params=params(),
        cost_estimate=cost(2 * rows * width * (H + 2 * KVH) * HD, 14 * 2**20),
    )(dq, dkv, wq, wk, wv, x, gain.reshape(1, width), mgrad, *after)


def gate_column(expert, gates):
    lanes = lax.broadcasted_iota(jnp.int32, gates.shape, 1)
    chosen = (lanes == expert) | (lanes == expert + LOW_LANE)
    return jnp.sum(jnp.where(chosen, gates.astype(f32), 0.0), axis=1, keepdims=True)


def experts_kernel(per, gated, extra, keeps, pos, x_ref, c_ref, *refs):
    weights = refs[:3]
    out_ref, grad_ref, *kept_refs, acc_o, acc_g = refs[3 + extra :]
    step = pl.program_id(0)
    last = pl.num_programs(0) - 1
    width = x_ref.shape[1]
    if keeps:

        @pl.when(step == 0)
        def _():
            kept_refs[0][...] = x_ref[...]
            kept_refs[1][...] = c_ref[...]
            kept_refs[2][...] = jnp.transpose(x_ref[...])
            kept_refs[3][...] = jnp.transpose(c_ref[:, :width])

    hid_ref, dgu_ref = kept_refs[-2:]

    def work(wg_ref, wu_ref, wd_ref):
        chunk = wg_ref.shape[1]
        x = x_ref[...]
        gate = dot(x, wg_ref[...])
        up = dot(x, wu_ref[...])
        slope = dot_nt(c_ref[:, :width], wd_ref[...])
        sigmoid = 1.0 / (1.0 + jnp.exp(-gate))
        act = gate * sigmoid
        hidden = act * up
        if gated:
            held = pl.num_programs(0) // per
            expert = (2 * pos[2] + pos[3]) * held + step // per
            weight = gate_column(expert, c_ref[:, width:])
            hidden = hidden * weight
            slope = slope * weight
        hidden = hidden.astype(bf16)
        dg = (slope * up * (sigmoid * (1.0 + gate * (1.0 - sigmoid)))).astype(bf16)
        du = (slope * act).astype(bf16)
        hid_ref[...] = hidden
        dgu_ref[:, :chunk] = dg
        dgu_ref[:, chunk:] = du
        out_term = dot(hidden, wd_ref[...])
        grad_term = dot_nt(dg, wg_ref[...]) + dot_nt(du, wu_ref[...])

        @pl.when(step == 0)
        def _():
            acc_o[...] = out_term
            acc_g[...] = grad_term

        @pl.when(step > 0)
        def _():
            acc_o[...] += out_term
            acc_g[...] += grad_term

    work(*weights)

    @pl.when(step == last)
    def _():
        out_ref[...] = acc_o[...].astype(out_ref.dtype)
        grad_ref[...] = acc_g[...].astype(grad_ref.dtype)


def experts(pos, x, c, weights, part, parts, kept, gated, kind, after=(), chunk=256):
    rows, width = x.shape
    inner = weights[2].shape[1]
    per = inner // chunk
    steps = weights[0].shape[0] * per
    specs = [
        pl.BlockSpec((None, width, chunk), lambda i, _: (i // per, 0, i % per)),
        pl.BlockSpec((None, width, chunk), lambda i, _: (i // per, 0, i % per)),
        pl.BlockSpec((None, chunk, width), lambda i, _: (i // per, i % per, 0)),
    ]
    collected = [
        jax.ShapeDtypeStruct((parts * rows, steps * chunk), bf16),
        jax.ShapeDtypeStruct((parts * rows, 2 * steps * chunk), bf16),
    ]
    collected_specs = [
        pl.BlockSpec((rows, chunk), lambda i, _: (part, i)),
        pl.BlockSpec((rows, 2 * chunk), lambda i, _: (part, i)),
    ]
    if gated:
        collected = [
            jax.ShapeDtypeStruct((parts * rows, width), bf16),
            jax.ShapeDtypeStruct((parts * rows, c.shape[1]), bf16),
            jax.ShapeDtypeStruct((width, parts * rows), bf16),
            jax.ShapeDtypeStruct((width, parts * rows), bf16),
        ] + collected
        collected_specs = [
            pl.BlockSpec((rows, width), lambda i, _: (part, 0)),
            pl.BlockSpec((rows, c.shape[1]), lambda i, _: (part, 0)),
            pl.BlockSpec((width, rows), lambda i, _: (0, part)),
            pl.BlockSpec((width, rows), lambda i, _: (0, part)),
        ] + collected_specs
    operands = [pos, x, c, *weights]
    aliases = {}
    if kept is not None:
        aliases = {len(operands) + j: 2 + j for j in range(len(collected))}
        operands += list(kept)
    extra = len(after) + (0 if kept is None else len(collected))
    operands += list(after)
    result = pl.pallas_call(
        functools.partial(experts_kernel, per, gated, extra, gated),
        grid_spec=pltpu.PrefetchScalarGridSpec(
            num_scalar_prefetch=1,
            grid=(steps,),
            in_specs=[whole((rows, width)), whole(c.shape)] + specs + anywhere(extra),
            out_specs=[whole((rows, width))] * 2 + collected_specs,
            scratch_shapes=[pltpu.VMEM((rows, width), f32)] * 2,
        ),
        out_shape=[jax.ShapeDtypeStruct((rows, width), kind)] * 2 + collected,
        input_output_aliases=aliases,
        compiler_params=params(),
        cost_estimate=cost(26 * rows * width * steps * chunk, 12 * 2**20),
    )(*operands)
    return result[0], result[1], result[2:]


def others_kernel(sets, per, extra, pos, x_ref, c_ref, *refs):
    weights = refs[: 3 * sets * per]
    out_ref, grad_ref, hid_ref, dgu_ref = refs[3 * sets * per + extra :]
    step = pl.program_id(0)
    chunk = weights[0].shape[1]
    width = x_ref.shape[1]
    tile = out_ref.shape[1]

    def places(t, n):
        at = (lax.rem(pos[1] + t, 2) * per + n) * chunk
        cut = lambda first: pl.ds(pl.multiple_of(first, chunk), chunk)
        return cut(at), cut(2 * at), cut(2 * at + chunk)

    def hidden_chunk(t, n, wg_ref, wu_ref, wd_ref):
        at_hidden, at_gate, at_up = places(t, n)
        expert = (2 * pos[2] + 1 - pos[3]) * sets + lax.rem(pos[1] + t, 2)
        for p in range(2):
            half = x_ref.shape[0] // 2
            part = slice(p * half, (p + 1) * half)
            x = x_ref[part, :]
            gate = dot(x, wg_ref[...])
            up = dot(x, wu_ref[...])
            slope = dot_nt(c_ref[part, :width], wd_ref[...])
            sigmoid = 1.0 / (1.0 + jnp.exp(-gate))
            act = gate * sigmoid
            weight = gate_column(expert, c_ref[part, width:])
            slope = slope * weight
            hid_ref[part, at_hidden] = (act * up * weight).astype(bf16)
            dgu_ref[part, at_gate] = (
                slope * up * (sigmoid * (1.0 + gate * (1.0 - sigmoid)))
            ).astype(bf16)
            dgu_ref[part, at_up] = (slope * act).astype(bf16)

    for t in range(sets):
        for n in range(per):
            at = t * per + n
            pl.when(step == at)(functools.partial(hidden_chunk, t, n, *weights[3 * at : 3 * at + 3]))

    @pl.when(step >= sets * per)
    def _():
        out = grad = 0.0
        first = pl.multiple_of((step - sets * per) * tile, tile)
        for t in range(sets):
            for n in range(per):
                at = t * per + n
                wg_ref, wu_ref, wd_ref = weights[3 * at : 3 * at + 3]
                at_hidden, at_gate, at_up = places(t, n)
                out = out + dot(hid_ref[:, at_hidden], wd_ref[:, pl.ds(first, tile)])
                grad = grad + dot_nt(dgu_ref[:, at_gate], wg_ref[pl.ds(first, tile), :])
                grad = grad + dot_nt(dgu_ref[:, at_up], wu_ref[pl.ds(first, tile), :])
        out_ref[...] = out.astype(bf16)
        grad_ref[...] = grad.astype(bf16)


def others(pos, x, c, weights, after=(), tile=512):
    taken, width = x.shape
    sets, per = len(weights), len(weights[0])
    inner = per * weights[0][0][0].shape[1]
    flat = [v for one in weights for triple in one for v in triple]
    resident = lambda v: pl.BlockSpec(v.shape, lambda *_: (0, 0), pipeline_mode=pl.Buffered(1))
    late = lambda i: jnp.maximum(i - sets * per, 0)
    return pl.pallas_call(
        functools.partial(others_kernel, sets, per, len(after)),
        grid_spec=pltpu.PrefetchScalarGridSpec(
            num_scalar_prefetch=1,
            grid=(sets * per + width // tile,),
            in_specs=[resident(v) for v in [x, c] + flat] + anywhere(len(after)),
            out_specs=[pl.BlockSpec((taken, tile), lambda i, _: (0, late(i)))] * 2
            + [whole((taken, sets * inner)), whole((taken, 2 * sets * inner))],
        ),
        out_shape=[jax.ShapeDtypeStruct((taken, width), bf16)] * 2
        + [
            jax.ShapeDtypeStruct((taken, sets * inner), bf16),
            jax.ShapeDtypeStruct((taken, 2 * sets * inner), bf16),
        ],
        compiler_params=params(),
        cost_estimate=cost(26 * taken * width * sets * inner, 12 * 2**20),
    )(pos, x, c, *flat, *after)


def side_of(outer, s, pos):
    return 2 * lax.rem(s, outer) + lax.rem(pos[1] + 1 - s // outer, 2)


def halves_kernel(shape, outer, pos, *refs):
    sent_ref, kept_ref = refs[-2:]

    def write(out_ref):
        out_ref[...] = jnp.zeros_like(out_ref)
        first = 0
        for i, rows in enumerate(shape):
            total = dot_tn(refs[2 * i][...], refs[2 * i + 1][...]).astype(bf16)
            for e in range(out_ref.shape[0]):
                part = total[e * rows : (e + 1) * rows]
                out_ref[e, first : first + rows, : total.shape[1]] = part
            first += rows

    pl.when(pl.program_id(0) < outer)(lambda: write(sent_ref))
    pl.when(pl.program_id(0) >= outer)(lambda: write(kept_ref))


def halves(pos, pairs, after=()):
    n_ctx, n_exp = lax.axis_size("ctx"), lax.axis_size("exp")
    outer = n_ctx // 2
    shape = [left.shape[1] // (n_ctx * n_exp) for left, _ in pairs]
    wide = max(right.shape[1] for _, right in pairs)
    full = (outer * n_exp, sum(shape), wide)
    if any((left.shape[1] // n_ctx) % 128 for left, _ in pairs):
        out = []
        for side in (1, 0):
            parts = []
            for left, right in pairs:
                split = left.reshape(left.shape[0], outer, 2, -1)
                mine = lax.dynamic_index_in_dim(split, (pos[1] + side) % 2, 2, keepdims=False)
                total = dot_tn(mine.reshape(left.shape[0], -1), right).astype(bf16)
                total = total.reshape(outer * n_exp, -1, right.shape[1])
                parts.append(jnp.pad(total, ((0, 0), (0, 0), (0, wide - right.shape[1]))))
            out.append(jnp.concatenate(parts, axis=1))
        return out
    in_specs, operands = [], []
    for left, right in pairs:
        columns = left.shape[1] // n_ctx
        in_specs.append(
            pl.BlockSpec((left.shape[0], columns), lambda s, pos: (0, side_of(outer, s, pos)))
        )
        in_specs.append(whole(right.shape))
        operands += [left, right]
    block = (n_exp,) + full[1:]
    flops = sum(2 * left.size * right.shape[1] for left, right in pairs)
    return pl.pallas_call(
        functools.partial(halves_kernel, shape, outer),
        grid_spec=pltpu.PrefetchScalarGridSpec(
            num_scalar_prefetch=1,
            grid=(2 * outer,),
            in_specs=in_specs + anywhere(len(after)),
            out_specs=[
                pl.BlockSpec(block, lambda s, pos: (jnp.minimum(s, outer - 1), 0, 0)),
                pl.BlockSpec(block, lambda s, pos: (jnp.maximum(s - outer, 0), 0, 0)),
            ],
        ),
        out_shape=[jax.ShapeDtypeStruct(full, bf16)] * 2,
        compiler_params=params(),
        cost_estimate=cost(2 * flops, 8 * 2**20),
    )(pos, *operands, *after)


def rows_product_kernel(blocks, pos, *refs):
    total = dot_tn(refs[0][...], refs[blocks][...])
    for b in range(1, blocks):
        total = total + dot_tn(refs[b][...], refs[blocks + b][...])
    refs[-1][...] = total.astype(bf16)


def rows_product(pos, lefts, rights, tile=512):
    n_ctx, n_exp = lax.axis_size("ctx"), lax.axis_size("exp")
    depth, height = lefts[0].shape
    high, wide = height // n_ctx, rights[0].shape[1]
    if high % 128:
        place = lax.axis_index("ctx") * high
        total = sum(
            dot_tn(lax.dynamic_slice_in_dim(a, place, high, 1), b) for a, b in zip(lefts, rights)
        )
        return total.astype(bf16).reshape(n_exp, -1, wide)
    blocks = len(lefts)
    left_spec = pl.BlockSpec((depth, high), lambda n, pos: (0, 2 * pos[0] + pos[1]))
    total = pl.pallas_call(
        functools.partial(rows_product_kernel, blocks),
        grid_spec=pltpu.PrefetchScalarGridSpec(
            num_scalar_prefetch=1,
            grid=(wide // tile,),
            in_specs=[left_spec] * blocks
            + [pl.BlockSpec((depth, tile), lambda n, pos: (0, n))] * blocks,
            out_specs=pl.BlockSpec((high, tile), lambda n, pos: (0, n)),
        ),
        out_shape=jax.ShapeDtypeStruct((high, wide), bf16),
        compiler_params=params(),
        cost_estimate=cost(4 * blocks * depth * high * wide, 4 * 2**20),
    )(pos, *lefts, *rights)
    return total.reshape(n_exp, -1, wide)


def expert_halves_kernel(outer, tiles, pos, rows_ref, cot_ref, dgu_ref, hid_ref, *refs):
    sent_ref, kept_ref = refs[-2:]
    s, n = pl.program_id(0), pl.program_id(1)

    def write(left_ref, right_ref):
        total = dot(left_ref[...], right_ref[...]).astype(bf16)

        def put(out_ref):
            for i in range(out_ref.shape[0]):
                out_ref[i] = total[i * out_ref.shape[1] : (i + 1) * out_ref.shape[1]]

        pl.when(s < outer)(lambda: put(sent_ref))
        pl.when(s >= outer)(lambda: put(kept_ref))

    pl.when(n < tiles)(lambda: write(rows_ref, dgu_ref))
    pl.when(n >= tiles)(lambda: write(cot_ref, hid_ref))


def expert_steps(width):
    high = width // lax.axis_size("ctx")
    return high // 128 if high % 128 == 0 else 1


def expert_halves(pos, rows_t, cot_t, dgu, hid, after=(), tile=1024):
    n_ctx = lax.axis_size("ctx")
    outer = n_ctx // 2
    width, depth = rows_t.shape
    high = width // n_ctx
    wide = dgu.shape[1] + hid.shape[1]
    tiles, down = dgu.shape[1] // tile, hid.shape[1] // tile
    steps = expert_steps(width)
    left_spec = pl.BlockSpec((high, depth), lambda s, n, pos: (side_of(outer, s, pos), 0))
    last = tiles + down - 1
    return pl.pallas_call(
        functools.partial(expert_halves_kernel, outer, tiles),
        grid_spec=pltpu.PrefetchScalarGridSpec(
            num_scalar_prefetch=1,
            grid=(2 * outer, tiles + down),
            in_specs=[
                left_spec,
                left_spec,
                pl.BlockSpec((depth, tile), lambda s, n, pos: (0, jnp.minimum(n, tiles - 1))),
                pl.BlockSpec((depth, tile), lambda s, n, pos: (0, jnp.maximum(n - tiles, 0))),
            ]
            + anywhere(len(after)),
            out_specs=[
                pl.BlockSpec(
                    (steps, high // steps, tile),
                    lambda s, n, pos: (jnp.minimum(s, outer - 1), 0, jnp.where(s < outer, n, last)),
                ),
                pl.BlockSpec(
                    (steps, high // steps, tile),
                    lambda s, n, pos: (jnp.maximum(s - outer, 0), 0, jnp.where(s < outer, 0, n)),
                ),
            ],
        ),
        out_shape=[jax.ShapeDtypeStruct((outer * steps, high // steps, wide), bf16)] * 2,
        compiler_params=params(),
        cost_estimate=cost(4 * depth * width * wide, 16 * 2**20),
    )(pos, rows_t, cot_t, dgu, hid, *after)


def sums_kernel(shape, extra, pos, *refs):
    ins, outs = refs[: sum(shape)], refs[sum(shape) + extra :]
    at = 0
    for count, out in zip(shape, outs):
        total = ins[at][...].astype(f32)
        for ref in ins[at + 1 : at + count]:
            total = total + ref[...].astype(f32)
        out[...] = total.astype(out.dtype)
        at += count


def sums(pos, steps, outputs, after=()):
    operands, in_specs, out_specs, out_shape = [], [], [], []
    for kind, block, terms in outputs:
        block = (1,) + tuple(block)
        for array, index in terms:
            operands.append(array)
            in_specs.append(pl.BlockSpec(block, functools.partial(place_of, index)))
        out_specs.append(pl.BlockSpec(block, lambda i, pos: (i, 0, 0)))
        out_shape.append(jax.ShapeDtypeStruct((steps,) + block[1:], kind))
    return pl.pallas_call(
        functools.partial(sums_kernel, [len(terms) for _, _, terms in outputs], len(after)),
        grid_spec=pltpu.PrefetchScalarGridSpec(
            num_scalar_prefetch=1,
            grid=(steps,),
            in_specs=in_specs + anywhere(len(after)),
            out_specs=out_specs,
        ),
        out_shape=out_shape,
        compiler_params=params(),
        cost_estimate=cost(0, 8 * 2**20),
    )(pos, *operands, *after)


def place_of(index, i, pos):
    at = index(i, pos)
    return at if isinstance(at, tuple) else (at, 0, 0)


def straight(i, pos):
    return i


def row_sum(terms, kind=bf16):
    total = terms[0].astype(f32)
    for term in terms[1:]:
        total = total + term.astype(f32)
    return total.astype(kind)


def expert_out_kernel(gates, each, *refs):
    in_refs, (gate_ref, up_ref, down_ref) = refs[:4], refs[4:]
    n = pl.program_id(0)

    def write(ref):
        @pl.when((n < gates) & (lax.rem(n, 2) == 0))
        def _():
            gate_ref[0] = ref[...].astype(f32)

        @pl.when((n < gates) & (lax.rem(n, 2) == 1))
        def _():
            up_ref[0] = ref[...].astype(f32)

        @pl.when(n >= gates)
        def _():
            down_ref[0] = jnp.transpose(ref[...].astype(f32))

    for q in range(4):
        pl.when(n // each == q)(functools.partial(write, in_refs[q]))


def expert_out(quarters, inner, chunk=256):
    rows, wide = quarters[0].shape
    each = wide // chunk
    held = 4 * wide // (3 * inner)
    per = inner // chunk
    gates = 2 * held * per
    tile = lambda n: jnp.minimum(n, gates - 1) // 2
    spec = pl.BlockSpec((1, rows, chunk), lambda n: (tile(n) // per, 0, lax.rem(tile(n), per)))
    at = lambda n: jnp.maximum(n - gates, 0)
    return pl.pallas_call(
        functools.partial(expert_out_kernel, gates, each),
        grid=(4 * each,),
        in_specs=[
            pl.BlockSpec(
                (rows, chunk),
                functools.partial(lambda q, n: (0, jnp.clip(n - q * each, 0, each - 1)), q),
            )
            for q in range(4)
        ],
        out_specs=[
            spec,
            spec,
            pl.BlockSpec((1, chunk, rows), lambda n: (at(n) // per, lax.rem(at(n), per), 0)),
        ],
        out_shape=[jax.ShapeDtypeStruct((held, rows, inner), f32)] * 2
        + [jax.ShapeDtypeStruct((held, inner, rows), f32)],
        compiler_params=params(),
        cost_estimate=cost(0, 8 * 2**20),
    )(*quarters)


def hold(values, after):
    count = len(values)
    return pl.pallas_call(
        lambda *_: None,
        in_specs=[pl.BlockSpec(memory_space=pl.ANY)] * (count + len(after)),
        out_specs=[pl.BlockSpec(memory_space=pl.ANY)] * count,
        out_shape=[jax.ShapeDtypeStruct(v.shape, v.dtype) for v in values],
        input_output_aliases={i: i for i in range(count)},
        compiler_params=params(),
        cost_estimate=cost(0, 0),
    )(*values, *after)


def swap_inner(value, axis):
    size = lax.axis_size(axis)
    return lax.ppermute(value, axis, [(i, i ^ 1) for i in range(size)])


def shift_outer(value, axis, by):
    outer = lax.axis_size(axis) // 2
    perm = [(o * 2 + i, ((o + by) % outer) * 2 + i) for o in range(outer) for i in range(2)]
    return lax.ppermute(value, axis, perm)


def ring_step(value, by):
    n_ctx, n_exp = lax.axis_size("ctx"), lax.axis_size("exp")
    outer = n_exp // 2
    perm = []
    for c in range(n_ctx):
        way = by if c % 2 == 0 else -by
        for o in range(outer):
            for i in range(2):
                perm.append((c * n_exp + o * 2 + i, c * n_exp + ((o + way) % outer) * 2 + i))
    return lax.ppermute(value, BOTH, perm)


def by_blocks(value, together):
    return value.reshape(-1, together * value.shape[1], value.shape[2])


def spread_outer(value):
    moved, out = value, []
    for _ in range(1, lax.axis_size("ctx") // 2):
        moved = shift_outer(moved, "ctx", 1)
        out.append(moved)
    return out, swap_inner(value, "ctx")


def spread_inner(moved):
    return [swap_inner(v, "ctx") for v in moved]


def spread_all(value, moved, across, moved_across):
    blocks = [value, across]
    for a, b in zip(moved, moved_across):
        blocks += [a, b]
    return blocks


def shared_x_send(pos, kept, got):
    outer, levels = lax.axis_size("ctx") // 2, lax.axis_size("exp") // 2
    outputs = []
    for y in range(outer):
        index = functools.partial(
            lambda y, i, pos: (y * levels + i) * 2 + 1 - pos[3], y
        )
        outputs.append((bf16, kept.shape[1:], [(v, index) for v in (kept, got)]))
    return sums(pos, levels, outputs)


def shared_terms(kept, got, arrived, d):
    outer, levels = lax.axis_size("ctx") // 2, lax.axis_size("exp") // 2
    place = lambda pos: lax.rem(pos[0] + d, outer) * levels
    terms = [(v, lambda i, pos: (place(pos) + i) * 2 + pos[3]) for v in (kept, got)]
    return terms + [(arrived, lambda i, pos: place(pos) + i)]


def shared_y(pos, kept, got, arrived):
    outer, levels = lax.axis_size("ctx") // 2, lax.axis_size("exp") // 2
    out = []
    for d in range(1, outer):
        terms = shared_terms(kept, got, arrived, d)
        (sent,) = sums(pos, levels, [(bf16, kept.shape[1:], terms)])
        out.append(shift_outer(sent, "ctx", d))
    return out


def shared_total(pos, kept, got, arrived, moved):
    levels = lax.axis_size("exp") // 2
    terms = shared_terms(kept, got, arrived, 0) + [(v, straight) for v in moved]
    (total,) = sums(pos, levels, [(bf16, kept.shape[1:], terms)])
    return total


def z_take(total, d):
    levels = total.shape[0]
    return lax.dynamic_index_in_dim(total, (lax.axis_index("exp") // 2 + d) % levels, 0, False)


def z_send(total, d):
    return shift_outer(z_take(total, d), "exp", d)


def over_x(total):
    pairs = total.reshape((-1, 2) + total.shape[1:])
    return swap_inner(lax.dynamic_index_in_dim(pairs, 1 - lax.axis_index("exp") % 2, 1, False), "exp")


def over_z(total, arrived):
    pairs = total.reshape((-1, 2) + total.shape[1:])
    mine = lax.dynamic_index_in_dim(pairs, lax.axis_index("exp") % 2, 1, False)
    mine = mine.astype(f32) + arrived.astype(f32)
    levels, level = mine.shape[0], lax.axis_index("exp") // 2
    take = lambda d: lax.dynamic_index_in_dim(mine, (level + d) % levels, 0, False)
    return [take(0)] + [shift_outer(take(d).astype(bf16), "exp", d) for d in range(1, levels)]


def dense_result(pairs, terms):
    devices = lax.axis_size("ctx") * lax.axis_size("exp")
    out, first = [], 0
    for left, right in pairs:
        rows = left.shape[1] // devices
        out.append(sum(t[first : first + rows, : right.shape[1]].astype(f32) for t in terms))
        first += rows
    return out


def expert_quarter(kept, got, q, row):
    block = (kept.shape[1], kept.shape[2] // 4)
    return block, [(v, lambda i, pos: (row(i, pos), 0, q)) for v in (kept, got)]


def expert_pieces(pos, kept, got, quarters):
    outputs = []
    for q in quarters:
        block, terms = expert_quarter(kept, got, q, straight)
        outputs.append((bf16, block, terms))
    return sums(pos, kept.shape[0], outputs)


def expert_rows(kept, d):
    outer = lax.axis_size("ctx") // 2
    steps = kept.shape[0] // outer
    return steps, lambda i, pos: lax.rem(pos[0] + d, outer) * steps + i


def expert_send(pos, kept, got, pieces, quarters):
    sent = []
    for d in range(1, lax.axis_size("ctx") // 2):
        steps, row = expert_rows(kept, d)
        outputs = []
        for q in quarters:
            block, terms = expert_quarter(kept, got, q, row)
            outputs.append((bf16, block, terms + [(pieces[q], row)]))
        sent.append(sums(pos, steps, outputs))
    return sent


def expert_move(sent):
    return [[shift_outer(v, "ctx", d + 1) for v in part] for d, part in enumerate(sent)]


def expert_total(pos, kept, got, pieces, arrived):
    steps, row = expert_rows(kept, 0)
    outputs = []
    for q in range(4):
        block, terms = expert_quarter(kept, got, q, row)
        terms = terms + [(pieces[q], row)] + [(v, straight) for v in arrived[q]]
        outputs.append((bf16, block, terms))
    return [v.reshape(-1, v.shape[2]) for v in sums(pos, steps, outputs)]


def shards(
    layer_input,
    attn_gain,
    w_query,
    w_key,
    w_value,
    w_out,
    ffn_gain,
    shared_gate,
    shared_up,
    shared_down,
    expert_gate,
    expert_up,
    expert_down,
    routes,
    gate_logits,
    span_order,
    cotangent,
):
    x = layer_input[0]
    cot = cotangent[0]
    tokens, width = x.shape
    span_rows = tokens // 2
    n_ctx, n_exp = lax.axis_size("ctx"), lax.axis_size("exp")
    ctx_id, exp_id = lax.axis_index("ctx"), lax.axis_index("exp")
    local_experts, _, inner = expert_gate.shape
    expert_count = local_experts * n_exp

    levels = n_exp // 2
    pos = jnp.stack([ctx_id // 2, ctx_id % 2, exp_id // 2, exp_id % 2]).astype(jnp.int32)

    always = pos[0] < n_ctx
    ring = n_ctx // 2

    def region(work):
        made = jax.eval_shape(work)
        return lax.cond(always, work, lambda: jax.tree.map(lambda v: jnp.zeros(v.shape, v.dtype), made))

    gate_vals = jax.nn.softmax(gate_logits[0], axis=-1)
    named = routes[0][:, None, :] == jnp.arange(expert_count, dtype=jnp.int32)[None, :, None]
    row_gates = jnp.sum(jnp.where(named, gate_vals[:, None, :], 0.0), axis=-1)
    high = row_gates.astype(bf16)
    low = (row_gates - high.astype(f32)).astype(bf16)
    fill = lambda width: ((0, 0), (0, width - expert_count))
    cot_ring = [
        jnp.concatenate(
            [cot, jnp.pad(high, fill(LOW_LANE)), jnp.pad(low, fill(GATE_LANES - LOW_LANE))], axis=1
        )
    ]

    normed, kv = keyvalue(x, attn_gain, w_key, w_value)
    chunk = 256
    per = inner // chunk

    def fetch(part):
        which, n = part % 3, part // 3
        array = (expert_gate, expert_up, expert_down)[which]
        mine = lax.dynamic_index_in_dim(array, pos[1], 0, keepdims=False)
        dim = 0 if which == 2 else 1
        return swap_inner(lax.slice_in_dim(mine, n * chunk, (n + 1) * chunk, axis=dim), "exp")

    fetches = [range(0, 1), range(1, 2), range(2, 4), range(4, 5), range(5, 3 * per)]

    def fetch_some(k):
        return [fetch(p) for p in fetches[k]]

    def gather_keys():
        moved, across = spread_outer(kv)
        queries = dot(normed, w_query).astype(bf16)
        return moved, across, spread_inner(moved), queries, ring_step(cot_ring[0], 1), fetch_some(0)

    moved, across, moved_across, queries, cot_next, fetched = region(gather_keys)
    kv_blocks = spread_all(kv, moved, across, moved_across)
    cot_ring.append(cot_next)

    def attention():
        attended, lse = attend(pos, span_order, queries, kv_blocks)
        middle, rows = middle_forward(x, attended, w_out, ffn_gain)
        moved = spread_outer(normed), ring_step(cot_ring[1], 1), fetch_some(1)
        return attended, lse, middle, rows, *moved

    attended, lse, middle, rows_low, normed_moved, cot_next, got = region(attention)
    fetched += got
    cot_ring.append(cot_next)

    def own_part(k, rows, kept):
        weights = (expert_gate, expert_up, expert_down)
        return experts(pos, rows, cot_ring[k], weights, k, levels, kept, True, bf16)

    def first():
        weights = (shared_gate[None], shared_up[None], shared_down[None])
        shared = experts(pos, rows_low, cot, weights, 0, 1, None, False, f32)
        moved = ring_step(rows_low, 1), ring_step(cot_ring[2], 1)
        more = spread_outer(attended), spread_inner(normed_moved[0]), fetch_some(2)
        return moved, shared, own_part(0, rows_low, None), *more

    moved, shared, (out_k, grad_k, kept), attended_moved, normed_across, got = region(first)
    fetched += got
    normed_blocks = spread_all(normed, *normed_moved, normed_across)
    shared_out, shared_grad, (shared_hidden, shared_dgu) = shared
    rows_k = moved[0]
    cot_ring.append(moved[1])
    out_own, grad_own = [out_k], [grad_k]
    shared_pairs = [(rows_low, shared_dgu), (shared_hidden, cot)]

    def second():
        result = own_part(1, rows_k, kept)
        across = spread_inner(attended_moved[0])
        return ring_step(rows_k, 1), result, halves(pos, shared_pairs), across, fetch_some(3)

    rows_next, (out_k, grad_k, kept), (shared_sent, shared_kept), across, got = region(second)
    fetched += got
    attended_blocks = spread_all(attended, *attended_moved, across)
    rows_k = rows_next
    out_own.append(out_k)
    grad_own.append(grad_k)

    def third():
        result = own_part(2, rows_k, kept)
        moved = ring_step(rows_k, 1), swap_inner(shared_sent, "ctx"), fetch_some(4)
        return result, [swap_inner(v, "ctx") for v in fetched], *moved

    (out_k, grad_k, kept), fetched_b, rows_next, shared_got, got = region(third)
    fetched += got
    rows_k = rows_next
    out_own.append(out_k)
    grad_own.append(grad_k)

    def fourth():
        across = fetched_b + [swap_inner(v, "ctx") for v in fetched[len(fetched_b) :]]
        sent = shared_x_send(pos, shared_kept, shared_got)
        got = [swap_inner(v, "exp") for v in sent[: ring // 2]]
        out_k, grad_k, new = own_part(3, rows_k, kept)
        weights = [[v[3 * n : 3 * n + 3] for n in range(per)] for v in (fetched, across)]
        return out_k, grad_k, new, others(pos, new[0], new[1], weights), got, sent[ring // 2 :]

    out_k, grad_k, kept, other, shared_first, shared_rest = region(fourth)
    out_own.append(out_k)
    grad_own.append(grad_k)
    rows_all, cot_all, rows_t, cot_t, hid_own, dgu_own = kept
    out_other, grad_other, hid_other, dgu_other = other
    split = lambda v: [v[k * tokens : (k + 1) * tokens] for k in range(levels)]
    out_other, grad_other = split(out_other), split(grad_other)

    def back_one():
        moved = ring_step(row_sum([grad_own[3], grad_other[3]]), -1)
        made = expert_halves(pos, rows_t, cot_t, dgu_other, hid_other)
        return moved, made, [swap_inner(v, "exp") for v in shared_rest]

    moved, (sent, kept_other), shared_second = region(back_one)
    shared_x = jnp.concatenate(shared_first + shared_second, axis=0)

    def back_two():
        total = row_sum([grad_own[2], grad_other[2], moved])
        got = swap_inner(sent, "ctx")
        made = expert_halves(pos, rows_t, cot_t, dgu_own, hid_own)
        shared_moved = shared_y(pos, shared_kept, shared_got, shared_x)
        return ring_step(total, -1), got, made, expert_pieces(pos, kept_other, got, [0])[0], shared_moved

    moved_two, got_other, (sent_own, kept_own), piece, shared_moved = region(back_two)

    def back_three():
        total = row_sum([grad_own[1], grad_other[1], moved_two])
        pieces = expert_pieces(pos, kept_other, got_other, [1, 2, 3])
        shared_sum = shared_total(pos, shared_kept, shared_got, shared_x, shared_moved)
        out_total = row_sum([out_own[3], out_other[3]])
        moved = ring_step(total, -1), swap_inner(sent_own, "ctx"), swap_inner(piece, "exp")
        return *moved, pieces, shared_sum, out_total

    moved, got_own, piece, pieces, shared_sum, out_total = region(back_three)
    pieces = [piece] + list(pieces)

    def attention_back():
        mgrad, mgrad_low, ffn_gain_grad, att_grad = middle_back(
            [shared_grad, grad_own[0], grad_other[0], moved], middle, cot, ffn_gain, w_out
        )
        back = attend_back(pos, span_order, queries, att_grad, lse, kv_blocks)
        out_moved = ring_step(out_total, -1)
        got = swap_inner(pieces[1], "exp"), z_send(shared_sum, 1), expert_move(expert_send(pos, kept_own, got_own, pieces, [0]))
        return mgrad, mgrad_low, spread_outer(mgrad_low), ffn_gain_grad, back, out_moved, *got

    mgrad, mgrad_low, mgrad_moved, ffn_gain_grad, (dq, same, across), out_moved, piece, shared_z, got = (
        region(attention_back)
    )
    pieces[1] = piece
    arrived = [[a[0] for a in got]]
    shared_z = [shared_z]

    def dense_one():
        got = swap_inner(across, "ctx")
        made = []
        for k in reversed(range(ring)):
            part = slice(k * tokens, (k + 1) * tokens)
            made = row_sum([same[part], got[part]] + made)
            if k:
                made = [shift_outer(made, "ctx", -1)]
        total = row_sum([out_own[2], out_other[2], out_moved])
        mgrad_across = spread_inner(mgrad_moved[0])
        moved = ring_step(total, -1), swap_inner(pieces[2], "exp"), z_send(shared_sum, 2)
        return made, spread_outer(dq), mgrad_across, *moved

    dkv, dq_moved, mgrad_across, out_moved_two, piece, got = region(dense_one)
    shared_z.append(got)
    mgrad_blocks = spread_all(mgrad_low, *mgrad_moved, mgrad_across)
    pieces[2] = piece

    def dense_two():
        total = row_sum([out_own[1], out_other[1], out_moved_two])
        moved = ring_step(total, -1)
        dq_across = spread_inner(dq_moved[0])
        total_out = rows_product(pos, attended_blocks, mgrad_blocks)
        back = input_back(dq, dkv, w_query, w_key, w_value, x, attn_gain, mgrad)
        got = expert_move(expert_send(pos, kept_own, got_own, pieces, [1]))
        more = moved, swap_inner(pieces[3], "exp"), z_send(shared_sum, 3), got
        return spread_outer(dkv), dq_across, total_out, back, *more

    dkv_moved, dq_across, total_out, (input_grad, attn_gain_grad), out_moved_three, piece, last_z, got = (
        region(dense_two)
    )
    shared_z.append(last_z)
    arrived.append([a[0] for a in got])
    dq_blocks = spread_all(dq, *dq_moved, dq_across)
    pieces[3] = piece

    def dense_three():
        devices = n_ctx * n_exp
        moved = expert_move(expert_send(pos, kept_own, got_own, pieces, [2, 3]))
        got = arrived + [[a[q] for a in moved] for q in range(2)]
        total_query = rows_product(pos, normed_blocks, dq_blocks)
        dkv_blocks = spread_all(dkv, *dkv_moved, spread_inner(dkv_moved[0]))
        total_kv = rows_product(pos, normed_blocks, dkv_blocks)
        shared_parts = [z_take(shared_sum, 0)] + shared_z
        dense = [over_z(t, over_x(t)) for t in (total_out, total_query, total_kv)]
        layer_out = row_sum([middle, shared_out, out_own[0], out_other[0], out_moved_three])
        gains = jnp.stack(
            [attn_gain_grad.reshape(devices, -1), ffn_gain_grad.reshape(devices, -1)], axis=1
        )
        gains = lax.all_to_all(gains, BOTH, split_axis=0, concat_axis=0, tiled=True)
        grads = expert_out(expert_total(pos, kept_own, got_own, pieces, got), inner)
        pairs = [(attended, mgrad), (normed, dq), (normed, dkv)]
        dense = [dense_result([p], t)[0] for p, t in zip(pairs, dense)]
        return layer_out, jnp.sum(gains, axis=0), dense_result(shared_pairs, shared_parts), dense, grads

    layer_out, gains, (sum_gate_up, sum_down), (sum_out, sum_query, sum_kv), expert_grads = region(
        dense_three
    )
    shared_rows = sum_gate_up.reshape(sum_gate_up.shape[0], -1, 2, 256)
    kv_rows = sum_kv.reshape(sum_kv.shape[0], KVH, 2, HD)
    return (
        layer_out[None],
        input_grad[None],
        gains[0],
        sum_query,
        kv_rows[:, :, 0].reshape(sum_kv.shape[0], -1),
        kv_rows[:, :, 1].reshape(sum_kv.shape[0], -1),
        sum_out,
        gains[1],
        shared_rows[:, :, 0].reshape(sum_gate_up.shape[0], -1),
        shared_rows[:, :, 1].reshape(sum_gate_up.shape[0], -1),
        sum_down,
        *expert_grads,
    )


def solution(mesh):
    return jax.shard_map(
        shards,
        mesh=mesh,
        in_specs=(
            P("exp", "ctx", None),
            P(),
            P(),
            P(),
            P(),
            P(),
            P(),
            P(),
            P(),
            P(),
            P("exp", None, None),
            P("exp", None, None),
            P("exp", None, None),
            P("exp", "ctx", None),
            P("exp", "ctx", None),
            P(),
            P("exp", "ctx", None),
        ),
        out_specs=(
            P("exp", "ctx", None),
            P("exp", "ctx", None),
            P(("ctx", "exp")),
            P(("ctx", "exp"), None),
            P(("ctx", "exp"), None),
            P(("ctx", "exp"), None),
            P(("ctx", "exp"), None),
            P(("ctx", "exp")),
            P(("ctx", "exp"), None),
            P(("ctx", "exp"), None),
            P(("ctx", "exp"), None),
            P("exp", "ctx", None),
            P("exp", "ctx", None),
            P("exp", None, "ctx"),
        ),
        check_vma=False,
    )
```

```python
import functools

import jax
import jax.numpy as jnp
from jax import lax
from jax.experimental import pallas as pl
from jax.experimental.pallas import tpu as pltpu
from jax.sharding import PartitionSpec as P

H = 12
HD = 128
KVH = 4
GROUPS = H // KVH
EPSILON = 1e-06
GATE_LANES = 128
LOW_LANE = 64
NEGATIVE = -1e30
SCALE = HD ** (-0.5)
BOTH = ("ctx", "exp")
VMEM_LIMIT = 60 * 2**20
bf16 = jnp.bfloat16
f32 = jnp.float32


def dot(left_op, right_op):
    return jnp.dot(left_op, right_op, preferred_element_type=f32)


def dot_nt(left_op, right_op):
    return lax.dot_general(left_op, right_op, (((1,), (1,)), ((), ())), preferred_element_type=f32)


def dot_tn(left_op, right_op):
    return lax.dot_general(left_op, right_op, (((0,), (0,)), ((), ())), preferred_element_type=f32)


def whole(shape):
    return pl.BlockSpec(shape, lambda *_: (0,) * len(shape))


def params():
    return pltpu.CompilerParams(vmem_limit_bytes=VMEM_LIMIT)


def anywhere(count):
    return [pl.BlockSpec(memory_space=pl.ANY)] * count


def cost(flops, nbytes):
    return pl.CostEstimate(flops=flops // 4, bytes_accessed=nbytes // 4, transcendentals=0)


def keyvalue_kernel(x_ref, gain_ref, wk_ref, wv_ref, normed_ref, kv_ref):
    @pl.when(pl.program_id(0) == 0)
    def _():
        x = x_ref[...].astype(f32)
        factor = lax.rsqrt(jnp.mean(x * x, axis=-1, keepdims=True) + EPSILON)
        normed_ref[...] = (x * factor * gain_ref[...]).astype(bf16)

    both = jnp.concatenate([wk_ref[...], wv_ref[...]], axis=1)
    kv_ref[...] = dot(normed_ref[...], both).astype(bf16)


def keyvalue(x, gain, wk, wv):
    rows, width = x.shape
    return pl.pallas_call(
        keyvalue_kernel,
        grid=(KVH,),
        in_specs=[
            whole((rows, width)),
            whole((1, width)),
            pl.BlockSpec((width, HD), lambda g: (0, g)),
            pl.BlockSpec((width, HD), lambda g: (0, g)),
        ],
        out_specs=[whole((rows, width)), pl.BlockSpec((rows, 2 * HD), lambda g: (0, g))],
        out_shape=[
            jax.ShapeDtypeStruct((rows, width), bf16),
            jax.ShapeDtypeStruct((rows, 2 * KVH * HD), bf16),
        ],
        compiler_params=params(),
        cost_estimate=cost(4 * rows * width * KVH * HD, 5 * 2**20),
    )(x, gain.reshape(1, width), wk, wv)


def stack_heads(ref):
    return jnp.concatenate([ref[:, r * HD : (r + 1) * HD] for r in range(GROUPS)], axis=0)


def places(pos, spans, block, shape, dim, rows):
    outer, side = (0, 0) if block is None else (block // 2, block % 2)
    ring = spans.shape[0] // 4
    owner = 2 * lax.rem(pos[0] + ring - outer, ring) + lax.rem(pos[1] + side, 2)
    row = lax.broadcasted_iota(jnp.int32, shape, dim) % rows
    half = rows // 2
    first, second = spans[2 * owner] * half, spans[2 * owner + 1] * half
    return jnp.where(row < half, first + row, second + row - half)


def attend_kernel(blocks, extra, pos, spans, q_ref, *refs):
    kv_refs = refs[:blocks]
    out_ref, lse_ref, score_ref = refs[blocks + extra :]
    rows = q_ref.shape[0]
    queries = stack_heads(q_ref)
    wanted = places(pos, spans, None, (1, GROUPS * rows), 1, rows)
    peak = jnp.full((1, GROUPS * rows), NEGATIVE, f32)
    for b in range(blocks):
        scores = dot_nt(kv_refs[b][:, :HD], queries) * SCALE
        visible = places(pos, spans, b, (rows, 1), 0, rows) <= wanted
        scores = jnp.where(visible, scores, NEGATIVE)
        score_ref[b * rows : (b + 1) * rows, :] = scores
        peak = jnp.maximum(peak, jnp.max(scores, axis=0, keepdims=True))
    total = jnp.zeros_like(peak)
    mixed = jnp.zeros((HD, GROUPS * rows), f32)
    for b in range(blocks):
        weights = jnp.exp(score_ref[b * rows : (b + 1) * rows, :] - peak)
        total = total + jnp.sum(weights, axis=0, keepdims=True)
        mixed = mixed + dot_tn(kv_refs[b][:, HD:], weights.astype(bf16))
    lse_ref[0] = peak + jnp.log(total)
    mixed = jnp.transpose(mixed / total)
    for r in range(GROUPS):
        out_ref[:, r * HD : (r + 1) * HD] = mixed[r * rows : (r + 1) * rows].astype(bf16)


def attend(pos, spans, queries, kv_blocks, after=()):
    rows = queries.shape[0]
    blocks = len(kv_blocks)
    wide = GROUPS * HD
    return pl.pallas_call(
        functools.partial(attend_kernel, blocks, len(after)),
        grid_spec=pltpu.PrefetchScalarGridSpec(
            num_scalar_prefetch=2,
            grid=(KVH,),
            in_specs=[pl.BlockSpec((rows, wide), lambda g, *_: (0, g))]
            + [pl.BlockSpec((rows, 2 * HD), lambda g, *_: (0, g))] * blocks
            + anywhere(len(after)),
            out_specs=[
                pl.BlockSpec((rows, wide), lambda g, *_: (0, g)),
                pl.BlockSpec((1, 1, GROUPS * rows), lambda g, *_: (g, 0, 0)),
            ],
            scratch_shapes=[pltpu.VMEM((blocks * rows, GROUPS * rows), f32)],
        ),
        out_shape=[
            jax.ShapeDtypeStruct((rows, H * HD), bf16),
            jax.ShapeDtypeStruct((KVH, 1, GROUPS * rows), f32),
        ],
        compiler_params=params(),
        cost_estimate=cost(8 * rows * rows * blocks * H * HD, 4 * 2**20),
    )(pos, spans, queries, *kv_blocks, *after)


def attend_back_kernel(blocks, extra, pos, spans, q_ref, grad_ref, lse_ref, *refs):
    kv_refs = refs[:blocks]
    dq_ref, same_ref, other_ref = refs[blocks + extra : -2]
    prob_ref, slope_ref = refs[-2:]
    rows = q_ref.shape[0]
    queries = stack_heads(q_ref)
    grads = stack_heads(grad_ref)
    wanted = places(pos, spans, None, (1, GROUPS * rows), 1, rows)
    lse = lse_ref[0]
    delta = jnp.zeros((1, GROUPS * rows), f32)
    for b in range(blocks):
        part = slice(b * rows, (b + 1) * rows)
        scores = dot_nt(kv_refs[b][:, :HD], queries) * SCALE - lse
        visible = places(pos, spans, b, (rows, 1), 0, rows) <= wanted
        prob = jnp.exp(jnp.where(visible, scores, NEGATIVE))
        slope = dot_nt(kv_refs[b][:, HD:], grads)
        delta = delta + jnp.sum(prob * slope, axis=0, keepdims=True)
        prob_ref[part, :] = prob
        slope_ref[part, :] = slope
        dkv_ref = other_ref if b % 2 else same_ref
        dkv_ref[rows * (b // 2) : rows * (b // 2 + 1), HD:] = dot(prob.astype(bf16), grads).astype(bf16)
    query_grad = jnp.zeros((HD, GROUPS * rows), f32)
    for b in range(blocks):
        part = slice(b * rows, (b + 1) * rows)
        dscore = (prob_ref[part, :] * (slope_ref[part, :] - delta) * SCALE).astype(bf16)
        dkv_ref = other_ref if b % 2 else same_ref
        dkv_ref[rows * (b // 2) : rows * (b // 2 + 1), :HD] = dot(dscore, queries).astype(bf16)
        query_grad = query_grad + dot_tn(kv_refs[b][:, :HD], dscore)
    query_grad = jnp.transpose(query_grad)
    for r in range(GROUPS):
        dq_ref[:, r * HD : (r + 1) * HD] = query_grad[r * rows : (r + 1) * rows].astype(bf16)


def attend_back(pos, spans, queries, grads, lse, kv_blocks, after=()):
    rows = queries.shape[0]
    blocks = len(kv_blocks)
    wide = GROUPS * HD
    by_group = pl.BlockSpec((rows, wide), lambda g, *_: (0, g))
    kv_spec = pl.BlockSpec((rows, 2 * HD), lambda g, *_: (0, g))
    return pl.pallas_call(
        functools.partial(attend_back_kernel, blocks, len(after)),
        grid_spec=pltpu.PrefetchScalarGridSpec(
            num_scalar_prefetch=2,
            grid=(KVH,),
            in_specs=[
                by_group,
                by_group,
                pl.BlockSpec((1, 1, GROUPS * rows), lambda g, *_: (g, 0, 0)),
            ]
            + [kv_spec] * blocks
            + anywhere(len(after)),
            out_specs=[by_group]
            + [pl.BlockSpec((blocks // 2 * rows, 2 * HD), lambda g, *_: (0, g))] * 2,
            scratch_shapes=[pltpu.VMEM((blocks * rows, GROUPS * rows), f32)] * 2,
        ),
        out_shape=[jax.ShapeDtypeStruct((rows, H * HD), bf16)]
        + [jax.ShapeDtypeStruct((blocks // 2 * rows, 2 * KVH * HD), bf16)] * 2,
        compiler_params=params(),
        cost_estimate=cost(20 * rows * rows * blocks * H * HD, 8 * 2**20),
    )(pos, spans, queries, grads, lse, *kv_blocks, *after)


def middle_kernel(x_ref, att_ref, w_ref, gain_ref, middle_ref, rows_ref):
    step = pl.program_id(0)
    tile = w_ref.shape[1]
    columns = pl.ds(pl.multiple_of(step * tile, tile), tile)
    middle_ref[:, columns] = x_ref[...].astype(f32) + dot(att_ref[...], w_ref[...])

    @pl.when(step == pl.num_programs(0) - 1)
    def _():
        middle = middle_ref[...]
        factor = lax.rsqrt(jnp.mean(middle * middle, axis=-1, keepdims=True) + EPSILON)
        rows_ref[...] = (middle * factor * gain_ref[...]).astype(bf16)


def middle_forward(x, attended, w_out, gain, tile=512):
    rows, width = x.shape
    return pl.pallas_call(
        middle_kernel,
        grid=(width // tile,),
        in_specs=[
            pl.BlockSpec((rows, tile), lambda n: (0, n)),
            whole(attended.shape),
            pl.BlockSpec((w_out.shape[0], tile), lambda n: (0, n)),
            whole((1, width)),
        ],
        out_specs=[whole((rows, width))] * 2,
        out_shape=[
            jax.ShapeDtypeStruct((rows, width), f32),
            jax.ShapeDtypeStruct((rows, width), bf16),
        ],
        compiler_params=params(),
        cost_estimate=cost(2 * rows * width * width, 8 * 2**20),
    )(x, attended, w_out, gain.reshape(1, width))


def middle_back_kernel(parts, *refs):
    grad_refs = refs[:parts]
    middle_ref, cot_ref, gain_ref, w_ref = refs[parts : parts + 4]
    mgrad_ref, low_ref, dgain_ref, out_ref = refs[-4:]

    @pl.when(pl.program_id(0) == 0)
    def _():
        upstream = grad_refs[0][...].astype(f32)
        for ref in grad_refs[1:]:
            upstream = upstream + ref[...].astype(f32)
        middle = middle_ref[...]
        factor = lax.rsqrt(jnp.mean(middle * middle, axis=-1, keepdims=True) + EPSILON)
        scaled = upstream * gain_ref[...]
        inner = jnp.mean(scaled * middle, axis=-1, keepdims=True)
        grad = factor * scaled - middle * (factor * factor * factor * inner)
        grad = cot_ref[...].astype(f32) + grad
        mgrad_ref[...] = grad
        low_ref[...] = grad.astype(bf16)
        dgain_ref[...] = jnp.sum(upstream * middle * factor, axis=0, keepdims=True)

    out_ref[...] = dot_nt(low_ref[...], w_ref[...]).astype(bf16)


def middle_back(grads, middle, cotangent, gain, w_out, after=(), tile=512):
    rows, width = middle.shape
    inner = w_out.shape[0]
    return pl.pallas_call(
        functools.partial(middle_back_kernel, len(grads)),
        grid=(inner // tile,),
        in_specs=[whole((rows, width))] * (len(grads) + 2)
        + [whole((1, width)), pl.BlockSpec((tile, width), lambda n: (n, 0))]
        + anywhere(len(after)),
        out_specs=[
            whole((rows, width)),
            whole((rows, width)),
            whole((1, width)),
            pl.BlockSpec((rows, tile), lambda n: (0, n)),
        ],
        out_shape=[
            jax.ShapeDtypeStruct((rows, width), f32),
            jax.ShapeDtypeStruct((rows, width), bf16),
            jax.ShapeDtypeStruct((1, width), f32),
            jax.ShapeDtypeStruct((rows, inner), bf16),
        ],
        compiler_params=params(),
        cost_estimate=cost(2 * rows * width * inner, 16 * 2**20),
    )(*grads, middle, cotangent, gain.reshape(1, width), w_out, *after)


def input_back_kernel(dq_ref, dkv_ref, wq_ref, wk_ref, wv_ref, x_ref, gain_ref, mgrad_ref, *refs):
    out_ref, dgain_ref = refs[-2:]
    step = pl.program_id(0)
    term = dot_nt(dq_ref[...], wq_ref[...])
    term = term + dot_nt(dkv_ref[:, :HD], wk_ref[...]) + dot_nt(dkv_ref[:, HD:], wv_ref[...])

    @pl.when(step == 0)
    def _():
        out_ref[...] = term

    @pl.when(step > 0)
    def _():
        out_ref[...] += term

    @pl.when(step == pl.num_programs(0) - 1)
    def _():
        upstream = out_ref[...]
        x = x_ref[...].astype(f32)
        factor = lax.rsqrt(jnp.mean(x * x, axis=-1, keepdims=True) + EPSILON)
        scaled = upstream * gain_ref[...]
        inner = jnp.mean(scaled * x, axis=-1, keepdims=True)
        out_ref[...] = mgrad_ref[...] + factor * scaled - x * (factor * factor * factor * inner)
        dgain_ref[...] = jnp.sum(upstream * x * factor, axis=0, keepdims=True)


def input_back(dq, dkv, wq, wk, wv, x, gain, mgrad, after=()):
    rows, width = x.shape
    wide = GROUPS * HD
    return pl.pallas_call(
        input_back_kernel,
        grid=(KVH,),
        in_specs=[
            pl.BlockSpec((rows, wide), lambda g: (0, g)),
            pl.BlockSpec((rows, 2 * HD), lambda g: (0, g)),
            pl.BlockSpec((width, wide), lambda g: (0, g)),
            pl.BlockSpec((width, HD), lambda g: (0, g)),
            pl.BlockSpec((width, HD), lambda g: (0, g)),
            whole((rows, width)),
            whole((1, width)),
            whole((rows, width)),
        ]
        + anywhere(len(after)),
        out_specs=[whole((rows, width)), whole((1, width))],
        out_shape=[
            jax.ShapeDtypeStruct((rows, width), f32),
            jax.ShapeDtypeStruct((1, width), f32),
        ],
        compiler_params=params(),
        cost_estimate=cost(2 * rows * width * (H + 2 * KVH) * HD, 14 * 2**20),
    )(dq, dkv, wq, wk, wv, x, gain.reshape(1, width), mgrad, *after)


def gate_column(expert, gates):
    lanes = lax.broadcasted_iota(jnp.int32, gates.shape, 1)
    chosen = (lanes == expert) | (lanes == expert + LOW_LANE)
    return jnp.sum(jnp.where(chosen, gates.astype(f32), 0.0), axis=1, keepdims=True)


def experts_kernel(per, gated, extra, keeps, pos, x_ref, c_ref, *refs):
    weights = refs[:3]
    out_ref, grad_ref, *kept_refs, acc_o, acc_g = refs[3 + extra :]
    step = pl.program_id(0)
    last = pl.num_programs(0) - 1
    width = x_ref.shape[1]
    if keeps:

        @pl.when(step == 0)
        def _():
            kept_refs[0][...] = x_ref[...]
            kept_refs[1][...] = c_ref[...]
            kept_refs[2][...] = jnp.transpose(x_ref[...])
            kept_refs[3][...] = jnp.transpose(c_ref[:, :width])

    hid_ref, dgu_ref = kept_refs[-2:]

    def work(wg_ref, wu_ref, wd_ref):
        chunk = wg_ref.shape[1]
        x = x_ref[...]
        gate = dot(x, wg_ref[...])
        up = dot(x, wu_ref[...])
        slope = dot_nt(c_ref[:, :width], wd_ref[...])
        sigmoid = 1.0 / (1.0 + jnp.exp(-gate))
        act = gate * sigmoid
        hidden = act * up
        if gated:
            held = pl.num_programs(0) // per
            expert = (2 * pos[2] + pos[3]) * held + step // per
            weight = gate_column(expert, c_ref[:, width:])
            hidden = hidden * weight
            slope = slope * weight
        hidden = hidden.astype(bf16)
        dg = (slope * up * (sigmoid * (1.0 + gate * (1.0 - sigmoid)))).astype(bf16)
        du = (slope * act).astype(bf16)
        hid_ref[...] = hidden
        dgu_ref[:, :chunk] = dg
        dgu_ref[:, chunk:] = du
        out_term = dot(hidden, wd_ref[...])
        grad_term = dot_nt(dg, wg_ref[...]) + dot_nt(du, wu_ref[...])

        @pl.when(step == 0)
        def _():
            acc_o[...] = out_term
            acc_g[...] = grad_term

        @pl.when(step > 0)
        def _():
            acc_o[...] += out_term
            acc_g[...] += grad_term

    work(*weights)

    @pl.when(step == last)
    def _():
        out_ref[...] = acc_o[...].astype(out_ref.dtype)
        grad_ref[...] = acc_g[...].astype(grad_ref.dtype)


def experts(pos, x, c, weights, part, parts, kept, gated, kind, after=(), chunk=256):
    rows, width = x.shape
    inner = weights[2].shape[1]
    per = inner // chunk
    steps = weights[0].shape[0] * per
    specs = [
        pl.BlockSpec((None, width, chunk), lambda i, _: (i // per, 0, i % per)),
        pl.BlockSpec((None, width, chunk), lambda i, _: (i // per, 0, i % per)),
        pl.BlockSpec((None, chunk, width), lambda i, _: (i // per, i % per, 0)),
    ]
    collected = [
        jax.ShapeDtypeStruct((parts * rows, steps * chunk), bf16),
        jax.ShapeDtypeStruct((parts * rows, 2 * steps * chunk), bf16),
    ]
    collected_specs = [
        pl.BlockSpec((rows, chunk), lambda i, _: (part, i)),
        pl.BlockSpec((rows, 2 * chunk), lambda i, _: (part, i)),
    ]
    if gated:
        collected = [
            jax.ShapeDtypeStruct((parts * rows, width), bf16),
            jax.ShapeDtypeStruct((parts * rows, c.shape[1]), bf16),
            jax.ShapeDtypeStruct((width, parts * rows), bf16),
            jax.ShapeDtypeStruct((width, parts * rows), bf16),
        ] + collected
        collected_specs = [
            pl.BlockSpec((rows, width), lambda i, _: (part, 0)),
            pl.BlockSpec((rows, c.shape[1]), lambda i, _: (part, 0)),
            pl.BlockSpec((width, rows), lambda i, _: (0, part)),
            pl.BlockSpec((width, rows), lambda i, _: (0, part)),
        ] + collected_specs
    operands = [pos, x, c, *weights]
    aliases = {}
    if kept is not None:
        aliases = {len(operands) + j: 2 + j for j in range(len(collected))}
        operands += list(kept)
    extra = len(after) + (0 if kept is None else len(collected))
    operands += list(after)
    result = pl.pallas_call(
        functools.partial(experts_kernel, per, gated, extra, gated),
        grid_spec=pltpu.PrefetchScalarGridSpec(
            num_scalar_prefetch=1,
            grid=(steps,),
            in_specs=[whole((rows, width)), whole(c.shape)] + specs + anywhere(extra),
            out_specs=[whole((rows, width))] * 2 + collected_specs,
            scratch_shapes=[pltpu.VMEM((rows, width), f32)] * 2,
        ),
        out_shape=[jax.ShapeDtypeStruct((rows, width), kind)] * 2 + collected,
        input_output_aliases=aliases,
        compiler_params=params(),
        cost_estimate=cost(26 * rows * width * steps * chunk, 12 * 2**20),
    )(*operands)
    return result[0], result[1], result[2:]


def others_kernel(sets, per, bands, extra, pos, x_ref, c_ref, *refs):
    each = bands + per
    weights = [refs[t * each : (t + 1) * each] for t in range(sets)]
    *result_refs, hid_ref, dgu_ref = refs[sets * each + extra :]
    out_refs, grad_refs = result_refs[: len(result_refs) // 2], result_refs[len(result_refs) // 2 :]
    step = pl.program_id(0)
    width = x_ref.shape[1]
    band = width // bands
    chunk = weights[0][bands].shape[0]
    rows = out_refs[0].shape[0]

    def places(t, n):
        at = (lax.rem(pos[1] + t, 2) * per + n) * chunk
        cut = lambda first: pl.ds(pl.multiple_of(first, chunk), chunk)
        return cut(at), cut(2 * at), cut(2 * at + chunk)

    def columns(n):
        return slice(n * chunk, (n + 1) * chunk), slice((per + n) * chunk, (per + n + 1) * chunk)

    def hidden_chunk(t, n):
        at_hidden, at_gate, at_up = places(t, n)
        gate_cut, up_cut = columns(n)
        expert = (2 * pos[2] + 1 - pos[3]) * sets + lax.rem(pos[1] + t, 2)
        gate = up = 0.0
        for k in range(bands):
            part = x_ref[:, k * band : (k + 1) * band]
            gate = gate + dot(part, weights[t][k][:, gate_cut])
            up = up + dot(part, weights[t][k][:, up_cut])
        slope = dot_nt(c_ref[:, :width], weights[t][bands + n][...])
        sigmoid = 1.0 / (1.0 + jnp.exp(-gate))
        act = gate * sigmoid
        weight = gate_column(expert, c_ref[:, width:])
        slope = slope * weight
        hid_ref[:, at_hidden] = (act * up * weight).astype(bf16)
        dgu_ref[:, at_gate] = (slope * up * (sigmoid * (1.0 + gate * (1.0 - sigmoid)))).astype(bf16)
        dgu_ref[:, at_up] = (slope * act).astype(bf16)

    def results(k):
        out = grad = 0.0
        for t in range(sets):
            for n in range(per):
                at_hidden, at_gate, at_up = places(t, n)
                gate_cut, up_cut = columns(n)
                down = weights[t][bands + n][:, k * band : (k + 1) * band]
                out = out + dot(hid_ref[:, at_hidden], down)
                grad = grad + dot_nt(dgu_ref[:, at_gate], weights[t][k][:, gate_cut])
                grad = grad + dot_nt(dgu_ref[:, at_up], weights[t][k][:, up_cut])
        for p in range(len(out_refs)):
            out_refs[p][...] = out[p * rows : (p + 1) * rows].astype(bf16)
            grad_refs[p][...] = grad[p * rows : (p + 1) * rows].astype(bf16)

    for t in range(sets):
        for n in range(per):
            pl.when(step == t * per + n)(functools.partial(hidden_chunk, t, n))
    for k in range(bands):
        pl.when(step == sets * per + k)(functools.partial(results, k))


def others(pos, x, c, weights, part, parts, count, kept):
    taken, width = x.shape[0] // parts, x.shape[1]
    sets = len(weights)
    bands, downs = weights[0]
    per = len(downs)
    inner = per * downs[0].shape[0]
    flat = [v for bands_t, downs_t in weights for v in [*bands_t, *downs_t]]
    tile = width // len(bands)
    rows_spec = lambda v: pl.BlockSpec(
        (taken, v.shape[1]), lambda *_: (part, 0), pipeline_mode=pl.Buffered(1)
    )
    resident = lambda v: pl.BlockSpec(v.shape, lambda *_: (0, 0), pipeline_mode=pl.Buffered(1))
    late = lambda i: jnp.maximum(i - sets * per, 0)
    operands = [pos, x, c] + flat
    extra = 0 if kept is None else 2
    aliases = {len(operands) + j: 2 * count + j for j in range(extra)}
    collected = [sets * inner, 2 * sets * inner]
    result = pl.pallas_call(
        functools.partial(others_kernel, sets, per, len(bands), extra),
        grid_spec=pltpu.PrefetchScalarGridSpec(
            num_scalar_prefetch=1,
            grid=(sets * per + len(bands),),
            in_specs=[rows_spec(x), rows_spec(c)] + [resident(v) for v in flat] + anywhere(extra),
            out_specs=[pl.BlockSpec((taken // count, tile), lambda i, _: (0, late(i)))] * (2 * count)
            + [pl.BlockSpec((taken, n), lambda *_: (part, 0)) for n in collected],
        ),
        out_shape=[jax.ShapeDtypeStruct((taken // count, width), bf16)] * (2 * count)
        + [jax.ShapeDtypeStruct((parts * taken, n), bf16) for n in collected],
        input_output_aliases=aliases,
        compiler_params=params(),
        cost_estimate=cost(26 * taken * width * sets * inner, 12 * 2**20),
    )(*operands, *(kept or []))
    return result[:count], result[count : 2 * count], result[2 * count :]


def side_of(outer, s, pos):
    return 2 * lax.rem(s, outer) + lax.rem(pos[1] + 1 - s // outer, 2)


def halves_kernel(shape, outer, pos, *refs):
    sent_ref, kept_ref = refs[-2:]

    def write(out_ref):
        out_ref[...] = jnp.zeros_like(out_ref)
        first = 0
        for i, rows in enumerate(shape):
            total = dot_tn(refs[2 * i][...], refs[2 * i + 1][...]).astype(bf16)
            for e in range(out_ref.shape[0]):
                part = total[e * rows : (e + 1) * rows]
                out_ref[e, first : first + rows, : total.shape[1]] = part
            first += rows

    pl.when(pl.program_id(0) < outer)(lambda: write(sent_ref))
    pl.when(pl.program_id(0) >= outer)(lambda: write(kept_ref))


def halves(pos, pairs, after=()):
    n_ctx, n_exp = lax.axis_size("ctx"), lax.axis_size("exp")
    outer = n_ctx // 2
    shape = [left.shape[1] // (n_ctx * n_exp) for left, _ in pairs]
    wide = max(right.shape[1] for _, right in pairs)
    full = (outer * n_exp, sum(shape), wide)
    if any((left.shape[1] // n_ctx) % 128 for left, _ in pairs):
        out = []
        for side in (1, 0):
            parts = []
            for left, right in pairs:
                split = left.reshape(left.shape[0], outer, 2, -1)
                mine = lax.dynamic_index_in_dim(split, (pos[1] + side) % 2, 2, keepdims=False)
                total = dot_tn(mine.reshape(left.shape[0], -1), right).astype(bf16)
                total = total.reshape(outer * n_exp, -1, right.shape[1])
                parts.append(jnp.pad(total, ((0, 0), (0, 0), (0, wide - right.shape[1]))))
            joined = jnp.concatenate(parts, axis=1)
            out.append(jnp.pad(joined, ((0, 0), (0, -joined.shape[1] % 16), (0, 0))))
        return out
    in_specs, operands = [], []
    for left, right in pairs:
        columns = left.shape[1] // n_ctx
        in_specs.append(
            pl.BlockSpec((left.shape[0], columns), lambda s, pos: (0, side_of(outer, s, pos)))
        )
        in_specs.append(whole(right.shape))
        operands += [left, right]
    block = (n_exp,) + full[1:]
    flops = sum(2 * left.size * right.shape[1] for left, right in pairs)
    return pl.pallas_call(
        functools.partial(halves_kernel, shape, outer),
        grid_spec=pltpu.PrefetchScalarGridSpec(
            num_scalar_prefetch=1,
            grid=(2 * outer,),
            in_specs=in_specs + anywhere(len(after)),
            out_specs=[
                pl.BlockSpec(block, lambda s, pos: (jnp.minimum(s, outer - 1), 0, 0)),
                pl.BlockSpec(block, lambda s, pos: (jnp.maximum(s - outer, 0), 0, 0)),
            ],
        ),
        out_shape=[jax.ShapeDtypeStruct(full, bf16)] * 2,
        compiler_params=params(),
        cost_estimate=cost(2 * flops, 8 * 2**20),
    )(pos, *operands, *after)


def rows_product_kernel(blocks, pos, *refs):
    total = dot_tn(refs[0][...], refs[blocks][...])
    for b in range(1, blocks):
        total = total + dot_tn(refs[b][...], refs[blocks + b][...])
    refs[-1][...] = total.astype(bf16)


def rows_product(pos, lefts, rights, tile=512):
    n_ctx, n_exp = lax.axis_size("ctx"), lax.axis_size("exp")
    depth, height = lefts[0][0].shape
    high, wide = height // n_ctx, rights[0][0].shape[1]
    if high % 128:
        place = lax.axis_index("ctx") * high
        cut = lambda v: lax.slice_in_dim(v[0], v[1] * depth, (v[1] + 1) * depth, axis=0)
        total = sum(
            dot_tn(lax.dynamic_slice_in_dim(cut(a), place, high, 1), cut(b))
            for a, b in zip(lefts, rights)
        )
        return total.astype(bf16).reshape(n_exp, -1, wide)
    blocks = len(lefts)
    left_specs = [
        pl.BlockSpec((depth, high), functools.partial(lambda k, n, pos: (k, 2 * pos[0] + pos[1]), k))
        for _, k in lefts
    ]
    right_specs = [
        pl.BlockSpec((depth, tile), functools.partial(lambda k, n, pos: (k, n), k)) for _, k in rights
    ]
    total = pl.pallas_call(
        functools.partial(rows_product_kernel, blocks),
        grid_spec=pltpu.PrefetchScalarGridSpec(
            num_scalar_prefetch=1,
            grid=(wide // tile,),
            in_specs=left_specs + right_specs,
            out_specs=pl.BlockSpec((high, tile), lambda n, pos: (0, n)),
        ),
        out_shape=jax.ShapeDtypeStruct((high, wide), bf16),
        compiler_params=params(),
        cost_estimate=cost(4 * blocks * depth * high * wide, 4 * 2**20),
    )(pos, *[v for v, _ in lefts], *[v for v, _ in rights])
    return total.reshape(n_exp, -1, wide)


def expert_halves_kernel(blocks, tiles, pos, *refs):
    rows_refs, cot_refs = refs[:blocks], refs[blocks : 2 * blocks]
    dgu_ref, hid_ref, sent_ref, kept_ref = refs[2 * blocks :]
    n = pl.program_id(0)
    high = sent_ref.shape[1]

    def write(left_refs, right_ref):
        left = jnp.concatenate([ref[...] for ref in left_refs], axis=0)
        total = dot(left, right_ref[...]).astype(bf16)
        count = sent_ref.shape[0]
        for i in range(count):
            sent_ref[i] = total[i * high : (i + 1) * high]
            kept_ref[i] = total[(count + i) * high : (count + i + 1) * high]

    pl.when(n < tiles)(lambda: write(rows_refs, dgu_ref))
    pl.when(n >= tiles)(lambda: write(cot_refs, hid_ref))


def expert_steps(width):
    high = width // lax.axis_size("ctx")
    return high // 128 if high % 128 == 0 else 1


def expert_halves(pos, rows_t, cot_t, dgu, hid, tile=512):
    n_ctx = lax.axis_size("ctx")
    width, depth = rows_t.shape
    high = width // n_ctx
    wide = dgu.shape[1] + hid.shape[1]
    steps = expert_steps(width)
    tiles, down = dgu.shape[1] // tile, hid.shape[1] // tile
    left_specs = [
        pl.BlockSpec((high, depth), functools.partial(lambda s, n, pos: (side_of(n_ctx // 2, s, pos), 0), s))
        for s in range(n_ctx)
    ]
    block = (n_ctx // 2 * steps, high // steps, tile)
    return pl.pallas_call(
        functools.partial(expert_halves_kernel, n_ctx, tiles),
        grid_spec=pltpu.PrefetchScalarGridSpec(
            num_scalar_prefetch=1,
            grid=(tiles + down,),
            in_specs=left_specs * 2
            + [
                pl.BlockSpec((depth, tile), lambda n, pos: (0, jnp.minimum(n, tiles - 1))),
                pl.BlockSpec((depth, tile), lambda n, pos: (0, jnp.maximum(n - tiles, 0))),
            ],
            out_specs=[pl.BlockSpec(block, lambda n, pos: (0, 0, n))] * 2,
        ),
        out_shape=[jax.ShapeDtypeStruct(block[:2] + (wide,), bf16)] * 2,
        compiler_params=params(),
        cost_estimate=cost(4 * depth * width * wide, 16 * 2**20),
    )(pos, *[rows_t] * n_ctx, *[cot_t] * n_ctx, dgu, hid)


def sums_kernel(shape, only, extra, pos, *refs):
    ins, outs = refs[: sum(shape)], refs[sum(shape) + extra :]
    at = 0
    for count, out in zip(shape, outs):
        total = ins[at][...].astype(f32)
        for k in range(at + 1, at + count):
            term = ins[k][...].astype(f32)
            if only[k] is not None:
                term = jnp.where(pl.program_id(0) == only[k], term, 0.0)
            total = total + term
        out[...] = total.astype(out.dtype)
        at += count


def sums(pos, steps, outputs, after=()):
    operands, in_specs, out_specs, out_shape, only = [], [], [], [], []
    for kind, block, terms in outputs:
        for array, index, *step in terms:
            operands.append(array)
            only.append(step[0] if step else None)
            in_specs.append(pl.BlockSpec(block, functools.partial(place_of, index)))
        out_specs.append(pl.BlockSpec(block, lambda i, pos: (i, 0, 0)))
        out_shape.append(jax.ShapeDtypeStruct((steps * block[0],) + tuple(block[1:]), kind))
    return pl.pallas_call(
        functools.partial(sums_kernel, [len(terms) for _, _, terms in outputs], only, len(after)),
        grid_spec=pltpu.PrefetchScalarGridSpec(
            num_scalar_prefetch=1,
            grid=(steps,),
            in_specs=in_specs + anywhere(len(after)),
            out_specs=out_specs,
        ),
        out_shape=out_shape,
        compiler_params=params(),
        cost_estimate=cost(0, 8 * 2**20),
    )(pos, *operands, *after)


def place_of(index, i, pos):
    at = index(i, pos)
    return at if isinstance(at, tuple) else (at, 0, 0)


def straight(i, pos):
    return i


def row_sum(terms, kind=bf16):
    total = terms[0].astype(f32)
    for term in terms[1:]:
        total = total + term.astype(f32)
    return total.astype(kind)


def expert_out_kernel(gates, each, *refs):
    in_refs, (gate_ref, up_ref, down_ref) = refs[:4], refs[4:]
    n = pl.program_id(0)

    def write(ref):
        @pl.when((n < gates) & (lax.rem(n, 2) == 0))
        def _():
            gate_ref[0] = ref[...].astype(f32)

        @pl.when((n < gates) & (lax.rem(n, 2) == 1))
        def _():
            up_ref[0] = ref[...].astype(f32)

        @pl.when(n >= gates)
        def _():
            down_ref[0] = jnp.transpose(ref[...].astype(f32))

    for q in range(4):
        pl.when(n // each == q)(functools.partial(write, in_refs[q]))


def expert_out(quarters, inner, chunk=256):
    rows, wide = quarters[0].shape
    each = wide // chunk
    held = 4 * wide // (3 * inner)
    per = inner // chunk
    gates = 2 * held * per
    tile = lambda n: jnp.minimum(n, gates - 1) // 2
    spec = pl.BlockSpec((1, rows, chunk), lambda n: (tile(n) // per, 0, lax.rem(tile(n), per)))
    at = lambda n: jnp.maximum(n - gates, 0)
    return pl.pallas_call(
        functools.partial(expert_out_kernel, gates, each),
        grid=(4 * each,),
        in_specs=[
            pl.BlockSpec(
                (rows, chunk),
                functools.partial(lambda q, n: (0, jnp.clip(n - q * each, 0, each - 1)), q),
            )
            for q in range(4)
        ],
        out_specs=[
            spec,
            spec,
            pl.BlockSpec((1, chunk, rows), lambda n: (at(n) // per, lax.rem(at(n), per), 0)),
        ],
        out_shape=[jax.ShapeDtypeStruct((held, rows, inner), f32)] * 2
        + [jax.ShapeDtypeStruct((held, inner, rows), f32)],
        compiler_params=params(),
        cost_estimate=cost(0, 8 * 2**20),
    )(*quarters)


def last_sum(refs):
    total = refs[0][...].astype(f32)
    for ref in refs[1:]:
        total = total + ref[...].astype(f32)
    return total


def dense_out_kernel(count, *refs):
    total = last_sum(refs[:count])
    out_ref, query_ref, key_ref, value_ref = refs[count:]
    wide = out_ref.shape[1]
    out_ref[...] = total[:, :wide]
    query_ref[...] = total[:, wide : 2 * wide]
    for g in range(KVH):
        first = 2 * wide + 2 * g * HD
        key_ref[:, g * HD : (g + 1) * HD] = total[:, first : first + HD]
        value_ref[:, g * HD : (g + 1) * HD] = total[:, first + HD : first + 2 * HD]


def dense_out(terms, wide):
    rows = terms[0].shape[0]
    shapes = [wide, wide, KVH * HD, KVH * HD]
    return pl.pallas_call(
        functools.partial(dense_out_kernel, len(terms)),
        out_shape=[jax.ShapeDtypeStruct((rows, n), f32) for n in shapes],
        compiler_params=params(),
        cost_estimate=cost(0, 2**20),
    )(*terms)


def shared_out_kernel(count, chunk, *refs):
    total = last_sum(refs[:count])
    gate_ref, up_ref, down_ref = refs[count:]
    rows = gate_ref.shape[0]
    for n in range(gate_ref.shape[1] // chunk):
        cut = slice(n * chunk, (n + 1) * chunk)
        gate_ref[:, cut] = total[:rows, 2 * n * chunk : (2 * n + 1) * chunk]
        up_ref[:, cut] = total[:rows, (2 * n + 1) * chunk : (2 * n + 2) * chunk]
    down_ref[...] = total[rows : rows + down_ref.shape[0], : down_ref.shape[1]]


def shared_grads(terms, gate, down, chunk=256):
    return pl.pallas_call(
        functools.partial(shared_out_kernel, len(terms), chunk),
        out_shape=[jax.ShapeDtypeStruct(v, f32) for v in (gate, gate, down)],
        compiler_params=params(),
        cost_estimate=cost(0, 2**20),
    )(*terms)


def hold(values, after):
    count = len(values)
    return pl.pallas_call(
        lambda *_: None,
        in_specs=[pl.BlockSpec(memory_space=pl.ANY)] * (count + len(after)),
        out_specs=[pl.BlockSpec(memory_space=pl.ANY)] * count,
        out_shape=[jax.ShapeDtypeStruct(v.shape, v.dtype) for v in values],
        input_output_aliases={i: i for i in range(count)},
        compiler_params=params(),
        cost_estimate=cost(0, 0),
    )(*values, *after)


def swap_inner(value, axis):
    size = lax.axis_size(axis)
    return lax.ppermute(value, axis, [(i, i ^ 1) for i in range(size)])


def shift_outer(value, axis, by):
    outer = lax.axis_size(axis) // 2
    perm = [(o * 2 + i, ((o + by) % outer) * 2 + i) for o in range(outer) for i in range(2)]
    return lax.ppermute(value, axis, perm)


def ring_step(value, by):
    n_ctx, n_exp = lax.axis_size("ctx"), lax.axis_size("exp")
    outer = n_exp // 2
    perm = []
    for c in range(n_ctx):
        way = by if c % 2 == 0 else -by
        for o in range(outer):
            for i in range(2):
                perm.append((c * n_exp + o * 2 + i, c * n_exp + ((o + way) % outer) * 2 + i))
    return lax.ppermute(value, BOTH, perm)


def by_blocks(value, together):
    return value.reshape(-1, together * value.shape[1], value.shape[2])


def spread_outer(value):
    moved, out = value, []
    for _ in range(1, lax.axis_size("ctx") // 2):
        moved = shift_outer(moved, "ctx", 1)
        out.append(moved)
    return out, swap_inner(value, "ctx")


def spread_inner(moved):
    return [swap_inner(v, "ctx") for v in moved]


def outer_blocks(value):
    moved, out = value, []
    for _ in range(1, lax.axis_size("ctx") // 2):
        moved = shift_outer(moved, "ctx", 1)
        out.append(moved)
    return out


def inner_blocks(value, moved):
    return swap_inner(jnp.concatenate([value] + moved, axis=0), "ctx")


def all_blocks(value, moved, across):
    out = []
    for k, v in enumerate([value] + moved):
        out += [(v, 0), (across, k)]
    return out


def spread_all(value, moved, across, moved_across):
    blocks = [value, across]
    for a, b in zip(moved, moved_across):
        blocks += [a, b]
    return blocks


class Shared:
    def __init__(self, pos, kept, got):
        self.pos = pos
        self.outer, self.levels = lax.axis_size("ctx") // 2, lax.axis_size("exp") // 2
        self.rows, self.wide = kept.shape[1:]
        self.pair = lambda v: v.reshape(-1, 2 * self.rows, self.wide)
        self.terms = [self.pair(v) for v in (kept, got)]
        self.together = 2 if self.levels % 2 == 0 else 1
        self.steps = self.levels // self.together

    def _sum(self, d, rows, inner, moved=()):
        at = lambda i, pos: lax.rem(pos[0] + d, self.outer) * self.steps + i
        terms = [(v, lambda i, pos: (at(i, pos), inner(pos), 0)) for v in self.terms]
        for parts in moved:
            for k, v in enumerate(parts):
                terms.append((self.pair(v), lambda i, pos: (0, inner(pos), 0), k))
        return terms, (self.together, rows, self.wide)

    def first(self):
        out = []
        for d in range(1, self.outer):
            terms, block = self._sum(d, 2 * self.rows, lambda pos: 0)
            outputs = []
            for k in range(self.steps):
                part = [(v, functools.partial(lambda f, k, i, pos: f(k, pos), f, k)) for v, f in terms]
                outputs.append((bf16, block, part))
            out.append(sums(self.pos, 1, outputs))
        return out

    def second(self, moved):
        terms, block = self._sum(0, self.rows, lambda pos: 1 - pos[3], moved)
        return swap_inner(sums(self.pos, self.steps, [(bf16, block, terms)])[0], "exp")

    def total(self, moved, crossed):
        terms, block = self._sum(0, self.rows, lambda pos: pos[3], moved)
        return sums(self.pos, self.steps, [(bf16, block, terms + [(crossed, straight)])])[0]


def z_take(total, d):
    levels = total.shape[0]
    return lax.dynamic_index_in_dim(total, (lax.axis_index("exp") // 2 + d) % levels, 0, False)


def z_send(total, d):
    return shift_outer(z_take(total, d), "exp", d)


def over_x(total):
    pairs = total.reshape((-1, 2) + total.shape[1:])
    return swap_inner(lax.dynamic_index_in_dim(pairs, 1 - lax.axis_index("exp") % 2, 1, False), "exp")


def mine_x(total):
    pairs = total.reshape((-1, 2) + total.shape[1:])
    return lax.dynamic_index_in_dim(pairs, lax.axis_index("exp") % 2, 1, False)


def over_z(mine, arrived):
    mine = mine.astype(f32) + arrived.astype(f32)
    levels, level = mine.shape[0], lax.axis_index("exp") // 2
    take = lambda d: lax.dynamic_index_in_dim(mine, (level + d) % levels, 0, False)
    return [take(0)] + [shift_outer(take(d).astype(bf16), "exp", d) for d in range(1, levels)]


def expert_quarter(kept, got, q, row):
    steps = kept.shape[0] // (lax.axis_size("ctx") // 2)
    block = (steps, kept.shape[1], kept.shape[2] // 4)
    return block, [(v, lambda i, pos: (row(i, pos), 0, q)) for v in (kept, got)]


def expert_pieces(pos, kept, got, quarters):
    outputs = []
    for q in quarters:
        block, terms = expert_quarter(kept, got, q, straight)
        outputs.append((bf16, block, terms))
    return sums(pos, lax.axis_size("ctx") // 2, outputs)


def expert_row(d):
    outer = lax.axis_size("ctx") // 2
    return lambda i, pos: lax.rem(pos[0] + d, outer)


def expert_send(pos, kept, got, pieces, half):
    sent = []
    for d in range(1, lax.axis_size("ctx") // 2):
        row = expert_row(d)
        block, terms = expert_quarter(kept, got, 0, row)
        terms = [(v, lambda i, pos: (row(i, pos), 0, 2 * half + i)) for v, _ in terms]
        terms += [(pieces[2 * half + k], lambda i, pos: row(0, pos), k) for k in range(2)]
        sent += sums(pos, 2, [(bf16, block, terms)])
    return sent


def expert_move(sent):
    return [shift_outer(v, "ctx", d + 1) for d, v in enumerate(sent)]


def expert_total(pos, kept, got, pieces, arrived):
    row = expert_row(0)
    outputs = []
    for q in range(4):
        block, terms = expert_quarter(kept, got, q, row)
        at = functools.partial(lambda k, i, pos: k, q % 2)
        terms = terms + [(pieces[q], row)] + [(v, at) for v in arrived[q // 2]]
        outputs.append((bf16, block, terms))
    return [v.reshape(-1, v.shape[2]) for v in sums(pos, 1, outputs)]


def shards(
    layer_input,
    attn_gain,
    w_query,
    w_key,
    w_value,
    w_out,
    ffn_gain,
    shared_gate,
    shared_up,
    shared_down,
    expert_gate,
    expert_up,
    expert_down,
    routes,
    gate_logits,
    span_order,
    cotangent,
):
    x = layer_input[0]
    cot = cotangent[0]
    tokens, width = x.shape
    span_rows = tokens // 2
    n_ctx, n_exp = lax.axis_size("ctx"), lax.axis_size("exp")
    ctx_id, exp_id = lax.axis_index("ctx"), lax.axis_index("exp")
    local_experts, _, inner = expert_gate.shape
    expert_count = local_experts * n_exp

    levels = n_exp // 2
    pos = jnp.stack([ctx_id // 2, ctx_id % 2, exp_id // 2, exp_id % 2]).astype(jnp.int32)

    always = pos[0] < n_ctx
    ring = n_ctx // 2

    def region(work):
        made = jax.eval_shape(work)
        return lax.cond(always, work, lambda: jax.tree.map(lambda v: jnp.zeros(v.shape, v.dtype), made))

    gate_vals = jax.nn.softmax(gate_logits[0], axis=-1)
    named = routes[0][:, None, :] == jnp.arange(expert_count, dtype=jnp.int32)[None, :, None]
    row_gates = jnp.sum(jnp.where(named, gate_vals[:, None, :], 0.0), axis=-1)
    high = row_gates.astype(bf16)
    low = (row_gates - high.astype(f32)).astype(bf16)
    fill = lambda width: ((0, 0), (0, width - expert_count))
    cot_ring = [
        jnp.concatenate(
            [cot, jnp.pad(high, fill(LOW_LANE)), jnp.pad(low, fill(GATE_LANES - LOW_LANE))], axis=1
        )
    ]

    chunk, bands = 256, 3
    mine = lambda v: lax.dynamic_index_in_dim(v, pos[1], 0, keepdims=False)
    over_core = lambda v: swap_inner(v, "ctx")

    def fetch(k):
        return swap_inner(asked[k], "exp")

    def arranged(parts):
        return parts[inner // chunk :], parts[: inner // chunk]

    def ask():
        down = mine(expert_down)
        out = [down[n * chunk : (n + 1) * chunk] for n in range(inner // chunk)]
        gate, up = mine(expert_gate), mine(expert_up)
        band = width // bands
        for k in range(bands):
            cut = slice(k * band, (k + 1) * band)
            out.append(jnp.concatenate([gate[cut], up[cut]], axis=1))
        return out

    def gather_keys():
        normed, kv = keyvalue(x, attn_gain, w_key, w_value)
        moved, across = spread_outer(kv)
        queries = dot(normed, w_query).astype(bf16)
        asked = ask()
        keys = kv, moved, across, spread_inner(moved)
        return normed, keys, queries, ring_step(cot_ring[0], 1), asked, swap_inner(asked[0], "exp")

    normed, keys, queries, cot_next, asked, got = region(gather_keys)
    kv_blocks = spread_all(*keys)
    cot_ring.append(cot_next)
    fetched, crossed = [got], []

    def attention():
        attended, lse = attend(pos, span_order, queries, kv_blocks)
        middle, rows = middle_forward(x, attended, w_out, ffn_gain)
        moved = outer_blocks(normed), ring_step(cot_ring[1], 1), fetch(1), over_core(fetched[0])
        return attended, lse, middle, rows, *moved

    attended, lse, middle, rows_low, normed_moved, cot_next, got, crossing = region(attention)
    cot_ring.append(cot_next)
    fetched.append(got)
    crossed.append(crossing)

    def own_part(k, rows, kept):
        weights = (expert_gate, expert_up, expert_down)
        return experts(pos, rows, cot_ring[k], weights, k, levels, kept, True, bf16)

    def first():
        weights = (shared_gate[None], shared_up[None], shared_down[None])
        shared = experts(pos, rows_low, cot, weights, 0, 1, None, False, f32)
        more = inner_blocks(normed, normed_moved), fetch(2), over_core(fetched[1]), outer_blocks(attended)
        return ring_step(rows_low, 1), shared, own_part(0, rows_low, None), *more

    rows_k, shared, (out_k, grad_k, kept), across, got, crossing, attended_moved = region(first)
    fetched.append(got)
    crossed.append(crossing)
    normed_blocks = all_blocks(normed, normed_moved, across)
    shared_out, shared_grad, (shared_hidden, shared_dgu) = shared
    out_own, grad_own = [out_k], [grad_k]
    shared_pairs = [(rows_low, shared_dgu), (shared_hidden, cot)]

    def second():
        result = own_part(1, rows_k, kept)
        more = fetch(3), over_core(fetched[2]), inner_blocks(attended, attended_moved)
        return ring_step(rows_k, 1), result, halves(pos, shared_pairs), *more

    rows_next, (out_k, grad_k, kept), (shared_sent, shared_kept), got, crossing, across = region(second)
    attended_blocks = all_blocks(attended, attended_moved, across)
    fetched.append(got)
    crossed.append(crossing)
    rows_k = rows_next
    out_own.append(out_k)
    grad_own.append(grad_k)

    def third():
        result = own_part(2, rows_k, kept)
        more = over_core(shared_sent), fetch(4), over_core(fetched[3])
        return ring_step(rows_k, 1), result, *more

    rows_next, (out_k, grad_k, kept), shared_got, got, crossing = region(third)
    fetched.append(got)
    crossed.append(crossing)
    rows_k = rows_next
    out_own.append(out_k)
    grad_own.append(grad_k)

    def over_y(parts, k):
        return [shift_outer(v[k], "ctx", d + 1) for d, v in enumerate(parts)]

    def fourth():
        moved = ring_step(cot_ring[2], 1)
        weights = [arranged(fetched), arranged(crossed + [over_core(fetched[4])])]
        half = levels // 2
        sent = Shared(pos, shared_kept, shared_got).first()
        arrived = [over_y(sent, k) for k in range(len(sent[0]) // 2)]
        out_a, grad_a, new = others(pos, kept[0], kept[1], weights, 0, 2, half, None)
        out_k, grad_k, more = experts(
            pos, rows_k, moved, (expert_gate, expert_up, expert_down), 3, levels, kept, True, bf16
        )
        out_b, grad_b, new = others(pos, more[0], more[1], weights, 1, 2, half, new)
        rest = [v[len(v) // 2 :] for v in sent]
        return out_k, grad_k, more, [*out_a, *out_b], [*grad_a, *grad_b], new, arrived, rest

    out_k, grad_k, kept, out_other, grad_other, kept_other, shared_first, shared_rest = region(fourth)
    out_own.append(out_k)
    grad_own.append(grad_k)
    rows_all, cot_all, rows_t, cot_t, hid_own, dgu_own = kept
    hid_other, dgu_other = kept_other

    def back_one():
        moved = ring_step(row_sum([grad_own[3], grad_other[3]]), -1)
        arrived = [over_y(shared_rest, k) for k in range(len(shared_rest[0]))]
        return moved, expert_halves(pos, rows_t, cot_t, dgu_other, hid_other), arrived

    moved, (sent, kept_other), got = region(back_one)
    shared_moved = [list(v) for v in zip(*(list(shared_first) + list(got)))]

    def back_two():
        total = row_sum([grad_own[2], grad_other[2], moved])
        got = swap_inner(sent, "ctx")
        crossed = Shared(pos, shared_kept, shared_got).second(shared_moved)
        made = expert_halves(pos, rows_t, cot_t, dgu_own, hid_own)
        return ring_step(total, -1), got, made, expert_pieces(pos, kept_other, got, [0])[0], crossed

    moved_two, got_other, (sent_own, kept_own), piece, shared_crossed = region(back_two)

    def back_three():
        total = row_sum([grad_own[1], grad_other[1], moved_two])
        made = expert_pieces(pos, kept_other, got_other, [1, 2, 3])
        shared_sum = Shared(pos, shared_kept, shared_got).total(shared_moved, shared_crossed)
        out_total = row_sum([out_own[3], out_other[3]])
        moved = ring_step(total, -1), swap_inner(sent_own, "ctx"), swap_inner(piece, "exp")
        return *moved, made, shared_sum, out_total

    moved, got_own, piece, made, shared_sum, out_total = region(back_three)
    pieces = [piece, *made]

    def attention_back():
        mgrad, mgrad_low, ffn_gain_grad, att_grad = middle_back(
            [shared_grad, grad_own[0], grad_other[0], moved], middle, cot, ffn_gain, w_out
        )
        back = attend_back(pos, span_order, queries, att_grad, lse, kv_blocks)
        got = ring_step(out_total, -1), swap_inner(pieces[1], "exp")
        return mgrad, mgrad_low, outer_blocks(mgrad_low), ffn_gain_grad, back, *got

    mgrad, mgrad_low, mgrad_moved, ffn_gain_grad, (dq, same, across), out_moved, piece = region(
        attention_back
    )
    pieces[1] = piece

    def dense_one():
        got = swap_inner(across, "ctx")
        made = []
        for k in reversed(range(ring)):
            part = slice(k * tokens, (k + 1) * tokens)
            made = row_sum([same[part], got[part]] + made)
            if k:
                made = [shift_outer(made, "ctx", -1)]
        total = row_sum([out_own[2], out_other[2], out_moved])
        mgrad_blocks = all_blocks(mgrad_low, mgrad_moved, inner_blocks(mgrad_low, mgrad_moved))
        total_out = rows_product(pos, attended_blocks, mgrad_blocks)
        sent = expert_send(pos, kept_own, got_own, pieces, 0)
        moved = ring_step(total, -1), swap_inner(pieces[2], "exp")
        return made, outer_blocks(dq), total_out, sent, *moved

    dkv, dq_moved, total_out, sent, out_moved_two, piece = region(dense_one)
    pieces[2] = piece

    def dense_two():
        total = row_sum([out_own[1], out_other[1], out_moved_two])
        dkv_moved = outer_blocks(dkv)
        dkv_blocks = all_blocks(dkv, dkv_moved, inner_blocks(dkv, dkv_moved))
        dq_blocks = all_blocks(dq, dq_moved, inner_blocks(dq, dq_moved))
        total_query = rows_product(pos, normed_blocks, dq_blocks)
        total_kv = rows_product(pos, normed_blocks, dkv_blocks)
        back = input_back(dq, dkv, w_query, w_key, w_value, x, attn_gain, mgrad)
        moved = ring_step(total, -1), swap_inner(pieces[3], "exp"), expert_move(sent)
        return total_query, total_kv, back, *moved

    total_query, total_kv, (input_grad, attn_gain_grad), out_moved_three, piece, got = region(dense_two)
    pieces[3] = piece
    arrived = [got]

    def dense_three():
        devices = n_ctx * n_exp
        total = jnp.concatenate([total_out, total_query, total_kv], axis=2)
        got = expert_move(expert_send(pos, kept_own, got_own, pieces, 1))
        layer_out = row_sum([middle, shared_out, out_own[0], out_other[0], out_moved_three])
        shared_z = [z_send(shared_sum, d) for d in range(1, levels)]
        gains = jnp.stack(
            [attn_gain_grad.reshape(devices, -1), ffn_gain_grad.reshape(devices, -1)], axis=1
        )
        gains = lax.all_to_all(gains, BOTH, split_axis=0, concat_axis=0, tiled=True)
        return mine_x(total), over_x(total), got, layer_out, shared_z, gains

    total, total_x, got, layer_out, shared_z, gains = region(dense_three)
    arrived.append(got)

    def dense_four():
        grads = expert_out(expert_total(pos, kept_own, got_own, pieces, arrived), inner)
        shape = lambda v: (v.shape[0] // (n_ctx * n_exp), v.shape[1])
        shared = shared_grads(
            [z_take(shared_sum, 0)] + shared_z, shape(shared_gate), shape(shared_down)
        )
        dense = dense_out(over_z(total, total_x), x.shape[1])
        return jnp.sum(gains, axis=0), shared, dense, grads

    gains, (sum_gate, sum_up, sum_down), dense, expert_grads = region(dense_four)
    sum_out, sum_query, sum_key, sum_value = dense
    return (
        layer_out[None],
        input_grad[None],
        gains[0],
        sum_query,
        sum_key,
        sum_value,
        sum_out,
        gains[1],
        sum_gate,
        sum_up,
        sum_down,
        *expert_grads,
    )


def solution(mesh):
    return jax.shard_map(
        shards,
        mesh=mesh,
        in_specs=(
            P("exp", "ctx", None),
            P(),
            P(),
            P(),
            P(),
            P(),
            P(),
            P(),
            P(),
            P(),
            P("exp", None, None),
            P("exp", None, None),
            P("exp", None, None),
            P("exp", "ctx", None),
            P("exp", "ctx", None),
            P(),
            P("exp", "ctx", None),
        ),
        out_specs=(
            P("exp", "ctx", None),
            P("exp", "ctx", None),
            P(("ctx", "exp")),
            P(("ctx", "exp"), None),
            P(("ctx", "exp"), None),
            P(("ctx", "exp"), None),
            P(("ctx", "exp"), None),
            P(("ctx", "exp")),
            P(("ctx", "exp"), None),
            P(("ctx", "exp"), None),
            P(("ctx", "exp"), None),
            P("exp", "ctx", None),
            P("exp", "ctx", None),
            P("exp", None, "ctx"),
        ),
        check_vma=False,
    )
```

```python
import functools

import jax
import jax.numpy as jnp
from jax import lax
from jax.experimental import pallas as pl
from jax.experimental.pallas import tpu as pltpu
from jax.sharding import PartitionSpec as P

H = 12
HD = 128
KVH = 4
GROUPS = H // KVH
EPSILON = 1e-06
GATE_LANES = 128
LOW_LANE = 64
NEGATIVE = -1e30
SCALE = HD ** (-0.5)
BOTH = ("ctx", "exp")
VMEM_LIMIT = 60 * 2**20
bf16 = jnp.bfloat16
f32 = jnp.float32


def dot(left_op, right_op):
    return jnp.dot(left_op, right_op, preferred_element_type=f32)


def dot_nt(left_op, right_op):
    return lax.dot_general(left_op, right_op, (((1,), (1,)), ((), ())), preferred_element_type=f32)


def dot_tn(left_op, right_op):
    return lax.dot_general(left_op, right_op, (((0,), (0,)), ((), ())), preferred_element_type=f32)


def whole(shape):
    return pl.BlockSpec(shape, lambda *_: (0,) * len(shape))


def params():
    return pltpu.CompilerParams(vmem_limit_bytes=VMEM_LIMIT)


def anywhere(count):
    return [pl.BlockSpec(memory_space=pl.ANY)] * count


def cost(flops, nbytes):
    return pl.CostEstimate(flops=flops // 4, bytes_accessed=nbytes // 4, transcendentals=0)


def keyvalue_kernel(x_ref, gain_ref, wk_ref, wv_ref, normed_ref, kv_ref):
    @pl.when(pl.program_id(0) == 0)
    def _():
        x = x_ref[...].astype(f32)
        factor = lax.rsqrt(jnp.mean(x * x, axis=-1, keepdims=True) + EPSILON)
        normed_ref[...] = (x * factor * gain_ref[...]).astype(bf16)

    both = jnp.concatenate([wk_ref[...], wv_ref[...]], axis=1)
    kv_ref[...] = dot(normed_ref[...], both).astype(bf16)


def keyvalue(x, gain, wk, wv):
    rows, width = x.shape
    return pl.pallas_call(
        keyvalue_kernel,
        grid=(KVH,),
        in_specs=[
            whole((rows, width)),
            whole((1, width)),
            pl.BlockSpec((width, HD), lambda g: (0, g)),
            pl.BlockSpec((width, HD), lambda g: (0, g)),
        ],
        out_specs=[whole((rows, width)), pl.BlockSpec((rows, 2 * HD), lambda g: (0, g))],
        out_shape=[
            jax.ShapeDtypeStruct((rows, width), bf16),
            jax.ShapeDtypeStruct((rows, 2 * KVH * HD), bf16),
        ],
        compiler_params=params(),
        cost_estimate=cost(4 * rows * width * KVH * HD, 5 * 2**20),
    )(x, gain.reshape(1, width), wk, wv)


def stack_heads(ref):
    return jnp.concatenate([ref[:, r * HD : (r + 1) * HD] for r in range(GROUPS)], axis=0)


def places(pos, spans, block, shape, dim, rows):
    outer, side = (0, 0) if block is None else (block // 2, block % 2)
    ring = spans.shape[0] // 4
    owner = 2 * lax.rem(pos[0] + ring - outer, ring) + lax.rem(pos[1] + side, 2)
    row = lax.broadcasted_iota(jnp.int32, shape, dim) % rows
    half = rows // 2
    first, second = spans[2 * owner] * half, spans[2 * owner + 1] * half
    return jnp.where(row < half, first + row, second + row - half)


def attend_kernel(blocks, extra, pos, spans, q_ref, *refs):
    kv_refs = refs[:blocks]
    out_ref, lse_ref, score_ref = refs[blocks + extra :]
    rows = q_ref.shape[0]
    queries = stack_heads(q_ref)
    wanted = places(pos, spans, None, (1, GROUPS * rows), 1, rows)
    peak = jnp.full((1, GROUPS * rows), NEGATIVE, f32)
    for b in range(blocks):
        scores = dot_nt(kv_refs[b][:, :HD], queries) * SCALE
        visible = places(pos, spans, b, (rows, 1), 0, rows) <= wanted
        scores = jnp.where(visible, scores, NEGATIVE)
        score_ref[b * rows : (b + 1) * rows, :] = scores
        peak = jnp.maximum(peak, jnp.max(scores, axis=0, keepdims=True))
    total = jnp.zeros_like(peak)
    mixed = jnp.zeros((HD, GROUPS * rows), f32)
    for b in range(blocks):
        weights = jnp.exp(score_ref[b * rows : (b + 1) * rows, :] - peak)
        total = total + jnp.sum(weights, axis=0, keepdims=True)
        mixed = mixed + dot_tn(kv_refs[b][:, HD:], weights.astype(bf16))
    lse_ref[0] = peak + jnp.log(total)
    mixed = jnp.transpose(mixed / total)
    for r in range(GROUPS):
        out_ref[:, r * HD : (r + 1) * HD] = mixed[r * rows : (r + 1) * rows].astype(bf16)


def attend(pos, spans, queries, kv_blocks, after=()):
    rows = queries.shape[0]
    blocks = len(kv_blocks)
    wide = GROUPS * HD
    return pl.pallas_call(
        functools.partial(attend_kernel, blocks, len(after)),
        grid_spec=pltpu.PrefetchScalarGridSpec(
            num_scalar_prefetch=2,
            grid=(KVH,),
            in_specs=[pl.BlockSpec((rows, wide), lambda g, *_: (0, g))]
            + [pl.BlockSpec((rows, 2 * HD), lambda g, *_: (0, g))] * blocks
            + anywhere(len(after)),
            out_specs=[
                pl.BlockSpec((rows, wide), lambda g, *_: (0, g)),
                pl.BlockSpec((1, 1, GROUPS * rows), lambda g, *_: (g, 0, 0)),
            ],
            scratch_shapes=[pltpu.VMEM((blocks * rows, GROUPS * rows), f32)],
        ),
        out_shape=[
            jax.ShapeDtypeStruct((rows, H * HD), bf16),
            jax.ShapeDtypeStruct((KVH, 1, GROUPS * rows), f32),
        ],
        compiler_params=params(),
        cost_estimate=cost(8 * rows * rows * blocks * H * HD, 4 * 2**20),
    )(pos, spans, queries, *kv_blocks, *after)


def attend_back_kernel(blocks, extra, pos, spans, q_ref, grad_ref, lse_ref, *refs):
    kv_refs = refs[:blocks]
    dq_ref, same_ref, other_ref = refs[blocks + extra : -2]
    prob_ref, slope_ref = refs[-2:]
    rows = q_ref.shape[0]
    queries = stack_heads(q_ref)
    grads = stack_heads(grad_ref)
    wanted = places(pos, spans, None, (1, GROUPS * rows), 1, rows)
    lse = lse_ref[0]
    delta = jnp.zeros((1, GROUPS * rows), f32)
    for b in range(blocks):
        part = slice(b * rows, (b + 1) * rows)
        scores = dot_nt(kv_refs[b][:, :HD], queries) * SCALE - lse
        visible = places(pos, spans, b, (rows, 1), 0, rows) <= wanted
        prob = jnp.exp(jnp.where(visible, scores, NEGATIVE))
        slope = dot_nt(kv_refs[b][:, HD:], grads)
        delta = delta + jnp.sum(prob * slope, axis=0, keepdims=True)
        prob_ref[part, :] = prob
        slope_ref[part, :] = slope
        dkv_ref = other_ref if b % 2 else same_ref
        dkv_ref[rows * (b // 2) : rows * (b // 2 + 1), HD:] = dot(prob.astype(bf16), grads).astype(bf16)
    query_grad = jnp.zeros((HD, GROUPS * rows), f32)
    for b in range(blocks):
        part = slice(b * rows, (b + 1) * rows)
        dscore = (prob_ref[part, :] * (slope_ref[part, :] - delta) * SCALE).astype(bf16)
        dkv_ref = other_ref if b % 2 else same_ref
        dkv_ref[rows * (b // 2) : rows * (b // 2 + 1), :HD] = dot(dscore, queries).astype(bf16)
        query_grad = query_grad + dot_tn(kv_refs[b][:, :HD], dscore)
    query_grad = jnp.transpose(query_grad)
    for r in range(GROUPS):
        dq_ref[:, r * HD : (r + 1) * HD] = query_grad[r * rows : (r + 1) * rows].astype(bf16)


def attend_back(pos, spans, queries, grads, lse, kv_blocks, after=()):
    rows = queries.shape[0]
    blocks = len(kv_blocks)
    wide = GROUPS * HD
    by_group = pl.BlockSpec((rows, wide), lambda g, *_: (0, g))
    kv_spec = pl.BlockSpec((rows, 2 * HD), lambda g, *_: (0, g))
    return pl.pallas_call(
        functools.partial(attend_back_kernel, blocks, len(after)),
        grid_spec=pltpu.PrefetchScalarGridSpec(
            num_scalar_prefetch=2,
            grid=(KVH,),
            in_specs=[
                by_group,
                by_group,
                pl.BlockSpec((1, 1, GROUPS * rows), lambda g, *_: (g, 0, 0)),
            ]
            + [kv_spec] * blocks
            + anywhere(len(after)),
            out_specs=[by_group]
            + [pl.BlockSpec((blocks // 2 * rows, 2 * HD), lambda g, *_: (0, g))] * 2,
            scratch_shapes=[pltpu.VMEM((blocks * rows, GROUPS * rows), f32)] * 2,
        ),
        out_shape=[jax.ShapeDtypeStruct((rows, H * HD), bf16)]
        + [jax.ShapeDtypeStruct((blocks // 2 * rows, 2 * KVH * HD), bf16)] * 2,
        compiler_params=params(),
        cost_estimate=cost(20 * rows * rows * blocks * H * HD, 8 * 2**20),
    )(pos, spans, queries, grads, lse, *kv_blocks, *after)


def middle_kernel(x_ref, att_ref, w_ref, gain_ref, middle_ref, rows_ref):
    step = pl.program_id(0)
    tile = w_ref.shape[1]
    columns = pl.ds(pl.multiple_of(step * tile, tile), tile)
    middle_ref[:, columns] = x_ref[...].astype(f32) + dot(att_ref[...], w_ref[...])

    @pl.when(step == pl.num_programs(0) - 1)
    def _():
        middle = middle_ref[...]
        factor = lax.rsqrt(jnp.mean(middle * middle, axis=-1, keepdims=True) + EPSILON)
        rows_ref[...] = (middle * factor * gain_ref[...]).astype(bf16)


def middle_forward(x, attended, w_out, gain, tile=512):
    rows, width = x.shape
    return pl.pallas_call(
        middle_kernel,
        grid=(width // tile,),
        in_specs=[
            pl.BlockSpec((rows, tile), lambda n: (0, n)),
            whole(attended.shape),
            pl.BlockSpec((w_out.shape[0], tile), lambda n: (0, n)),
            whole((1, width)),
        ],
        out_specs=[whole((rows, width))] * 2,
        out_shape=[
            jax.ShapeDtypeStruct((rows, width), f32),
            jax.ShapeDtypeStruct((rows, width), bf16),
        ],
        compiler_params=params(),
        cost_estimate=cost(2 * rows * width * width, 8 * 2**20),
    )(x, attended, w_out, gain.reshape(1, width))


def middle_back_kernel(parts, *refs):
    grad_refs = refs[:parts]
    middle_ref, cot_ref, gain_ref, w_ref = refs[parts : parts + 4]
    mgrad_ref, low_ref, dgain_ref, out_ref = refs[-4:]

    @pl.when(pl.program_id(0) == 0)
    def _():
        upstream = grad_refs[0][...].astype(f32)
        for ref in grad_refs[1:]:
            upstream = upstream + ref[...].astype(f32)
        middle = middle_ref[...]
        factor = lax.rsqrt(jnp.mean(middle * middle, axis=-1, keepdims=True) + EPSILON)
        scaled = upstream * gain_ref[...]
        inner = jnp.mean(scaled * middle, axis=-1, keepdims=True)
        grad = factor * scaled - middle * (factor * factor * factor * inner)
        grad = cot_ref[...].astype(f32) + grad
        mgrad_ref[...] = grad
        low_ref[...] = grad.astype(bf16)
        dgain_ref[...] = jnp.sum(upstream * middle * factor, axis=0, keepdims=True)

    out_ref[...] = dot_nt(low_ref[...], w_ref[...]).astype(bf16)


def middle_back(grads, middle, cotangent, gain, w_out, after=(), tile=512):
    rows, width = middle.shape
    inner = w_out.shape[0]
    return pl.pallas_call(
        functools.partial(middle_back_kernel, len(grads)),
        grid=(inner // tile,),
        in_specs=[whole((rows, width))] * (len(grads) + 2)
        + [whole((1, width)), pl.BlockSpec((tile, width), lambda n: (n, 0))]
        + anywhere(len(after)),
        out_specs=[
            whole((rows, width)),
            whole((rows, width)),
            whole((1, width)),
            pl.BlockSpec((rows, tile), lambda n: (0, n)),
        ],
        out_shape=[
            jax.ShapeDtypeStruct((rows, width), f32),
            jax.ShapeDtypeStruct((rows, width), bf16),
            jax.ShapeDtypeStruct((1, width), f32),
            jax.ShapeDtypeStruct((rows, inner), bf16),
        ],
        compiler_params=params(),
        cost_estimate=cost(2 * rows * width * inner, 16 * 2**20),
    )(*grads, middle, cotangent, gain.reshape(1, width), w_out, *after)


def input_back_kernel(dq_ref, dkv_ref, wq_ref, wk_ref, wv_ref, x_ref, gain_ref, mgrad_ref, *refs):
    out_ref, dgain_ref = refs[-2:]
    step = pl.program_id(0)
    term = dot_nt(dq_ref[...], wq_ref[...])
    term = term + dot_nt(dkv_ref[:, :HD], wk_ref[...]) + dot_nt(dkv_ref[:, HD:], wv_ref[...])

    @pl.when(step == 0)
    def _():
        out_ref[...] = term

    @pl.when(step > 0)
    def _():
        out_ref[...] += term

    @pl.when(step == pl.num_programs(0) - 1)
    def _():
        upstream = out_ref[...]
        x = x_ref[...].astype(f32)
        factor = lax.rsqrt(jnp.mean(x * x, axis=-1, keepdims=True) + EPSILON)
        scaled = upstream * gain_ref[...]
        inner = jnp.mean(scaled * x, axis=-1, keepdims=True)
        out_ref[...] = mgrad_ref[...] + factor * scaled - x * (factor * factor * factor * inner)
        dgain_ref[...] = jnp.sum(upstream * x * factor, axis=0, keepdims=True)


def input_back(dq, dkv, wq, wk, wv, x, gain, mgrad, after=()):
    rows, width = x.shape
    wide = GROUPS * HD
    return pl.pallas_call(
        input_back_kernel,
        grid=(KVH,),
        in_specs=[
            pl.BlockSpec((rows, wide), lambda g: (0, g)),
            pl.BlockSpec((rows, 2 * HD), lambda g: (0, g)),
            pl.BlockSpec((width, wide), lambda g: (0, g)),
            pl.BlockSpec((width, HD), lambda g: (0, g)),
            pl.BlockSpec((width, HD), lambda g: (0, g)),
            whole((rows, width)),
            whole((1, width)),
            whole((rows, width)),
        ]
        + anywhere(len(after)),
        out_specs=[whole((rows, width)), whole((1, width))],
        out_shape=[
            jax.ShapeDtypeStruct((rows, width), f32),
            jax.ShapeDtypeStruct((1, width), f32),
        ],
        compiler_params=params(),
        cost_estimate=cost(2 * rows * width * (H + 2 * KVH) * HD, 14 * 2**20),
    )(dq, dkv, wq, wk, wv, x, gain.reshape(1, width), mgrad, *after)


def gate_column(expert, gates):
    lanes = lax.broadcasted_iota(jnp.int32, gates.shape, 1)
    chosen = (lanes == expert) | (lanes == expert + LOW_LANE)
    return jnp.sum(jnp.where(chosen, gates.astype(f32), 0.0), axis=1, keepdims=True)


def experts_kernel(per, gated, extra, keeps, pos, x_ref, c_ref, *refs):
    weights = refs[:3]
    out_ref, grad_ref, *kept_refs, acc_o, acc_g = refs[3 + extra :]
    step = pl.program_id(0)
    last = pl.num_programs(0) - 1
    width = x_ref.shape[1]
    if keeps:

        @pl.when(step == 0)
        def _():
            kept_refs[0][...] = x_ref[...]
            kept_refs[1][...] = c_ref[...]
            kept_refs[2][...] = jnp.transpose(x_ref[...])
            kept_refs[3][...] = jnp.transpose(c_ref[:, :width])

    hid_ref, dgu_ref = kept_refs[-2:]

    def work(wg_ref, wu_ref, wd_ref):
        chunk = wg_ref.shape[1]
        x = x_ref[...]
        gate = dot(x, wg_ref[...])
        up = dot(x, wu_ref[...])
        slope = dot_nt(c_ref[:, :width], wd_ref[...])
        sigmoid = 1.0 / (1.0 + jnp.exp(-gate))
        act = gate * sigmoid
        hidden = act * up
        if gated:
            held = pl.num_programs(0) // per
            expert = (2 * pos[2] + pos[3]) * held + step // per
            weight = gate_column(expert, c_ref[:, width:])
            hidden = hidden * weight
            slope = slope * weight
        hidden = hidden.astype(bf16)
        dg = (slope * up * (sigmoid * (1.0 + gate * (1.0 - sigmoid)))).astype(bf16)
        du = (slope * act).astype(bf16)
        hid_ref[...] = hidden
        dgu_ref[:, :chunk] = dg
        dgu_ref[:, chunk:] = du
        out_term = dot(hidden, wd_ref[...])
        grad_term = dot_nt(dg, wg_ref[...]) + dot_nt(du, wu_ref[...])

        @pl.when(step == 0)
        def _():
            acc_o[...] = out_term
            acc_g[...] = grad_term

        @pl.when(step > 0)
        def _():
            acc_o[...] += out_term
            acc_g[...] += grad_term

    work(*weights)

    @pl.when(step == last)
    def _():
        out_ref[...] = acc_o[...].astype(out_ref.dtype)
        grad_ref[...] = acc_g[...].astype(grad_ref.dtype)


def experts(pos, x, c, weights, part, parts, kept, gated, kind, after=(), chunk=256):
    rows, width = x.shape
    inner = weights[2].shape[1]
    per = inner // chunk
    steps = weights[0].shape[0] * per
    specs = [
        pl.BlockSpec((None, width, chunk), lambda i, _: (i // per, 0, i % per)),
        pl.BlockSpec((None, width, chunk), lambda i, _: (i // per, 0, i % per)),
        pl.BlockSpec((None, chunk, width), lambda i, _: (i // per, i % per, 0)),
    ]
    collected = [
        jax.ShapeDtypeStruct((parts * rows, steps * chunk), bf16),
        jax.ShapeDtypeStruct((parts * rows, 2 * steps * chunk), bf16),
    ]
    collected_specs = [
        pl.BlockSpec((rows, chunk), lambda i, _: (part, i)),
        pl.BlockSpec((rows, 2 * chunk), lambda i, _: (part, i)),
    ]
    if gated:
        collected = [
            jax.ShapeDtypeStruct((parts * rows, width), bf16),
            jax.ShapeDtypeStruct((parts * rows, c.shape[1]), bf16),
            jax.ShapeDtypeStruct((width, parts * rows), bf16),
            jax.ShapeDtypeStruct((width, parts * rows), bf16),
        ] + collected
        collected_specs = [
            pl.BlockSpec((rows, width), lambda i, _: (part, 0)),
            pl.BlockSpec((rows, c.shape[1]), lambda i, _: (part, 0)),
            pl.BlockSpec((width, rows), lambda i, _: (0, part)),
            pl.BlockSpec((width, rows), lambda i, _: (0, part)),
        ] + collected_specs
    operands = [pos, x, c, *weights]
    aliases = {}
    if kept is not None:
        aliases = {len(operands) + j: 2 + j for j in range(len(collected))}
        operands += list(kept)
    extra = len(after) + (0 if kept is None else len(collected))
    operands += list(after)
    result = pl.pallas_call(
        functools.partial(experts_kernel, per, gated, extra, gated),
        grid_spec=pltpu.PrefetchScalarGridSpec(
            num_scalar_prefetch=1,
            grid=(steps,),
            in_specs=[whole((rows, width)), whole(c.shape)] + specs + anywhere(extra),
            out_specs=[whole((rows, width))] * 2 + collected_specs,
            scratch_shapes=[pltpu.VMEM((rows, width), f32)] * 2,
        ),
        out_shape=[jax.ShapeDtypeStruct((rows, width), kind)] * 2 + collected,
        input_output_aliases=aliases,
        compiler_params=params(),
        cost_estimate=cost(26 * rows * width * steps * chunk, 12 * 2**20),
    )(*operands)
    return result[0], result[1], result[2:]


def others_kernel(sets, per, bands, extra, pos, x_ref, c_ref, *refs):
    each = bands + per
    weights = [refs[t * each : (t + 1) * each] for t in range(sets)]
    *result_refs, hid_ref, dgu_ref = refs[sets * each + extra :]
    out_refs, grad_refs = result_refs[: len(result_refs) // 2], result_refs[len(result_refs) // 2 :]
    step = pl.program_id(0)
    width = x_ref.shape[1]
    band = width // bands
    chunk = weights[0][bands].shape[0]
    rows = out_refs[0].shape[0]

    def places(t, n):
        at = (lax.rem(pos[1] + t, 2) * per + n) * chunk
        cut = lambda first: pl.ds(pl.multiple_of(first, chunk), chunk)
        return cut(at), cut(2 * at), cut(2 * at + chunk)

    def columns(n):
        return slice(n * chunk, (n + 1) * chunk), slice((per + n) * chunk, (per + n + 1) * chunk)

    def hidden_chunk(t, n):
        at_hidden, at_gate, at_up = places(t, n)
        gate_cut, up_cut = columns(n)
        expert = (2 * pos[2] + 1 - pos[3]) * sets + lax.rem(pos[1] + t, 2)
        gate = up = 0.0
        for k in range(bands):
            part = x_ref[:, k * band : (k + 1) * band]
            gate = gate + dot(part, weights[t][k][:, gate_cut])
            up = up + dot(part, weights[t][k][:, up_cut])
        slope = dot_nt(c_ref[:, :width], weights[t][bands + n][...])
        sigmoid = 1.0 / (1.0 + jnp.exp(-gate))
        act = gate * sigmoid
        weight = gate_column(expert, c_ref[:, width:])
        slope = slope * weight
        hid_ref[:, at_hidden] = (act * up * weight).astype(bf16)
        dgu_ref[:, at_gate] = (slope * up * (sigmoid * (1.0 + gate * (1.0 - sigmoid)))).astype(bf16)
        dgu_ref[:, at_up] = (slope * act).astype(bf16)

    def results(k):
        out = grad = 0.0
        for t in range(sets):
            for n in range(per):
                at_hidden, at_gate, at_up = places(t, n)
                gate_cut, up_cut = columns(n)
                down = weights[t][bands + n][:, k * band : (k + 1) * band]
                out = out + dot(hid_ref[:, at_hidden], down)
                grad = grad + dot_nt(dgu_ref[:, at_gate], weights[t][k][:, gate_cut])
                grad = grad + dot_nt(dgu_ref[:, at_up], weights[t][k][:, up_cut])
        for p in range(len(out_refs)):
            out_refs[p][...] = out[p * rows : (p + 1) * rows].astype(bf16)
            grad_refs[p][...] = grad[p * rows : (p + 1) * rows].astype(bf16)

    for t in range(sets):
        for n in range(per):
            pl.when(step == t * per + n)(functools.partial(hidden_chunk, t, n))
    for k in range(bands):
        pl.when(step == sets * per + k)(functools.partial(results, k))


def others(pos, x, c, weights, part, parts, count, kept):
    taken, width = x.shape[0] // parts, x.shape[1]
    sets = len(weights)
    bands, downs = weights[0]
    per = len(downs)
    inner = per * downs[0].shape[0]
    flat = [v for bands_t, downs_t in weights for v in [*bands_t, *downs_t]]
    tile = width // len(bands)
    rows_spec = lambda v: pl.BlockSpec(
        (taken, v.shape[1]), lambda *_: (part, 0), pipeline_mode=pl.Buffered(1)
    )
    resident = lambda v: pl.BlockSpec(v.shape, lambda *_: (0, 0), pipeline_mode=pl.Buffered(1))
    late = lambda i: jnp.maximum(i - sets * per, 0)
    operands = [pos, x, c] + flat
    extra = 0 if kept is None else 2
    aliases = {len(operands) + j: 2 * count + j for j in range(extra)}
    collected = [sets * inner, 2 * sets * inner]
    result = pl.pallas_call(
        functools.partial(others_kernel, sets, per, len(bands), extra),
        grid_spec=pltpu.PrefetchScalarGridSpec(
            num_scalar_prefetch=1,
            grid=(sets * per + len(bands),),
            in_specs=[rows_spec(x), rows_spec(c)] + [resident(v) for v in flat] + anywhere(extra),
            out_specs=[pl.BlockSpec((taken // count, tile), lambda i, _: (0, late(i)))] * (2 * count)
            + [pl.BlockSpec((taken, n), lambda *_: (part, 0)) for n in collected],
        ),
        out_shape=[jax.ShapeDtypeStruct((taken // count, width), bf16)] * (2 * count)
        + [jax.ShapeDtypeStruct((parts * taken, n), bf16) for n in collected],
        input_output_aliases=aliases,
        compiler_params=params(),
        cost_estimate=cost(26 * taken * width * sets * inner, 12 * 2**20),
    )(*operands, *(kept or []))
    return result[:count], result[count : 2 * count], result[2 * count :]


def side_of(outer, s, pos):
    return 2 * lax.rem(s, outer) + lax.rem(pos[1] + 1 - s // outer, 2)


def halves_kernel(shape, outer, pos, *refs):
    sent_ref, kept_ref = refs[-2:]

    def write(out_ref):
        first = 0
        for i, rows in enumerate(shape):
            total = dot_tn(refs[2 * i][...], refs[2 * i + 1][...]).astype(bf16)
            blank = out_ref.shape[2] - total.shape[1]
            if blank:
                out_ref[:, first : first + rows, total.shape[1] :] = jnp.zeros(
                    (out_ref.shape[0], rows, blank), bf16
                )
            for e in range(out_ref.shape[0]):
                part = total[e * rows : (e + 1) * rows]
                out_ref[e, first : first + rows, : total.shape[1]] = part
            first += rows

    pl.when(pl.program_id(0) < outer)(lambda: write(sent_ref))
    pl.when(pl.program_id(0) >= outer)(lambda: write(kept_ref))


def halves(pos, pairs, after=()):
    n_ctx, n_exp = lax.axis_size("ctx"), lax.axis_size("exp")
    outer = n_ctx // 2
    shape = [left.shape[1] // (n_ctx * n_exp) for left, _ in pairs]
    wide = max(right.shape[1] for _, right in pairs)
    full = (outer * n_exp, sum(shape), wide)
    if any((left.shape[1] // n_ctx) % 128 for left, _ in pairs):
        out = []
        for side in (1, 0):
            parts = []
            for left, right in pairs:
                split = left.reshape(left.shape[0], outer, 2, -1)
                mine = lax.dynamic_index_in_dim(split, (pos[1] + side) % 2, 2, keepdims=False)
                total = dot_tn(mine.reshape(left.shape[0], -1), right).astype(bf16)
                total = total.reshape(outer * n_exp, -1, right.shape[1])
                parts.append(jnp.pad(total, ((0, 0), (0, 0), (0, wide - right.shape[1]))))
            joined = jnp.concatenate(parts, axis=1)
            out.append(jnp.pad(joined, ((0, 0), (0, -joined.shape[1] % 16), (0, 0))))
        return out
    in_specs, operands = [], []
    for left, right in pairs:
        columns = left.shape[1] // n_ctx
        in_specs.append(
            pl.BlockSpec((left.shape[0], columns), lambda s, pos: (0, side_of(outer, s, pos)))
        )
        in_specs.append(whole(right.shape))
        operands += [left, right]
    block = (n_exp,) + full[1:]
    flops = sum(2 * left.size * right.shape[1] for left, right in pairs)
    return pl.pallas_call(
        functools.partial(halves_kernel, shape, outer),
        grid_spec=pltpu.PrefetchScalarGridSpec(
            num_scalar_prefetch=1,
            grid=(2 * outer,),
            in_specs=in_specs + anywhere(len(after)),
            out_specs=[
                pl.BlockSpec(block, lambda s, pos: (jnp.minimum(s, outer - 1), 0, 0)),
                pl.BlockSpec(block, lambda s, pos: (jnp.maximum(s - outer, 0), 0, 0)),
            ],
        ),
        out_shape=[jax.ShapeDtypeStruct(full, bf16)] * 2,
        compiler_params=params(),
        cost_estimate=cost(2 * flops, 8 * 2**20),
    )(pos, *operands, *after)


def rows_product_kernel(blocks, pos, *refs):
    total = dot_tn(refs[0][...], refs[blocks][...])
    for b in range(1, blocks):
        total = total + dot_tn(refs[b][...], refs[blocks + b][...])
    refs[-1][...] = total.astype(bf16)


def rows_product(pos, lefts, rights, tile=512):
    n_ctx, n_exp = lax.axis_size("ctx"), lax.axis_size("exp")
    depth, height = lefts[0][0].shape
    high, wide = height // n_ctx, rights[0][0].shape[1]
    if high % 128:
        place = lax.axis_index("ctx") * high
        cut = lambda v: lax.slice_in_dim(v[0], v[1] * depth, (v[1] + 1) * depth, axis=0)
        total = sum(
            dot_tn(lax.dynamic_slice_in_dim(cut(a), place, high, 1), cut(b))
            for a, b in zip(lefts, rights)
        )
        return total.astype(bf16).reshape(n_exp, -1, wide)
    blocks = len(lefts)
    left_specs = [
        pl.BlockSpec((depth, high), functools.partial(lambda k, n, pos: (k, 2 * pos[0] + pos[1]), k))
        for _, k in lefts
    ]
    right_specs = [
        pl.BlockSpec((depth, tile), functools.partial(lambda k, n, pos: (k, n), k)) for _, k in rights
    ]
    total = pl.pallas_call(
        functools.partial(rows_product_kernel, blocks),
        grid_spec=pltpu.PrefetchScalarGridSpec(
            num_scalar_prefetch=1,
            grid=(wide // tile,),
            in_specs=left_specs + right_specs,
            out_specs=pl.BlockSpec((high, tile), lambda n, pos: (0, n)),
        ),
        out_shape=jax.ShapeDtypeStruct((high, wide), bf16),
        compiler_params=params(),
        cost_estimate=cost(4 * blocks * depth * high * wide, 4 * 2**20),
    )(pos, *[v for v, _ in lefts], *[v for v, _ in rights])
    return total.reshape(n_exp, -1, wide)


def expert_halves_kernel(blocks, tiles, pos, *refs):
    rows_refs, cot_refs = refs[:blocks], refs[blocks : 2 * blocks]
    dgu_ref, hid_ref, sent_ref, kept_ref = refs[2 * blocks :]
    n = pl.program_id(0)
    high = sent_ref.shape[1]

    def write(left_refs, right_ref):
        left = jnp.concatenate([ref[...] for ref in left_refs], axis=0)
        total = dot(left, right_ref[...]).astype(bf16)
        count = sent_ref.shape[0]
        for i in range(count):
            sent_ref[i] = total[i * high : (i + 1) * high]
            kept_ref[i] = total[(count + i) * high : (count + i + 1) * high]

    pl.when(n < tiles)(lambda: write(rows_refs, dgu_ref))
    pl.when(n >= tiles)(lambda: write(cot_refs, hid_ref))


def expert_steps(width):
    high = width // lax.axis_size("ctx")
    return high // 128 if high % 128 == 0 else 1


def expert_halves(pos, rows_t, cot_t, dgu, hid, tile=512):
    n_ctx = lax.axis_size("ctx")
    width, depth = rows_t.shape
    high = width // n_ctx
    wide = dgu.shape[1] + hid.shape[1]
    steps = expert_steps(width)
    tiles, down = dgu.shape[1] // tile, hid.shape[1] // tile
    left_specs = [
        pl.BlockSpec((high, depth), functools.partial(lambda s, n, pos: (side_of(n_ctx // 2, s, pos), 0), s))
        for s in range(n_ctx)
    ]
    block = (n_ctx // 2 * steps, high // steps, tile)
    return pl.pallas_call(
        functools.partial(expert_halves_kernel, n_ctx, tiles),
        grid_spec=pltpu.PrefetchScalarGridSpec(
            num_scalar_prefetch=1,
            grid=(tiles + down,),
            in_specs=left_specs * 2
            + [
                pl.BlockSpec((depth, tile), lambda n, pos: (0, jnp.minimum(n, tiles - 1))),
                pl.BlockSpec((depth, tile), lambda n, pos: (0, jnp.maximum(n - tiles, 0))),
            ],
            out_specs=[pl.BlockSpec(block, lambda n, pos: (0, 0, n))] * 2,
        ),
        out_shape=[jax.ShapeDtypeStruct(block[:2] + (wide,), bf16)] * 2,
        compiler_params=params(),
        cost_estimate=cost(4 * depth * width * wide, 16 * 2**20),
    )(pos, *[rows_t] * n_ctx, *[cot_t] * n_ctx, dgu, hid)


def sums_kernel(shape, only, extra, pos, *refs):
    ins, outs = refs[: sum(shape)], refs[sum(shape) + extra :]
    at = 0
    for count, out in zip(shape, outs):
        total = ins[at][...].astype(f32)
        for k in range(at + 1, at + count):
            term = ins[k][...].astype(f32)
            if only[k] is not None:
                term = jnp.where(pl.program_id(0) == only[k], term, 0.0)
            total = total + term
        out[...] = total.astype(out.dtype)
        at += count


def sums(pos, steps, outputs, after=()):
    operands, in_specs, out_specs, out_shape, only = [], [], [], [], []
    for kind, block, terms in outputs:
        for array, index, *step in terms:
            operands.append(array)
            only.append(step[0] if step else None)
            in_specs.append(pl.BlockSpec(block, functools.partial(place_of, index)))
        out_specs.append(pl.BlockSpec(block, lambda i, pos: (i, 0, 0)))
        out_shape.append(jax.ShapeDtypeStruct((steps * block[0],) + tuple(block[1:]), kind))
    return pl.pallas_call(
        functools.partial(sums_kernel, [len(terms) for _, _, terms in outputs], only, len(after)),
        grid_spec=pltpu.PrefetchScalarGridSpec(
            num_scalar_prefetch=1,
            grid=(steps,),
            in_specs=in_specs + anywhere(len(after)),
            out_specs=out_specs,
        ),
        out_shape=out_shape,
        compiler_params=params(),
        cost_estimate=cost(0, 8 * 2**20),
    )(pos, *operands, *after)


def place_of(index, i, pos):
    at = index(i, pos)
    return at if isinstance(at, tuple) else (at, 0, 0)


def straight(i, pos):
    return i


def row_sum(terms, kind=bf16):
    total = terms[0].astype(f32)
    for term in terms[1:]:
        total = total + term.astype(f32)
    return total.astype(kind)


def expert_out_kernel(gates, each, *refs):
    in_refs, (gate_ref, up_ref, down_ref) = refs[:4], refs[4:]
    n = pl.program_id(0)

    def write(ref):
        @pl.when((n < gates) & (lax.rem(n, 2) == 0))
        def _():
            gate_ref[0] = ref[...].astype(f32)

        @pl.when((n < gates) & (lax.rem(n, 2) == 1))
        def _():
            up_ref[0] = ref[...].astype(f32)

        @pl.when(n >= gates)
        def _():
            down_ref[0] = jnp.transpose(ref[...].astype(f32))

    for q in range(4):
        pl.when(n // each == q)(functools.partial(write, in_refs[q]))


def expert_out(quarters, inner, chunk=256):
    rows, wide = quarters[0].shape
    each = wide // chunk
    held = 4 * wide // (3 * inner)
    per = inner // chunk
    gates = 2 * held * per
    tile = lambda n: jnp.minimum(n, gates - 1) // 2
    spec = pl.BlockSpec((1, rows, chunk), lambda n: (tile(n) // per, 0, lax.rem(tile(n), per)))
    at = lambda n: jnp.maximum(n - gates, 0)
    return pl.pallas_call(
        functools.partial(expert_out_kernel, gates, each),
        grid=(4 * each,),
        in_specs=[
            pl.BlockSpec(
                (rows, chunk),
                functools.partial(lambda q, n: (0, jnp.clip(n - q * each, 0, each - 1)), q),
            )
            for q in range(4)
        ],
        out_specs=[
            spec,
            spec,
            pl.BlockSpec((1, chunk, rows), lambda n: (at(n) // per, lax.rem(at(n), per), 0)),
        ],
        out_shape=[jax.ShapeDtypeStruct((held, rows, inner), f32)] * 2
        + [jax.ShapeDtypeStruct((held, inner, rows), f32)],
        compiler_params=params(),
        cost_estimate=cost(0, 8 * 2**20),
    )(*quarters)


def last_sum(refs):
    total = refs[0][...].astype(f32)
    for ref in refs[1:]:
        total = total + ref[...].astype(f32)
    return total


def dense_out_kernel(count, *refs):
    total = last_sum(refs[:count])
    out_ref, query_ref, key_ref, value_ref = refs[count:]
    wide = out_ref.shape[1]
    out_ref[...] = total[:, :wide]
    query_ref[...] = total[:, wide : 2 * wide]
    for g in range(KVH):
        first = 2 * wide + 2 * g * HD
        key_ref[:, g * HD : (g + 1) * HD] = total[:, first : first + HD]
        value_ref[:, g * HD : (g + 1) * HD] = total[:, first + HD : first + 2 * HD]


def dense_out(terms, wide):
    rows = terms[0].shape[0]
    shapes = [wide, wide, KVH * HD, KVH * HD]
    return pl.pallas_call(
        functools.partial(dense_out_kernel, len(terms)),
        out_shape=[jax.ShapeDtypeStruct((rows, n), f32) for n in shapes],
        compiler_params=params(),
        cost_estimate=cost(0, 2**20),
    )(*terms)


def shared_out_kernel(count, chunk, *refs):
    total = last_sum(refs[:count])
    gate_ref, up_ref, down_ref = refs[count:]
    rows = gate_ref.shape[0]
    for n in range(gate_ref.shape[1] // chunk):
        cut = slice(n * chunk, (n + 1) * chunk)
        gate_ref[:, cut] = total[:rows, 2 * n * chunk : (2 * n + 1) * chunk]
        up_ref[:, cut] = total[:rows, (2 * n + 1) * chunk : (2 * n + 2) * chunk]
    down_ref[...] = total[rows : rows + down_ref.shape[0], : down_ref.shape[1]]


def shared_grads(terms, gate, down, chunk=256):
    return pl.pallas_call(
        functools.partial(shared_out_kernel, len(terms), chunk),
        out_shape=[jax.ShapeDtypeStruct(v, f32) for v in (gate, gate, down)],
        compiler_params=params(),
        cost_estimate=cost(0, 2**20),
    )(*terms)


def hold(values, after):
    count = len(values)
    return pl.pallas_call(
        lambda *_: None,
        in_specs=[pl.BlockSpec(memory_space=pl.ANY)] * (count + len(after)),
        out_specs=[pl.BlockSpec(memory_space=pl.ANY)] * count,
        out_shape=[jax.ShapeDtypeStruct(v.shape, v.dtype) for v in values],
        input_output_aliases={i: i for i in range(count)},
        compiler_params=params(),
        cost_estimate=cost(0, 0),
    )(*values, *after)


def swap_inner(value, axis):
    size = lax.axis_size(axis)
    return lax.ppermute(value, axis, [(i, i ^ 1) for i in range(size)])


def shift_outer(value, axis, by):
    outer = lax.axis_size(axis) // 2
    perm = [(o * 2 + i, ((o + by) % outer) * 2 + i) for o in range(outer) for i in range(2)]
    return lax.ppermute(value, axis, perm)


def ring_step(value, by):
    n_ctx, n_exp = lax.axis_size("ctx"), lax.axis_size("exp")
    outer = n_exp // 2
    perm = []
    for c in range(n_ctx):
        way = by if c % 2 == 0 else -by
        for o in range(outer):
            for i in range(2):
                perm.append((c * n_exp + o * 2 + i, c * n_exp + ((o + way) % outer) * 2 + i))
    return lax.ppermute(value, BOTH, perm)


def by_blocks(value, together):
    return value.reshape(-1, together * value.shape[1], value.shape[2])


def spread_outer(value):
    moved, out = value, []
    for _ in range(1, lax.axis_size("ctx") // 2):
        moved = shift_outer(moved, "ctx", 1)
        out.append(moved)
    return out, swap_inner(value, "ctx")


def spread_inner(moved):
    return [swap_inner(v, "ctx") for v in moved]


def outer_blocks(value):
    moved, out = value, []
    for _ in range(1, lax.axis_size("ctx") // 2):
        moved = shift_outer(moved, "ctx", 1)
        out.append(moved)
    return out


def inner_blocks(value, moved):
    return swap_inner(jnp.concatenate([value] + moved, axis=0), "ctx")


def all_blocks(value, moved, across):
    out = []
    for k, v in enumerate([value] + moved):
        out += [(v, 0), (across, k)]
    return out


def spread_all(value, moved, across, moved_across):
    blocks = [value, across]
    for a, b in zip(moved, moved_across):
        blocks += [a, b]
    return blocks


def paired_blocks(value, across, moved, moved_across):
    out = [(value, 0), (across, 0)]
    for a, b in zip(moved, moved_across):
        out += [(a, 0), (b, 0)]
    return out


class Shared:
    def __init__(self, pos, kept, got):
        self.pos = pos
        self.outer, self.levels = lax.axis_size("ctx") // 2, lax.axis_size("exp") // 2
        self.rows, self.wide = kept.shape[1:]
        self.pair = lambda v: v.reshape(-1, 2 * self.rows, self.wide)
        self.terms = [self.pair(v) for v in (kept, got)]
        self.together = 2 if self.levels % 2 == 0 else 1
        self.steps = self.levels // self.together

    def _sum(self, d, rows, inner, moved=()):
        at = lambda i, pos: lax.rem(pos[0] + d, self.outer) * self.steps + i
        terms = [(v, lambda i, pos: (at(i, pos), inner(pos), 0)) for v in self.terms]
        for parts in moved:
            for k, v in enumerate(parts):
                terms.append((self.pair(v), lambda i, pos: (0, inner(pos), 0), k))
        return terms, (self.together, rows, self.wide)

    def first(self):
        out = []
        for d in range(1, self.outer):
            terms, block = self._sum(d, 2 * self.rows, lambda pos: 0)
            outputs = []
            for k in range(self.steps):
                part = [(v, functools.partial(lambda f, k, i, pos: f(k, pos), f, k)) for v, f in terms]
                outputs.append((bf16, block, part))
            out.append(sums(self.pos, 1, outputs))
        return out

    def second(self, moved):
        terms, block = self._sum(0, self.rows, lambda pos: 1 - pos[3], moved)
        outputs = []
        for k in range(self.steps):
            part = [(v, functools.partial(lambda f, k, i, pos: f(k, pos), f, k)) for v, f, *o in terms if not o or o[0] == k]
            outputs.append((bf16, block, part))
        return sums(self.pos, 1, outputs)

    def total(self, moved, crossed):
        terms, block = self._sum(0, self.rows, lambda pos: pos[3], moved)
        terms = terms + [(v, lambda i, pos: 0, k) for k, v in enumerate(crossed)]
        return sums(self.pos, self.steps, [(bf16, block, terms)])[0]


def z_take(total, d):
    levels = total.shape[0]
    return lax.dynamic_index_in_dim(total, (lax.axis_index("exp") // 2 + d) % levels, 0, False)


def z_send(total, d):
    return shift_outer(z_take(total, d), "exp", d)


def over_x(total):
    pairs = total.reshape((-1, 2) + total.shape[1:])
    return swap_inner(lax.dynamic_index_in_dim(pairs, 1 - lax.axis_index("exp") % 2, 1, False), "exp")


def mine_x(total):
    pairs = total.reshape((-1, 2) + total.shape[1:])
    return lax.dynamic_index_in_dim(pairs, lax.axis_index("exp") % 2, 1, False)


def over_z(mine, arrived):
    mine = mine.astype(f32) + arrived.astype(f32)
    levels, level = mine.shape[0], lax.axis_index("exp") // 2
    take = lambda d: lax.dynamic_index_in_dim(mine, (level + d) % levels, 0, False)
    return [take(0)] + [shift_outer(take(d).astype(bf16), "exp", d) for d in range(1, levels)]


def expert_quarter(kept, got, q, row):
    steps = kept.shape[0] // (lax.axis_size("ctx") // 2)
    block = (steps, kept.shape[1], kept.shape[2] // 4)
    return block, [(v, lambda i, pos: (row(i, pos), 0, q)) for v in (kept, got)]


def expert_pieces(pos, kept, got, quarters):
    outputs = []
    for q in quarters:
        block, terms = expert_quarter(kept, got, q, straight)
        outputs.append((bf16, block, terms))
    return sums(pos, lax.axis_size("ctx") // 2, outputs)


def expert_row(d):
    outer = lax.axis_size("ctx") // 2
    return lambda i, pos: lax.rem(pos[0] + d, outer)


def expert_send(pos, kept, got, pieces, half):
    sent = []
    for d in range(1, lax.axis_size("ctx") // 2):
        row = expert_row(d)
        block, terms = expert_quarter(kept, got, 0, row)
        terms = [(v, lambda i, pos: (row(i, pos), 0, 2 * half + i)) for v, _ in terms]
        terms += [(pieces[2 * half + k], lambda i, pos: row(0, pos), k) for k in range(2)]
        sent += sums(pos, 2, [(bf16, block, terms)])
    return sent


def expert_move(sent):
    return [shift_outer(v, "ctx", d + 1) for d, v in enumerate(sent)]


def expert_total(pos, kept, got, pieces, arrived):
    row = expert_row(0)
    outputs = []
    for q in range(4):
        block, terms = expert_quarter(kept, got, q, row)
        at = functools.partial(lambda k, i, pos: k, q % 2)
        terms = terms + [(pieces[q], row)] + [(v, at) for v in arrived[q // 2]]
        outputs.append((bf16, block, terms))
    return [v.reshape(-1, v.shape[2]) for v in sums(pos, 1, outputs)]


def shards(
    layer_input,
    attn_gain,
    w_query,
    w_key,
    w_value,
    w_out,
    ffn_gain,
    shared_gate,
    shared_up,
    shared_down,
    expert_gate,
    expert_up,
    expert_down,
    routes,
    gate_logits,
    span_order,
    cotangent,
):
    x = layer_input[0]
    cot = cotangent[0]
    tokens, width = x.shape
    span_rows = tokens // 2
    n_ctx, n_exp = lax.axis_size("ctx"), lax.axis_size("exp")
    ctx_id, exp_id = lax.axis_index("ctx"), lax.axis_index("exp")
    local_experts, _, inner = expert_gate.shape
    expert_count = local_experts * n_exp

    levels = n_exp // 2
    pos = jnp.stack([ctx_id // 2, ctx_id % 2, exp_id // 2, exp_id % 2]).astype(jnp.int32)

    always = pos[0] < n_ctx
    ring = n_ctx // 2

    def region(work):
        made = jax.eval_shape(work)
        return lax.cond(always, work, lambda: jax.tree.map(lambda v: jnp.zeros(v.shape, v.dtype), made))

    gate_vals = jax.nn.softmax(gate_logits[0], axis=-1)
    named = routes[0][:, None, :] == jnp.arange(expert_count, dtype=jnp.int32)[None, :, None]
    row_gates = jnp.sum(jnp.where(named, gate_vals[:, None, :], 0.0), axis=-1)
    high = row_gates.astype(bf16)
    low = (row_gates - high.astype(f32)).astype(bf16)
    fill = lambda width: ((0, 0), (0, width - expert_count))
    cot_ring = [
        jnp.concatenate(
            [cot, jnp.pad(high, fill(LOW_LANE)), jnp.pad(low, fill(GATE_LANES - LOW_LANE))], axis=1
        )
    ]

    chunk, bands = 256, 3
    mine = lambda v: lax.dynamic_index_in_dim(v, pos[1], 0, keepdims=False)
    over_core = lambda v: swap_inner(v, "ctx")

    def fetch(k):
        return swap_inner(asked[k], "exp")

    def arranged(parts):
        return parts[inner // chunk :], parts[: inner // chunk]

    def ask():
        down = mine(expert_down)
        out = [down[n * chunk : (n + 1) * chunk] for n in range(inner // chunk)]
        gate, up = mine(expert_gate), mine(expert_up)
        band = width // bands
        for k in range(bands):
            cut = slice(k * band, (k + 1) * band)
            out.append(jnp.concatenate([gate[cut], up[cut]], axis=1))
        return out

    def gather_keys():
        normed, kv = keyvalue(x, attn_gain, w_key, w_value)
        moved, across = spread_outer(kv)
        queries = dot(normed, w_query).astype(bf16)
        asked = ask()
        keys = kv, moved, across, spread_inner(moved)
        return normed, keys, queries, ring_step(cot_ring[0], 1), asked, swap_inner(asked[0], "exp")

    normed, keys, queries, cot_next, asked, got = region(gather_keys)
    kv_blocks = spread_all(*keys)
    cot_ring.append(cot_next)
    fetched, crossed = [got], []

    def attention():
        attended, lse = attend(pos, span_order, queries, kv_blocks)
        middle, rows = middle_forward(x, attended, w_out, ffn_gain)
        moved = outer_blocks(normed), ring_step(cot_ring[1], 1), fetch(1), over_core(fetched[0])
        return attended, lse, middle, rows, over_core(normed), *moved

    attended, lse, middle, rows_low, across, normed_moved, cot_next, got, crossing = region(attention)
    normed_across = across
    cot_ring.append(cot_next)
    fetched.append(got)
    crossed.append(crossing)

    def own_part(k, rows, kept):
        weights = (expert_gate, expert_up, expert_down)
        return experts(pos, rows, cot_ring[k], weights, k, levels, kept, True, bf16)

    def first():
        weights = (shared_gate[None], shared_up[None], shared_down[None])
        shared = experts(pos, rows_low, cot, weights, 0, 1, None, False, f32)
        more = spread_inner(normed_moved), fetch(2), over_core(fetched[1]), outer_blocks(attended)
        return ring_step(rows_low, 1), shared, *more

    rows_one, shared, across, got, crossing, attended_moved = region(first)
    fetched.append(got)
    crossed.append(crossing)
    normed_blocks = paired_blocks(normed, normed_across, normed_moved, across)
    shared_out, shared_grad, (shared_hidden, shared_dgu) = shared
    shared_pairs = [(rows_low, shared_dgu), (shared_hidden, cot)]

    def second():
        result = own_part(0, rows_low, None)
        more = fetch(3), over_core(fetched[2]), [over_core(attended), *spread_inner(attended_moved)]
        return ring_step(rows_one, 1), result, halves(pos, shared_pairs), *more

    rows_two, (out_k, grad_k, kept), (shared_sent, shared_kept), got, crossing, across = region(second)
    attended_blocks = paired_blocks(attended, across[0], attended_moved, across[1:])
    fetched.append(got)
    crossed.append(crossing)
    out_own, grad_own = [out_k], [grad_k]

    def third():
        more = over_core(shared_sent), fetch(4), over_core(fetched[3])
        one = own_part(1, rows_one, kept)
        two = own_part(2, rows_two, one[2])
        return ring_step(rows_two, 1), one[:2], two, *more

    rows_k, one, two, shared_got, got, crossing = region(third)
    fetched.append(got)
    crossed.append(crossing)
    kept = two[2]
    out_own += [one[0], two[0]]
    grad_own += [one[1], two[1]]

    def over_y(parts, k):
        return [shift_outer(v[k], "ctx", d + 1) for d, v in enumerate(parts)]

    def fourth():
        moved = ring_step(cot_ring[2], 1)
        weights = [arranged(fetched), arranged(crossed + [over_core(fetched[4])])]
        half = levels // 2
        sent = Shared(pos, shared_kept, shared_got).first()
        arrived = [over_y(sent, k) for k in range(len(sent[0]))]
        out_a, grad_a, new = others(pos, kept[0], kept[1], weights, 0, 2, half, None)
        out_k, grad_k, more = experts(
            pos, rows_k, moved, (expert_gate, expert_up, expert_down), 3, levels, kept, True, bf16
        )
        out_b, grad_b, new = others(pos, more[0], more[1], weights, 1, 2, half, new)
        return out_k, grad_k, more, [*out_a, *out_b], [*grad_a, *grad_b], new, arrived

    out_k, grad_k, kept, out_other, grad_other, kept_other, got = region(fourth)
    shared_moved = [list(v) for v in zip(*got)]
    out_own.append(out_k)
    grad_own.append(grad_k)
    rows_all, cot_all, rows_t, cot_t, hid_own, dgu_own = kept
    hid_other, dgu_other = kept_other

    def back_one():
        moved = ring_step(row_sum([grad_own[3], grad_other[3]]), -1)
        parts = Shared(pos, shared_kept, shared_got).second(shared_moved)
        crossed = [swap_inner(v, "exp") for v in parts[: len(parts) // 2]]
        made = expert_halves(pos, rows_t, cot_t, dgu_other, hid_other)
        return moved, made, crossed, parts[len(parts) // 2 :]

    moved, (sent, kept_other), shared_crossed, shared_rest = region(back_one)

    def back_two():
        total = row_sum([grad_own[2], grad_other[2], moved])
        got = swap_inner(sent, "ctx")
        crossed = [swap_inner(v, "exp") for v in shared_rest]
        made = expert_halves(pos, rows_t, cot_t, dgu_own, hid_own)
        return ring_step(total, -1), got, made, expert_pieces(pos, kept_other, got, [0])[0], crossed

    moved_two, got_other, (sent_own, kept_own), piece, got = region(back_two)
    shared_crossed = shared_crossed + got

    def back_three():
        total = row_sum([grad_own[1], grad_other[1], moved_two])
        made = expert_pieces(pos, kept_other, got_other, [1, 2, 3])
        shared_sum = Shared(pos, shared_kept, shared_got).total(shared_moved, shared_crossed)
        out_total = row_sum([out_own[3], out_other[3]])
        middle_grads = middle_back(
            [shared_grad, grad_own[0], grad_other[0], ring_step(total, -1)],
            middle,
            cot,
            ffn_gain,
            w_out,
        )
        moved = middle_grads, swap_inner(sent_own, "ctx"), swap_inner(piece, "exp")
        shared_z = [z_take(shared_sum, d) for d in range(levels)]
        return *moved, made, shared_z, out_total

    middle_grads, got_own, piece, made, shared_z, out_total = region(back_three)
    mgrad, mgrad_low, ffn_gain_grad, att_grad = middle_grads
    pieces = [piece, *made]

    def attention_back():
        dq, same, across = attend_back(pos, span_order, queries, att_grad, lse, kv_blocks)
        got = ring_step(out_total, -1), swap_inner(pieces[1], "exp"), shift_outer(shared_z[1], "exp", 1)
        mgrad_parts = mgrad_low, over_core(mgrad_low), outer_blocks(mgrad_low)
        return mgrad_parts, dq, same, across, *got

    mgrad_parts, dq, same, across, out_moved, piece, got = region(attention_back)
    pieces[1] = piece
    shared_parts = [shared_z[0], got]

    def dense_one():
        got = over_core(across)
        made = []
        for k in reversed(range(ring)):
            part = slice(k * tokens, (k + 1) * tokens)
            made = row_sum([same[part], got[part]] + made)
            if k:
                made = [shift_outer(made, "ctx", -1)]
        total = row_sum([out_own[2], out_other[2], out_moved])
        mgrad_blocks = paired_blocks(*mgrad_parts, spread_inner(mgrad_parts[2]))
        total_out = rows_product(pos, attended_blocks, mgrad_blocks)
        sent = expert_send(pos, kept_own, got_own, pieces, 0)
        total = row_sum([out_own[1], out_other[1], ring_step(total, -1)])
        return made, outer_blocks(dq), total_out, sent, total, swap_inner(pieces[2], "exp")

    dkv, dq_moved, total_out, sent, out_total_two, piece = region(dense_one)
    pieces[2] = piece

    def dense_two():
        dkv_moved = outer_blocks(dkv)
        dkv_blocks = all_blocks(dkv, dkv_moved, inner_blocks(dkv, dkv_moved))
        dq_blocks = all_blocks(dq, dq_moved, inner_blocks(dq, dq_moved))
        total_query = rows_product(pos, normed_blocks, dq_blocks)
        total_kv = rows_product(pos, normed_blocks, dkv_blocks)
        back = input_back(dq, dkv, w_query, w_key, w_value, x, attn_gain, mgrad)
        moved = ring_step(out_total_two, -1), swap_inner(pieces[3], "exp"), expert_move(sent)
        return total_query, total_kv, back, *moved

    total_query, total_kv, (input_grad, attn_gain_grad), out_moved_three, piece, got = region(dense_two)
    pieces[3] = piece
    arrived = [got]

    def dense_three():
        devices = n_ctx * n_exp
        total = jnp.concatenate([total_out, total_query, total_kv], axis=2)
        got = expert_move(expert_send(pos, kept_own, got_own, pieces, 1))
        layer_out = row_sum([middle, shared_out, out_own[0], out_other[0], out_moved_three])
        more = [shift_outer(shared_z[d], "exp", d) for d in range(2, levels)]
        gains = jnp.stack(
            [attn_gain_grad.reshape(devices, -1), ffn_gain_grad.reshape(devices, -1)], axis=1
        )
        gains = lax.all_to_all(gains, BOTH, split_axis=0, concat_axis=0, tiled=True)
        return mine_x(total), over_x(total), got, layer_out, more, gains

    total, total_x, got, layer_out, more, gains = region(dense_three)
    shared_parts += more
    arrived.append(got)

    def dense_four():
        grads = expert_out(expert_total(pos, kept_own, got_own, pieces, arrived), inner)
        shape = lambda v: (v.shape[0] // (n_ctx * n_exp), v.shape[1])
        shared = shared_grads(
            shared_parts, shape(shared_gate), shape(shared_down)
        )
        dense = dense_out(over_z(total, total_x), x.shape[1])
        return jnp.sum(gains, axis=0), shared, dense, grads

    gains, (sum_gate, sum_up, sum_down), dense, expert_grads = region(dense_four)
    sum_out, sum_query, sum_key, sum_value = dense
    return (
        layer_out[None],
        input_grad[None],
        gains[0],
        sum_query,
        sum_key,
        sum_value,
        sum_out,
        gains[1],
        sum_gate,
        sum_up,
        sum_down,
        *expert_grads,
    )


def solution(mesh):
    return jax.shard_map(
        shards,
        mesh=mesh,
        in_specs=(
            P("exp", "ctx", None),
            P(),
            P(),
            P(),
            P(),
            P(),
            P(),
            P(),
            P(),
            P(),
            P("exp", None, None),
            P("exp", None, None),
            P("exp", None, None),
            P("exp", "ctx", None),
            P("exp", "ctx", None),
            P(),
            P("exp", "ctx", None),
        ),
        out_specs=(
            P("exp", "ctx", None),
            P("exp", "ctx", None),
            P(("ctx", "exp")),
            P(("ctx", "exp"), None),
            P(("ctx", "exp"), None),
            P(("ctx", "exp"), None),
            P(("ctx", "exp"), None),
            P(("ctx", "exp")),
            P(("ctx", "exp"), None),
            P(("ctx", "exp"), None),
            P(("ctx", "exp"), None),
            P("exp", "ctx", None),
            P("exp", "ctx", None),
            P("exp", None, "ctx"),
        ),
        check_vma=False,
    )
```

```python
import functools

import jax
import jax.numpy as jnp
from jax import lax
from jax.experimental import pallas as pl
from jax.experimental.pallas import tpu as pltpu
from jax.sharding import PartitionSpec as P

H = 12
HD = 128
KVH = 4
GROUPS = H // KVH
EPSILON = 1e-06
GATE_LANES = 128
LOW_LANE = 64
NEGATIVE = -1e30
SCALE = HD ** (-0.5)
BOTH = ("ctx", "exp")
VMEM_LIMIT = 60 * 2**20
bf16 = jnp.bfloat16
f32 = jnp.float32


def dot(left_op, right_op):
    return jnp.dot(left_op, right_op, preferred_element_type=f32)


def dot_nt(left_op, right_op):
    return lax.dot_general(left_op, right_op, (((1,), (1,)), ((), ())), preferred_element_type=f32)


def dot_tn(left_op, right_op):
    return lax.dot_general(left_op, right_op, (((0,), (0,)), ((), ())), preferred_element_type=f32)


def whole(shape):
    return pl.BlockSpec(shape, lambda *_: (0,) * len(shape))


def params():
    return pltpu.CompilerParams(vmem_limit_bytes=VMEM_LIMIT)


def anywhere(count):
    return [pl.BlockSpec(memory_space=pl.ANY)] * count


def cost(flops, nbytes):
    return pl.CostEstimate(flops=flops // 4, bytes_accessed=nbytes // 4, transcendentals=0)


def keyvalue_kernel(x_ref, gain_ref, wk_ref, wv_ref, normed_ref, kv_ref):
    @pl.when(pl.program_id(0) == 0)
    def _():
        x = x_ref[...].astype(f32)
        factor = lax.rsqrt(jnp.mean(x * x, axis=-1, keepdims=True) + EPSILON)
        normed_ref[...] = (x * factor * gain_ref[...]).astype(bf16)

    both = jnp.concatenate([wk_ref[...], wv_ref[...]], axis=1)
    kv_ref[...] = dot(normed_ref[...], both).astype(bf16)


def keyvalue(x, gain, wk, wv):
    rows, width = x.shape
    return pl.pallas_call(
        keyvalue_kernel,
        grid=(KVH,),
        in_specs=[
            whole((rows, width)),
            whole((1, width)),
            pl.BlockSpec((width, HD), lambda g: (0, g)),
            pl.BlockSpec((width, HD), lambda g: (0, g)),
        ],
        out_specs=[whole((rows, width)), pl.BlockSpec((rows, 2 * HD), lambda g: (0, g))],
        out_shape=[
            jax.ShapeDtypeStruct((rows, width), bf16),
            jax.ShapeDtypeStruct((rows, 2 * KVH * HD), bf16),
        ],
        compiler_params=params(),
        cost_estimate=cost(4 * rows * width * KVH * HD, 5 * 2**20),
    )(x, gain.reshape(1, width), wk, wv)


def stack_heads(ref):
    return jnp.concatenate([ref[:, r * HD : (r + 1) * HD] for r in range(GROUPS)], axis=0)


def places(pos, spans, block, shape, dim, rows):
    outer, side = (0, 0) if block is None else (block // 2, block % 2)
    ring = spans.shape[0] // 4
    owner = 2 * lax.rem(pos[0] + ring - outer, ring) + lax.rem(pos[1] + side, 2)
    row = lax.broadcasted_iota(jnp.int32, shape, dim) % rows
    half = rows // 2
    first, second = spans[2 * owner] * half, spans[2 * owner + 1] * half
    return jnp.where(row < half, first + row, second + row - half)


def attend_kernel(blocks, extra, pos, spans, q_ref, *refs):
    kv_refs = refs[:blocks]
    out_ref, lse_ref, score_ref = refs[blocks + extra :]
    rows = q_ref.shape[0]
    queries = stack_heads(q_ref)
    wanted = places(pos, spans, None, (1, GROUPS * rows), 1, rows)
    peak = jnp.full((1, GROUPS * rows), NEGATIVE, f32)
    for b in range(blocks):
        scores = dot_nt(kv_refs[b][:, :HD], queries) * SCALE
        visible = places(pos, spans, b, (rows, 1), 0, rows) <= wanted
        scores = jnp.where(visible, scores, NEGATIVE)
        score_ref[b * rows : (b + 1) * rows, :] = scores
        peak = jnp.maximum(peak, jnp.max(scores, axis=0, keepdims=True))
    total = jnp.zeros_like(peak)
    mixed = jnp.zeros((HD, GROUPS * rows), f32)
    for b in range(blocks):
        weights = jnp.exp(score_ref[b * rows : (b + 1) * rows, :] - peak)
        total = total + jnp.sum(weights, axis=0, keepdims=True)
        mixed = mixed + dot_tn(kv_refs[b][:, HD:], weights.astype(bf16))
    lse_ref[0] = peak + jnp.log(total)
    mixed = jnp.transpose(mixed / total)
    for r in range(GROUPS):
        out_ref[:, r * HD : (r + 1) * HD] = mixed[r * rows : (r + 1) * rows].astype(bf16)


def attend(pos, spans, queries, kv_blocks, after=()):
    rows = queries.shape[0]
    blocks = len(kv_blocks)
    wide = GROUPS * HD
    return pl.pallas_call(
        functools.partial(attend_kernel, blocks, len(after)),
        grid_spec=pltpu.PrefetchScalarGridSpec(
            num_scalar_prefetch=2,
            grid=(KVH,),
            in_specs=[pl.BlockSpec((rows, wide), lambda g, *_: (0, g))]
            + [pl.BlockSpec((rows, 2 * HD), lambda g, *_: (0, g))] * blocks
            + anywhere(len(after)),
            out_specs=[
                pl.BlockSpec((rows, wide), lambda g, *_: (0, g)),
                pl.BlockSpec((1, 1, GROUPS * rows), lambda g, *_: (g, 0, 0)),
            ],
            scratch_shapes=[pltpu.VMEM((blocks * rows, GROUPS * rows), f32)],
        ),
        out_shape=[
            jax.ShapeDtypeStruct((rows, H * HD), bf16),
            jax.ShapeDtypeStruct((KVH, 1, GROUPS * rows), f32),
        ],
        compiler_params=params(),
        cost_estimate=cost(8 * rows * rows * blocks * H * HD, 4 * 2**20),
    )(pos, spans, queries, *kv_blocks, *after)


def attend_back_kernel(blocks, extra, pos, spans, q_ref, grad_ref, lse_ref, *refs):
    kv_refs = refs[:blocks]
    dq_ref, same_ref, other_ref = refs[blocks + extra : -2]
    prob_ref, slope_ref = refs[-2:]
    rows = q_ref.shape[0]
    queries = stack_heads(q_ref)
    grads = stack_heads(grad_ref)
    wanted = places(pos, spans, None, (1, GROUPS * rows), 1, rows)
    lse = lse_ref[0]
    delta = jnp.zeros((1, GROUPS * rows), f32)
    for b in range(blocks):
        part = slice(b * rows, (b + 1) * rows)
        scores = dot_nt(kv_refs[b][:, :HD], queries) * SCALE - lse
        visible = places(pos, spans, b, (rows, 1), 0, rows) <= wanted
        prob = jnp.exp(jnp.where(visible, scores, NEGATIVE))
        slope = dot_nt(kv_refs[b][:, HD:], grads)
        delta = delta + jnp.sum(prob * slope, axis=0, keepdims=True)
        prob_ref[part, :] = prob
        slope_ref[part, :] = slope
        dkv_ref = other_ref if b % 2 else same_ref
        dkv_ref[rows * (b // 2) : rows * (b // 2 + 1), HD:] = dot(prob.astype(bf16), grads).astype(bf16)
    query_grad = jnp.zeros((HD, GROUPS * rows), f32)
    for b in range(blocks):
        part = slice(b * rows, (b + 1) * rows)
        dscore = (prob_ref[part, :] * (slope_ref[part, :] - delta) * SCALE).astype(bf16)
        dkv_ref = other_ref if b % 2 else same_ref
        dkv_ref[rows * (b // 2) : rows * (b // 2 + 1), :HD] = dot(dscore, queries).astype(bf16)
        query_grad = query_grad + dot_tn(kv_refs[b][:, :HD], dscore)
    query_grad = jnp.transpose(query_grad)
    for r in range(GROUPS):
        dq_ref[:, r * HD : (r + 1) * HD] = query_grad[r * rows : (r + 1) * rows].astype(bf16)


def attend_back(pos, spans, queries, grads, lse, kv_blocks, after=()):
    rows = queries.shape[0]
    blocks = len(kv_blocks)
    wide = GROUPS * HD
    by_group = pl.BlockSpec((rows, wide), lambda g, *_: (0, g))
    kv_spec = pl.BlockSpec((rows, 2 * HD), lambda g, *_: (0, g))
    return pl.pallas_call(
        functools.partial(attend_back_kernel, blocks, len(after)),
        grid_spec=pltpu.PrefetchScalarGridSpec(
            num_scalar_prefetch=2,
            grid=(KVH,),
            in_specs=[
                by_group,
                by_group,
                pl.BlockSpec((1, 1, GROUPS * rows), lambda g, *_: (g, 0, 0)),
            ]
            + [kv_spec] * blocks
            + anywhere(len(after)),
            out_specs=[by_group]
            + [pl.BlockSpec((blocks // 2 * rows, 2 * HD), lambda g, *_: (0, g))] * 2,
            scratch_shapes=[pltpu.VMEM((blocks * rows, GROUPS * rows), f32)] * 2,
        ),
        out_shape=[jax.ShapeDtypeStruct((rows, H * HD), bf16)]
        + [jax.ShapeDtypeStruct((blocks // 2 * rows, 2 * KVH * HD), bf16)] * 2,
        compiler_params=params(),
        cost_estimate=cost(20 * rows * rows * blocks * H * HD, 8 * 2**20),
    )(pos, spans, queries, grads, lse, *kv_blocks, *after)


def middle_kernel(x_ref, att_ref, w_ref, gain_ref, middle_ref, rows_ref):
    step = pl.program_id(0)
    tile = w_ref.shape[1]
    columns = pl.ds(pl.multiple_of(step * tile, tile), tile)
    middle_ref[:, columns] = x_ref[...].astype(f32) + dot(att_ref[...], w_ref[...])

    @pl.when(step == pl.num_programs(0) - 1)
    def _():
        middle = middle_ref[...]
        factor = lax.rsqrt(jnp.mean(middle * middle, axis=-1, keepdims=True) + EPSILON)
        rows_ref[...] = (middle * factor * gain_ref[...]).astype(bf16)


def middle_forward(x, attended, w_out, gain, tile=512):
    rows, width = x.shape
    return pl.pallas_call(
        middle_kernel,
        grid=(width // tile,),
        in_specs=[
            pl.BlockSpec((rows, tile), lambda n: (0, n)),
            whole(attended.shape),
            pl.BlockSpec((w_out.shape[0], tile), lambda n: (0, n)),
            whole((1, width)),
        ],
        out_specs=[whole((rows, width))] * 2,
        out_shape=[
            jax.ShapeDtypeStruct((rows, width), f32),
            jax.ShapeDtypeStruct((rows, width), bf16),
        ],
        compiler_params=params(),
        cost_estimate=cost(2 * rows * width * width, 8 * 2**20),
    )(x, attended, w_out, gain.reshape(1, width))


def middle_back_kernel(parts, *refs):
    grad_refs = refs[:parts]
    middle_ref, cot_ref, gain_ref, w_ref = refs[parts : parts + 4]
    mgrad_ref, low_ref, dgain_ref, out_ref = refs[-4:]

    @pl.when(pl.program_id(0) == 0)
    def _():
        upstream = grad_refs[0][...].astype(f32)
        for ref in grad_refs[1:]:
            upstream = upstream + ref[...].astype(f32)
        middle = middle_ref[...]
        factor = lax.rsqrt(jnp.mean(middle * middle, axis=-1, keepdims=True) + EPSILON)
        scaled = upstream * gain_ref[...]
        inner = jnp.mean(scaled * middle, axis=-1, keepdims=True)
        grad = factor * scaled - middle * (factor * factor * factor * inner)
        grad = cot_ref[...].astype(f32) + grad
        mgrad_ref[...] = grad
        low_ref[...] = grad.astype(bf16)
        dgain_ref[...] = jnp.sum(upstream * middle * factor, axis=0, keepdims=True)

    out_ref[...] = dot_nt(low_ref[...], w_ref[...]).astype(bf16)


def middle_back(grads, middle, cotangent, gain, w_out, after=(), tile=512):
    rows, width = middle.shape
    inner = w_out.shape[0]
    return pl.pallas_call(
        functools.partial(middle_back_kernel, len(grads)),
        grid=(inner // tile,),
        in_specs=[whole((rows, width))] * (len(grads) + 2)
        + [whole((1, width)), pl.BlockSpec((tile, width), lambda n: (n, 0))]
        + anywhere(len(after)),
        out_specs=[
            whole((rows, width)),
            whole((rows, width)),
            whole((1, width)),
            pl.BlockSpec((rows, tile), lambda n: (0, n)),
        ],
        out_shape=[
            jax.ShapeDtypeStruct((rows, width), f32),
            jax.ShapeDtypeStruct((rows, width), bf16),
            jax.ShapeDtypeStruct((1, width), f32),
            jax.ShapeDtypeStruct((rows, inner), bf16),
        ],
        compiler_params=params(),
        cost_estimate=cost(2 * rows * width * inner, 16 * 2**20),
    )(*grads, middle, cotangent, gain.reshape(1, width), w_out, *after)


def input_back_kernel(dq_ref, dkv_ref, wq_ref, wk_ref, wv_ref, x_ref, gain_ref, mgrad_ref, *refs):
    out_ref, dgain_ref = refs[-2:]
    step = pl.program_id(0)
    term = dot_nt(dq_ref[...], wq_ref[...])
    term = term + dot_nt(dkv_ref[:, :HD], wk_ref[...]) + dot_nt(dkv_ref[:, HD:], wv_ref[...])

    @pl.when(step == 0)
    def _():
        out_ref[...] = term

    @pl.when(step > 0)
    def _():
        out_ref[...] += term

    @pl.when(step == pl.num_programs(0) - 1)
    def _():
        upstream = out_ref[...]
        x = x_ref[...].astype(f32)
        factor = lax.rsqrt(jnp.mean(x * x, axis=-1, keepdims=True) + EPSILON)
        scaled = upstream * gain_ref[...]
        inner = jnp.mean(scaled * x, axis=-1, keepdims=True)
        out_ref[...] = mgrad_ref[...] + factor * scaled - x * (factor * factor * factor * inner)
        dgain_ref[...] = jnp.sum(upstream * x * factor, axis=0, keepdims=True)


def input_back(dq, dkv, wq, wk, wv, x, gain, mgrad, after=()):
    rows, width = x.shape
    wide = GROUPS * HD
    return pl.pallas_call(
        input_back_kernel,
        grid=(KVH,),
        in_specs=[
            pl.BlockSpec((rows, wide), lambda g: (0, g)),
            pl.BlockSpec((rows, 2 * HD), lambda g: (0, g)),
            pl.BlockSpec((width, wide), lambda g: (0, g)),
            pl.BlockSpec((width, HD), lambda g: (0, g)),
            pl.BlockSpec((width, HD), lambda g: (0, g)),
            whole((rows, width)),
            whole((1, width)),
            whole((rows, width)),
        ]
        + anywhere(len(after)),
        out_specs=[whole((rows, width)), whole((1, width))],
        out_shape=[
            jax.ShapeDtypeStruct((rows, width), f32),
            jax.ShapeDtypeStruct((1, width), f32),
        ],
        compiler_params=params(),
        cost_estimate=cost(2 * rows * width * (H + 2 * KVH) * HD, 14 * 2**20),
    )(dq, dkv, wq, wk, wv, x, gain.reshape(1, width), mgrad, *after)


def gate_column(expert, gates):
    lanes = lax.broadcasted_iota(jnp.int32, gates.shape, 1)
    chosen = (lanes == expert) | (lanes == expert + LOW_LANE)
    return jnp.sum(jnp.where(chosen, gates.astype(f32), 0.0), axis=1, keepdims=True)


def experts_kernel(count, per, gated, extra, pos, *refs):
    x_refs, c_refs, weights = refs[:count], refs[count : 2 * count], refs[2 * count : 2 * count + 3]
    *outs, acc_o, acc_g = refs[2 * count + 3 + extra :]
    out_refs, grad_refs, kept_refs = outs[:count], outs[count : 2 * count], outs[2 * count :]
    wg_ref, wu_ref, wd_ref = weights
    hid_ref, dgu_ref = kept_refs[-2:]
    step = pl.program_id(0)
    last = pl.num_programs(0) - 1
    rows, width = x_refs[0].shape
    chunk = wg_ref.shape[1]
    parts = [slice(b * rows, (b + 1) * rows) for b in range(count)]
    if gated:

        @pl.when(step == 0)
        def _():
            for part, x_ref, c_ref in zip(parts, x_refs, c_refs):
                kept_refs[0][part, :] = x_ref[...]
                kept_refs[1][part, :] = c_ref[...]
                kept_refs[2][:, part] = jnp.transpose(x_ref[...])
                kept_refs[3][:, part] = jnp.transpose(c_ref[:, :width])

    for part, x_ref, c_ref in zip(parts, x_refs, c_refs):
        x = x_ref[...]
        gate = dot(x, wg_ref[...])
        up = dot(x, wu_ref[...])
        slope = dot_nt(c_ref[:, :width], wd_ref[...])
        sigmoid = 1.0 / (1.0 + jnp.exp(-gate))
        act = gate * sigmoid
        hidden = act * up
        if gated:
            held = pl.num_programs(0) // per
            expert = (2 * pos[2] + pos[3]) * held + step // per
            weight = gate_column(expert, c_ref[:, width:])
            hidden = hidden * weight
            slope = slope * weight
        hidden = hidden.astype(bf16)
        dg = (slope * up * (sigmoid * (1.0 + gate * (1.0 - sigmoid)))).astype(bf16)
        du = (slope * act).astype(bf16)
        hid_ref[part, :] = hidden
        dgu_ref[part, :chunk] = dg
        dgu_ref[part, chunk:] = du
        out_term = dot(hidden, wd_ref[...])
        grad_term = dot_nt(dg, wg_ref[...]) + dot_nt(du, wu_ref[...])

        @pl.when(step == 0)
        def _():
            acc_o[part, :] = out_term
            acc_g[part, :] = grad_term

        @pl.when(step > 0)
        def _():
            acc_o[part, :] += out_term
            acc_g[part, :] += grad_term

    @pl.when(step == last)
    def _():
        for part, out_ref, grad_ref in zip(parts, out_refs, grad_refs):
            out_ref[...] = acc_o[part, :].astype(out_ref.dtype)
            grad_ref[...] = acc_g[part, :].astype(grad_ref.dtype)


def experts(pos, xs, cs, weights, part, parts, kept, gated, kind, chunk=256):
    count = len(xs)
    rows, width = xs[0].shape
    taken = count * rows
    inner = weights[2].shape[1]
    per = inner // chunk
    steps = weights[0].shape[0] * per
    specs = [
        pl.BlockSpec((None, width, chunk), lambda i, _: (i // per, 0, i % per)),
        pl.BlockSpec((None, width, chunk), lambda i, _: (i // per, 0, i % per)),
        pl.BlockSpec((None, chunk, width), lambda i, _: (i // per, i % per, 0)),
    ]
    all_rows = parts * taken
    collected = [
        jax.ShapeDtypeStruct((all_rows, steps * chunk), bf16),
        jax.ShapeDtypeStruct((all_rows, 2 * steps * chunk), bf16),
    ]
    collected_specs = [
        pl.BlockSpec((taken, chunk), lambda i, _: (part, i)),
        pl.BlockSpec((taken, 2 * chunk), lambda i, _: (part, i)),
    ]
    if gated:
        collected = [
            jax.ShapeDtypeStruct((all_rows, width), bf16),
            jax.ShapeDtypeStruct((all_rows, cs[0].shape[1]), bf16),
            jax.ShapeDtypeStruct((width, all_rows), bf16),
            jax.ShapeDtypeStruct((width, all_rows), bf16),
        ] + collected
        collected_specs = [
            pl.BlockSpec((taken, width), lambda i, _: (part, 0)),
            pl.BlockSpec((taken, cs[0].shape[1]), lambda i, _: (part, 0)),
            pl.BlockSpec((width, taken), lambda i, _: (0, part)),
            pl.BlockSpec((width, taken), lambda i, _: (0, part)),
        ] + collected_specs
    operands = [pos, *xs, *cs, *weights]
    aliases = {}
    if kept is not None:
        aliases = {len(operands) + j: 2 * count + j for j in range(len(collected))}
        operands += list(kept)
    extra = 0 if kept is None else len(collected)
    result = pl.pallas_call(
        functools.partial(experts_kernel, count, per, gated, extra),
        grid_spec=pltpu.PrefetchScalarGridSpec(
            num_scalar_prefetch=1,
            grid=(steps,),
            in_specs=[whole((rows, width))] * count + [whole(cs[0].shape)] * count + specs + anywhere(extra),
            out_specs=[whole((rows, width))] * (2 * count) + collected_specs,
            scratch_shapes=[pltpu.VMEM((taken, width), f32)] * 2,
        ),
        out_shape=[jax.ShapeDtypeStruct((rows, width), kind)] * (2 * count) + collected,
        input_output_aliases=aliases,
        compiler_params=params(),
        cost_estimate=cost(26 * taken * width * steps * chunk, 12 * 2**20),
    )(*operands)
    return result[:count], result[count : 2 * count], result[2 * count :]


def others_kernel(sets, per, bands, extra, pos, x_ref, c_ref, *refs):
    each = bands + per
    weights = [refs[t * each : (t + 1) * each] for t in range(sets)]
    *result_refs, hid_ref, dgu_ref = refs[sets * each + extra :]
    out_refs, grad_refs = result_refs[: len(result_refs) // 2], result_refs[len(result_refs) // 2 :]
    step = pl.program_id(0)
    width = x_ref.shape[1]
    band = width // bands
    chunk = weights[0][bands].shape[0]
    rows = out_refs[0].shape[0]

    def places(t, n):
        at = (lax.rem(pos[1] + t, 2) * per + n) * chunk
        cut = lambda first: pl.ds(pl.multiple_of(first, chunk), chunk)
        return cut(at), cut(2 * at), cut(2 * at + chunk)

    def columns(n):
        return slice(n * chunk, (n + 1) * chunk), slice((per + n) * chunk, (per + n + 1) * chunk)

    def hidden_chunk(t, n):
        at_hidden, at_gate, at_up = places(t, n)
        gate_cut, up_cut = columns(n)
        expert = (2 * pos[2] + 1 - pos[3]) * sets + lax.rem(pos[1] + t, 2)
        gate = up = 0.0
        for k in range(bands):
            part = x_ref[:, k * band : (k + 1) * band]
            gate = gate + dot(part, weights[t][k][:, gate_cut])
            up = up + dot(part, weights[t][k][:, up_cut])
        slope = dot_nt(c_ref[:, :width], weights[t][bands + n][...])
        sigmoid = 1.0 / (1.0 + jnp.exp(-gate))
        act = gate * sigmoid
        weight = gate_column(expert, c_ref[:, width:])
        slope = slope * weight
        hid_ref[:, at_hidden] = (act * up * weight).astype(bf16)
        dgu_ref[:, at_gate] = (slope * up * (sigmoid * (1.0 + gate * (1.0 - sigmoid)))).astype(bf16)
        dgu_ref[:, at_up] = (slope * act).astype(bf16)

    def results(k):
        out = grad = 0.0
        for t in range(sets):
            for n in range(per):
                at_hidden, at_gate, at_up = places(t, n)
                gate_cut, up_cut = columns(n)
                down = weights[t][bands + n][:, k * band : (k + 1) * band]
                out = out + dot(hid_ref[:, at_hidden], down)
                grad = grad + dot_nt(dgu_ref[:, at_gate], weights[t][k][:, gate_cut])
                grad = grad + dot_nt(dgu_ref[:, at_up], weights[t][k][:, up_cut])
        for p in range(len(out_refs)):
            out_refs[p][...] = out[p * rows : (p + 1) * rows].astype(bf16)
            grad_refs[p][...] = grad[p * rows : (p + 1) * rows].astype(bf16)

    for t in range(sets):
        for n in range(per):
            pl.when(step == t * per + n)(functools.partial(hidden_chunk, t, n))
    for k in range(bands):
        pl.when(step == sets * per + k)(functools.partial(results, k))


def others(pos, x, c, weights, part, parts, count, kept):
    taken, width = x.shape[0] // parts, x.shape[1]
    sets = len(weights)
    bands, downs = weights[0]
    per = len(downs)
    inner = per * downs[0].shape[0]
    flat = [v for bands_t, downs_t in weights for v in [*bands_t, *downs_t]]
    tile = width // len(bands)
    rows_spec = lambda v: pl.BlockSpec(
        (taken, v.shape[1]), lambda *_: (part, 0), pipeline_mode=pl.Buffered(1)
    )
    resident = lambda v: pl.BlockSpec(v.shape, lambda *_: (0, 0), pipeline_mode=pl.Buffered(1))
    late = lambda i: jnp.maximum(i - sets * per, 0)
    operands = [pos, x, c] + flat
    extra = 0 if kept is None else 2
    aliases = {len(operands) + j: 2 * count + j for j in range(extra)}
    collected = [sets * inner, 2 * sets * inner]
    result = pl.pallas_call(
        functools.partial(others_kernel, sets, per, len(bands), extra),
        grid_spec=pltpu.PrefetchScalarGridSpec(
            num_scalar_prefetch=1,
            grid=(sets * per + len(bands),),
            in_specs=[rows_spec(x), rows_spec(c)] + [resident(v) for v in flat] + anywhere(extra),
            out_specs=[pl.BlockSpec((taken // count, tile), lambda i, _: (0, late(i)))] * (2 * count)
            + [pl.BlockSpec((taken, n), lambda *_: (part, 0)) for n in collected],
        ),
        out_shape=[jax.ShapeDtypeStruct((taken // count, width), bf16)] * (2 * count)
        + [jax.ShapeDtypeStruct((parts * taken, n), bf16) for n in collected],
        input_output_aliases=aliases,
        compiler_params=params(),
        cost_estimate=cost(26 * taken * width * sets * inner, 12 * 2**20),
    )(*operands, *(kept or []))
    return result[:count], result[count : 2 * count], result[2 * count :]


def side_of(outer, s, pos):
    return 2 * lax.rem(s, outer) + lax.rem(pos[1] + 1 - s // outer, 2)


def halves_kernel(shape, outer, pos, *refs):
    sent_ref, kept_ref = refs[-2:]

    def write(out_ref):
        first = 0
        for i, rows in enumerate(shape):
            total = dot_tn(refs[2 * i][...], refs[2 * i + 1][...]).astype(bf16)
            blank = out_ref.shape[2] - total.shape[1]
            if blank:
                out_ref[:, first : first + rows, total.shape[1] :] = jnp.zeros(
                    (out_ref.shape[0], rows, blank), bf16
                )
            for e in range(out_ref.shape[0]):
                part = total[e * rows : (e + 1) * rows]
                out_ref[e, first : first + rows, : total.shape[1]] = part
            first += rows

    pl.when(pl.program_id(0) < outer)(lambda: write(sent_ref))
    pl.when(pl.program_id(0) >= outer)(lambda: write(kept_ref))


def halves(pos, pairs, after=()):
    n_ctx, n_exp = lax.axis_size("ctx"), lax.axis_size("exp")
    outer = n_ctx // 2
    shape = [left.shape[1] // (n_ctx * n_exp) for left, _ in pairs]
    wide = max(right.shape[1] for _, right in pairs)
    full = (outer * n_exp, sum(shape), wide)
    if any((left.shape[1] // n_ctx) % 128 for left, _ in pairs):
        out = []
        for side in (1, 0):
            parts = []
            for left, right in pairs:
                split = left.reshape(left.shape[0], outer, 2, -1)
                mine = lax.dynamic_index_in_dim(split, (pos[1] + side) % 2, 2, keepdims=False)
                total = dot_tn(mine.reshape(left.shape[0], -1), right).astype(bf16)
                total = total.reshape(outer * n_exp, -1, right.shape[1])
                parts.append(jnp.pad(total, ((0, 0), (0, 0), (0, wide - right.shape[1]))))
            joined = jnp.concatenate(parts, axis=1)
            out.append(jnp.pad(joined, ((0, 0), (0, -joined.shape[1] % 16), (0, 0))))
        return out
    in_specs, operands = [], []
    for left, right in pairs:
        columns = left.shape[1] // n_ctx
        in_specs.append(
            pl.BlockSpec((left.shape[0], columns), lambda s, pos: (0, side_of(outer, s, pos)))
        )
        in_specs.append(whole(right.shape))
        operands += [left, right]
    block = (n_exp,) + full[1:]
    flops = sum(2 * left.size * right.shape[1] for left, right in pairs)
    return pl.pallas_call(
        functools.partial(halves_kernel, shape, outer),
        grid_spec=pltpu.PrefetchScalarGridSpec(
            num_scalar_prefetch=1,
            grid=(2 * outer,),
            in_specs=in_specs + anywhere(len(after)),
            out_specs=[
                pl.BlockSpec(block, lambda s, pos: (jnp.minimum(s, outer - 1), 0, 0)),
                pl.BlockSpec(block, lambda s, pos: (jnp.maximum(s - outer, 0), 0, 0)),
            ],
        ),
        out_shape=[jax.ShapeDtypeStruct(full, bf16)] * 2,
        compiler_params=params(),
        cost_estimate=cost(2 * flops, 8 * 2**20),
    )(pos, *operands, *after)


def rows_product_kernel(blocks, pos, *refs):
    total = dot_tn(refs[0][...], refs[blocks][...])
    for b in range(1, blocks):
        total = total + dot_tn(refs[b][...], refs[blocks + b][...])
    refs[-1][...] = total.astype(bf16)


def rows_product(pos, lefts, rights, tile=512):
    n_ctx, n_exp = lax.axis_size("ctx"), lax.axis_size("exp")
    depth, height = lefts[0][0].shape
    high, wide = height // n_ctx, rights[0][0].shape[1]
    if high % 128:
        place = lax.axis_index("ctx") * high
        cut = lambda v: lax.slice_in_dim(v[0], v[1] * depth, (v[1] + 1) * depth, axis=0)
        total = sum(
            dot_tn(lax.dynamic_slice_in_dim(cut(a), place, high, 1), cut(b))
            for a, b in zip(lefts, rights)
        )
        return total.astype(bf16).reshape(n_exp, -1, wide)
    blocks = len(lefts)
    left_specs = [
        pl.BlockSpec((depth, high), functools.partial(lambda k, n, pos: (k, 2 * pos[0] + pos[1]), k))
        for _, k in lefts
    ]
    right_specs = [
        pl.BlockSpec((depth, tile), functools.partial(lambda k, n, pos: (k, n), k)) for _, k in rights
    ]
    total = pl.pallas_call(
        functools.partial(rows_product_kernel, blocks),
        grid_spec=pltpu.PrefetchScalarGridSpec(
            num_scalar_prefetch=1,
            grid=(wide // tile,),
            in_specs=left_specs + right_specs,
            out_specs=pl.BlockSpec((high, tile), lambda n, pos: (0, n)),
        ),
        out_shape=jax.ShapeDtypeStruct((high, wide), bf16),
        compiler_params=params(),
        cost_estimate=cost(4 * blocks * depth * high * wide, 4 * 2**20),
    )(pos, *[v for v, _ in lefts], *[v for v, _ in rights])
    return total.reshape(n_exp, -1, wide)


def expert_halves_kernel(blocks, tiles, pos, *refs):
    rows_refs, cot_refs = refs[:blocks], refs[blocks : 2 * blocks]
    dgu_ref, hid_ref, sent_ref, kept_ref = refs[2 * blocks :]
    n = pl.program_id(0)
    high = sent_ref.shape[1]

    def write(left_refs, right_ref):
        left = jnp.concatenate([ref[...] for ref in left_refs], axis=0)
        total = dot(left, right_ref[...]).astype(bf16)
        count = sent_ref.shape[0]
        for i in range(count):
            sent_ref[i] = total[i * high : (i + 1) * high]
            kept_ref[i] = total[(count + i) * high : (count + i + 1) * high]

    pl.when(n < tiles)(lambda: write(rows_refs, dgu_ref))
    pl.when(n >= tiles)(lambda: write(cot_refs, hid_ref))


def expert_steps(width):
    high = width // lax.axis_size("ctx")
    return high // 128 if high % 128 == 0 else 1


def expert_halves(pos, rows_t, cot_t, dgu, hid, tile=512):
    n_ctx = lax.axis_size("ctx")
    width, depth = rows_t.shape
    high = width // n_ctx
    wide = dgu.shape[1] + hid.shape[1]
    steps = expert_steps(width)
    tiles, down = dgu.shape[1] // tile, hid.shape[1] // tile
    left_specs = [
        pl.BlockSpec((high, depth), functools.partial(lambda s, n, pos: (side_of(n_ctx // 2, s, pos), 0), s))
        for s in range(n_ctx)
    ]
    block = (n_ctx // 2 * steps, high // steps, tile)
    return pl.pallas_call(
        functools.partial(expert_halves_kernel, n_ctx, tiles),
        grid_spec=pltpu.PrefetchScalarGridSpec(
            num_scalar_prefetch=1,
            grid=(tiles + down,),
            in_specs=left_specs * 2
            + [
                pl.BlockSpec((depth, tile), lambda n, pos: (0, jnp.minimum(n, tiles - 1))),
                pl.BlockSpec((depth, tile), lambda n, pos: (0, jnp.maximum(n - tiles, 0))),
            ],
            out_specs=[pl.BlockSpec(block, lambda n, pos: (0, 0, n))] * 2,
        ),
        out_shape=[jax.ShapeDtypeStruct(block[:2] + (wide,), bf16)] * 2,
        compiler_params=params(),
        cost_estimate=cost(4 * depth * width * wide, 16 * 2**20),
    )(pos, *[rows_t] * n_ctx, *[cot_t] * n_ctx, dgu, hid)


def sums_kernel(shape, only, extra, pos, *refs):
    ins, outs = refs[: sum(shape)], refs[sum(shape) + extra :]
    at = 0
    for count, out in zip(shape, outs):
        total = ins[at][...].astype(f32)
        for k in range(at + 1, at + count):
            term = ins[k][...].astype(f32)
            if only[k] is not None:
                term = jnp.where(pl.program_id(0) == only[k], term, 0.0)
            total = total + term
        out[...] = total.astype(out.dtype)
        at += count


def sums(pos, steps, outputs, after=()):
    operands, in_specs, out_specs, out_shape, only = [], [], [], [], []
    for kind, block, terms in outputs:
        for array, index, *step in terms:
            operands.append(array)
            only.append(step[0] if step else None)
            in_specs.append(pl.BlockSpec(block, functools.partial(place_of, index)))
        out_specs.append(pl.BlockSpec(block, lambda i, pos: (i, 0, 0)))
        out_shape.append(jax.ShapeDtypeStruct((steps * block[0],) + tuple(block[1:]), kind))
    return pl.pallas_call(
        functools.partial(sums_kernel, [len(terms) for _, _, terms in outputs], only, len(after)),
        grid_spec=pltpu.PrefetchScalarGridSpec(
            num_scalar_prefetch=1,
            grid=(steps,),
            in_specs=in_specs + anywhere(len(after)),
            out_specs=out_specs,
        ),
        out_shape=out_shape,
        compiler_params=params(),
        cost_estimate=cost(0, 8 * 2**20),
    )(pos, *operands, *after)


def place_of(index, i, pos):
    at = index(i, pos)
    return at if isinstance(at, tuple) else (at, 0, 0)


def straight(i, pos):
    return i


def row_sum(terms, kind=bf16):
    total = terms[0].astype(f32)
    for term in terms[1:]:
        total = total + term.astype(f32)
    return total.astype(kind)


def expert_out_kernel(gates, each, *refs):
    in_refs, (gate_ref, up_ref, down_ref) = refs[:4], refs[4:]
    n = pl.program_id(0)

    def write(ref):
        @pl.when((n < gates) & (lax.rem(n, 2) == 0))
        def _():
            gate_ref[0] = ref[...].astype(f32)

        @pl.when((n < gates) & (lax.rem(n, 2) == 1))
        def _():
            up_ref[0] = ref[...].astype(f32)

        @pl.when(n >= gates)
        def _():
            down_ref[0] = jnp.transpose(ref[...].astype(f32))

    for q in range(4):
        pl.when(n // each == q)(functools.partial(write, in_refs[q]))


def expert_out(quarters, inner, chunk=256):
    rows, wide = quarters[0].shape
    each = wide // chunk
    held = 4 * wide // (3 * inner)
    per = inner // chunk
    gates = 2 * held * per
    tile = lambda n: jnp.minimum(n, gates - 1) // 2
    spec = pl.BlockSpec((1, rows, chunk), lambda n: (tile(n) // per, 0, lax.rem(tile(n), per)))
    at = lambda n: jnp.maximum(n - gates, 0)
    return pl.pallas_call(
        functools.partial(expert_out_kernel, gates, each),
        grid=(4 * each,),
        in_specs=[
            pl.BlockSpec(
                (rows, chunk),
                functools.partial(lambda q, n: (0, jnp.clip(n - q * each, 0, each - 1)), q),
            )
            for q in range(4)
        ],
        out_specs=[
            spec,
            spec,
            pl.BlockSpec((1, chunk, rows), lambda n: (at(n) // per, lax.rem(at(n), per), 0)),
        ],
        out_shape=[jax.ShapeDtypeStruct((held, rows, inner), f32)] * 2
        + [jax.ShapeDtypeStruct((held, inner, rows), f32)],
        compiler_params=params(),
        cost_estimate=cost(0, 8 * 2**20),
    )(*quarters)


def last_sum(refs):
    total = refs[0][...].astype(f32)
    for ref in refs[1:]:
        total = total + ref[...].astype(f32)
    return total


def dense_out_kernel(count, *refs):
    total = last_sum(refs[:count])
    out_ref, query_ref, key_ref, value_ref = refs[count:]
    wide = out_ref.shape[1]
    out_ref[...] = total[:, :wide]
    query_ref[...] = total[:, wide : 2 * wide]
    for g in range(KVH):
        first = 2 * wide + 2 * g * HD
        key_ref[:, g * HD : (g + 1) * HD] = total[:, first : first + HD]
        value_ref[:, g * HD : (g + 1) * HD] = total[:, first + HD : first + 2 * HD]


def dense_out(terms, wide):
    rows = terms[0].shape[0]
    shapes = [wide, wide, KVH * HD, KVH * HD]
    return pl.pallas_call(
        functools.partial(dense_out_kernel, len(terms)),
        out_shape=[jax.ShapeDtypeStruct((rows, n), f32) for n in shapes],
        compiler_params=params(),
        cost_estimate=cost(0, 2**20),
    )(*terms)


def shared_out_kernel(count, chunk, *refs):
    total = last_sum(refs[:count])
    gate_ref, up_ref, down_ref = refs[count:]
    rows = gate_ref.shape[0]
    for n in range(gate_ref.shape[1] // chunk):
        cut = slice(n * chunk, (n + 1) * chunk)
        gate_ref[:, cut] = total[:rows, 2 * n * chunk : (2 * n + 1) * chunk]
        up_ref[:, cut] = total[:rows, (2 * n + 1) * chunk : (2 * n + 2) * chunk]
    down_ref[...] = total[rows : rows + down_ref.shape[0], : down_ref.shape[1]]


def shared_grads(terms, gate, down, chunk=256):
    return pl.pallas_call(
        functools.partial(shared_out_kernel, len(terms), chunk),
        out_shape=[jax.ShapeDtypeStruct(v, f32) for v in (gate, gate, down)],
        compiler_params=params(),
        cost_estimate=cost(0, 2**20),
    )(*terms)


def hold(values, after):
    count = len(values)
    return pl.pallas_call(
        lambda *_: None,
        in_specs=[pl.BlockSpec(memory_space=pl.ANY)] * (count + len(after)),
        out_specs=[pl.BlockSpec(memory_space=pl.ANY)] * count,
        out_shape=[jax.ShapeDtypeStruct(v.shape, v.dtype) for v in values],
        input_output_aliases={i: i for i in range(count)},
        compiler_params=params(),
        cost_estimate=cost(0, 0),
    )(*values, *after)


def swap_inner(value, axis):
    size = lax.axis_size(axis)
    return lax.ppermute(value, axis, [(i, i ^ 1) for i in range(size)])


def shift_outer(value, axis, by):
    outer = lax.axis_size(axis) // 2
    perm = [(o * 2 + i, ((o + by) % outer) * 2 + i) for o in range(outer) for i in range(2)]
    return lax.ppermute(value, axis, perm)


def ring_step(value, by):
    n_ctx, n_exp = lax.axis_size("ctx"), lax.axis_size("exp")
    outer = n_exp // 2
    perm = []
    for c in range(n_ctx):
        way = by if c % 2 == 0 else -by
        for o in range(outer):
            for i in range(2):
                perm.append((c * n_exp + o * 2 + i, c * n_exp + ((o + way) % outer) * 2 + i))
    return lax.ppermute(value, BOTH, perm)


def by_blocks(value, together):
    return value.reshape(-1, together * value.shape[1], value.shape[2])


def spread_outer(value):
    moved, out = value, []
    for _ in range(1, lax.axis_size("ctx") // 2):
        moved = shift_outer(moved, "ctx", 1)
        out.append(moved)
    return out, swap_inner(value, "ctx")


def spread_inner(moved):
    return [swap_inner(v, "ctx") for v in moved]


def outer_blocks(value):
    moved, out = value, []
    for _ in range(1, lax.axis_size("ctx") // 2):
        moved = shift_outer(moved, "ctx", 1)
        out.append(moved)
    return out


def inner_blocks(value, moved):
    return swap_inner(jnp.concatenate([value] + moved, axis=0), "ctx")


def all_blocks(value, moved, across):
    out = []
    for k, v in enumerate([value] + moved):
        out += [(v, 0), (across, k)]
    return out


def spread_all(value, moved, across, moved_across):
    blocks = [value, across]
    for a, b in zip(moved, moved_across):
        blocks += [a, b]
    return blocks


def paired_blocks(value, across, moved, moved_across):
    out = [(value, 0), (across, 0)]
    for a, b in zip(moved, moved_across):
        out += [(a, 0), (b, 0)]
    return out


class Shared:
    def __init__(self, pos, kept, got):
        self.pos = pos
        self.outer, self.levels = lax.axis_size("ctx") // 2, lax.axis_size("exp") // 2
        self.rows, self.wide = kept.shape[1:]
        self.pair = lambda v: v.reshape(-1, 2 * self.rows, self.wide)
        self.terms = [self.pair(v) for v in (kept, got)]
        self.together = 2 if self.levels % 2 == 0 else 1
        self.steps = self.levels // self.together

    def _sum(self, d, rows, inner, moved=()):
        at = lambda i, pos: lax.rem(pos[0] + d, self.outer) * self.steps + i
        terms = [(v, lambda i, pos: (at(i, pos), inner(pos), 0)) for v in self.terms]
        for parts in moved:
            for k, v in enumerate(parts):
                terms.append((self.pair(v), lambda i, pos: (0, inner(pos), 0), k))
        return terms, (self.together, rows, self.wide)

    def first(self):
        out = []
        for d in range(1, self.outer):
            terms, block = self._sum(d, 2 * self.rows, lambda pos: 0)
            outputs = []
            for k in range(self.steps):
                part = [(v, functools.partial(lambda f, k, i, pos: f(k, pos), f, k)) for v, f in terms]
                outputs.append((bf16, block, part))
            out.append(sums(self.pos, 1, outputs))
        return out

    def second(self, moved):
        terms, block = self._sum(0, self.rows, lambda pos: 1 - pos[3], moved)
        outputs = []
        for k in range(self.steps):
            part = [(v, functools.partial(lambda f, k, i, pos: f(k, pos), f, k)) for v, f, *o in terms if not o or o[0] == k]
            outputs.append((bf16, block, part))
        return sums(self.pos, 1, outputs)

    def total(self, moved, crossed):
        terms, block = self._sum(0, self.rows, lambda pos: pos[3], moved)
        terms = terms + [(v, lambda i, pos: 0, k) for k, v in enumerate(crossed)]
        return sums(self.pos, self.steps, [(bf16, block, terms)])[0]


def z_take(total, d):
    levels = total.shape[0]
    return lax.dynamic_index_in_dim(total, (lax.axis_index("exp") // 2 + d) % levels, 0, False)


def z_send(total, d):
    return shift_outer(z_take(total, d), "exp", d)


def over_x(total):
    pairs = total.reshape((-1, 2) + total.shape[1:])
    return swap_inner(lax.dynamic_index_in_dim(pairs, 1 - lax.axis_index("exp") % 2, 1, False), "exp")


def mine_x(total):
    pairs = total.reshape((-1, 2) + total.shape[1:])
    return lax.dynamic_index_in_dim(pairs, lax.axis_index("exp") % 2, 1, False)


def over_z(pos, mine, arrived):
    levels, rows, wide = mine.shape
    outputs = []
    for d in range(levels):
        at = functools.partial(lambda d, i, pos: lax.rem(pos[2] + d, levels), d)
        outputs.append((bf16 if d else f32, (1, rows, wide), [(mine, at), (arrived, at)]))
    own, *sent = [v[0] for v in sums(pos, 1, outputs)]
    return [own] + [shift_outer(v, "exp", d + 1) for d, v in enumerate(sent)]


def expert_quarter(kept, got, q, row):
    steps = kept.shape[0] // (lax.axis_size("ctx") // 2)
    block = (steps, kept.shape[1], kept.shape[2] // 4)
    return block, [(v, lambda i, pos: (row(i, pos), 0, q)) for v in (kept, got)]


def expert_pieces(pos, kept, got, quarters):
    outputs = []
    for q in quarters:
        block, terms = expert_quarter(kept, got, q, straight)
        outputs.append((bf16, block, terms))
    return sums(pos, lax.axis_size("ctx") // 2, outputs)


def expert_row(d):
    outer = lax.axis_size("ctx") // 2
    return lambda i, pos: lax.rem(pos[0] + d, outer)


def expert_send(pos, kept, got, pieces, half):
    sent = []
    for d in range(1, lax.axis_size("ctx") // 2):
        row = expert_row(d)
        block, terms = expert_quarter(kept, got, 0, row)
        terms = [(v, lambda i, pos: (row(i, pos), 0, 2 * half + i)) for v, _ in terms]
        terms += [(pieces[2 * half + k], lambda i, pos: row(0, pos), k) for k in range(2)]
        sent += sums(pos, 2, [(bf16, block, terms)])
    return sent


def expert_move(sent):
    return [shift_outer(v, "ctx", d + 1) for d, v in enumerate(sent)]


def expert_total(pos, kept, got, pieces, arrived):
    row = expert_row(0)
    outputs = []
    for q in range(4):
        block, terms = expert_quarter(kept, got, q, row)
        at = functools.partial(lambda k, i, pos: k, q % 2)
        terms = terms + [(pieces[q], row)] + [(v, at) for v in arrived[q // 2]]
        outputs.append((bf16, block, terms))
    return [v.reshape(-1, v.shape[2]) for v in sums(pos, 1, outputs)]


def shards(
    layer_input,
    attn_gain,
    w_query,
    w_key,
    w_value,
    w_out,
    ffn_gain,
    shared_gate,
    shared_up,
    shared_down,
    expert_gate,
    expert_up,
    expert_down,
    routes,
    gate_logits,
    span_order,
    cotangent,
):
    x = layer_input[0]
    cot = cotangent[0]
    tokens, width = x.shape
    span_rows = tokens // 2
    n_ctx, n_exp = lax.axis_size("ctx"), lax.axis_size("exp")
    ctx_id, exp_id = lax.axis_index("ctx"), lax.axis_index("exp")
    local_experts, _, inner = expert_gate.shape
    expert_count = local_experts * n_exp

    levels = n_exp // 2
    pos = jnp.stack([ctx_id // 2, ctx_id % 2, exp_id // 2, exp_id % 2]).astype(jnp.int32)

    always = pos[0] < n_ctx
    ring = n_ctx // 2

    def region(work):
        made = jax.eval_shape(work)
        return lax.cond(always, work, lambda: jax.tree.map(lambda v: jnp.zeros(v.shape, v.dtype), made))

    gate_vals = jax.nn.softmax(gate_logits[0], axis=-1)
    named = routes[0][:, None, :] == jnp.arange(expert_count, dtype=jnp.int32)[None, :, None]
    row_gates = jnp.sum(jnp.where(named, gate_vals[:, None, :], 0.0), axis=-1)
    high = row_gates.astype(bf16)
    low = (row_gates - high.astype(f32)).astype(bf16)
    fill = lambda width: ((0, 0), (0, width - expert_count))
    cot_ring = [
        jnp.concatenate(
            [cot, jnp.pad(high, fill(LOW_LANE)), jnp.pad(low, fill(GATE_LANES - LOW_LANE))], axis=1
        )
    ]

    chunk, bands = 256, 3
    mine = lambda v: lax.dynamic_index_in_dim(v, pos[1], 0, keepdims=False)
    over_core = lambda v: swap_inner(v, "ctx")

    def fetch(k):
        return swap_inner(asked[k], "exp")

    def arranged(parts):
        return parts[inner // chunk :], parts[: inner // chunk]

    def ask():
        down = mine(expert_down)
        out = [down[n * chunk : (n + 1) * chunk] for n in range(inner // chunk)]
        gate, up = mine(expert_gate), mine(expert_up)
        band = width // bands
        for k in range(bands):
            cut = slice(k * band, (k + 1) * band)
            out.append(jnp.concatenate([gate[cut], up[cut]], axis=1))
        return out

    def gather_keys():
        normed, kv = keyvalue(x, attn_gain, w_key, w_value)
        moved, across = spread_outer(kv)
        queries = dot(normed, w_query).astype(bf16)
        asked = ask()
        keys = kv, moved, across, spread_inner(moved)
        return normed, keys, queries, ring_step(cot_ring[0], 1), asked, swap_inner(asked[0], "exp")

    normed, keys, queries, cot_next, asked, got = region(gather_keys)
    kv_blocks = spread_all(*keys)
    cot_ring.append(cot_next)
    fetched, crossed = [got], []

    def attention():
        attended, lse = attend(pos, span_order, queries, kv_blocks)
        middle, rows = middle_forward(x, attended, w_out, ffn_gain)
        moved = outer_blocks(normed), ring_step(cot_ring[1], 1), fetch(1), over_core(fetched[0])
        return attended, lse, middle, rows, over_core(normed), *moved

    attended, lse, middle, rows_low, across, normed_moved, cot_next, got, crossing = region(attention)
    normed_across = across
    cot_ring.append(cot_next)
    fetched.append(got)
    crossed.append(crossing)

    own_weights = (expert_gate, expert_up, expert_down)

    def own_part(ks, rows, part, parts, kept):
        return experts(pos, rows, [cot_ring[k] for k in ks], own_weights, part, parts, kept, True, bf16)

    def first():
        weights = (shared_gate[None], shared_up[None], shared_down[None])
        shared = experts(pos, [rows_low], [cot], weights, 0, 1, None, False, f32)
        more = spread_inner(normed_moved), fetch(2), over_core(fetched[1]), outer_blocks(attended)
        return ring_step(rows_low, 1), shared, *more

    rows_one, shared, across, got, crossing, attended_moved = region(first)
    fetched.append(got)
    crossed.append(crossing)
    normed_blocks = paired_blocks(normed, normed_across, normed_moved, across)
    (shared_out,), (shared_grad,), (shared_hidden, shared_dgu) = shared
    shared_pairs = [(rows_low, shared_dgu), (shared_hidden, cot)]

    def second():
        result = own_part([0], [rows_low], 2, 4, None)
        more = fetch(3), over_core(fetched[2]), [over_core(attended), *spread_inner(attended_moved)]
        return ring_step(rows_one, 1), result, halves(pos, shared_pairs), *more

    rows_two, (out_k, grad_k, kept), (shared_sent, shared_kept), got, crossing, across = region(second)
    attended_blocks = paired_blocks(attended, across[0], attended_moved, across[1:])
    fetched.append(got)
    crossed.append(crossing)
    out_own, grad_own = list(out_k), list(grad_k)

    def third():
        more = over_core(shared_sent), fetch(4), over_core(fetched[3])
        pair = own_part([1, 2], [rows_one, rows_two], 0, 2, kept)
        sent = Shared(pos, shared_kept, more[0]).first()
        return ring_step(rows_two, 1), pair, sent, *more

    rows_k, (out_k, grad_k, kept), shared_sent, shared_got, got, crossing = region(third)
    fetched.append(got)
    crossed.append(crossing)
    out_own += out_k
    grad_own += grad_k

    def over_y(parts, k):
        return [shift_outer(v[k], "ctx", d + 1) for d, v in enumerate(parts)]

    def fourth():
        moved = ring_step(cot_ring[2], 1)
        weights = [arranged(fetched), arranged(crossed + [over_core(fetched[4])])]
        half = levels // 2
        arrived = [over_y(shared_sent, k) for k in range(len(shared_sent[0]))]
        out_a, grad_a, new = others(pos, kept[0], kept[1], weights, 0, 2, half, None)
        last = experts(pos, [rows_k], [moved], own_weights, 3, 4, kept, True, bf16)
        out_b, grad_b, new = others(pos, last[2][0], last[2][1], weights, 1, 2, half, new)
        return last, [out_b[0], *out_a, out_b[1]], [grad_b[0], *grad_a, grad_b[1]], new, arrived

    (out_k, grad_k, kept), out_other, grad_other, kept_other, got = region(fourth)
    shared_moved = [list(v) for v in zip(*got)]
    out_own += out_k
    grad_own += grad_k
    rows_all, cot_all, rows_t, cot_t, hid_own, dgu_own = kept
    hid_other, dgu_other = kept_other

    def back_one():
        moved = ring_step(row_sum([grad_own[3], grad_other[3]]), -1)
        parts = Shared(pos, shared_kept, shared_got).second(shared_moved)
        crossed = [swap_inner(v, "exp") for v in parts[: len(parts) // 2]]
        made = expert_halves(pos, rows_t, cot_t, dgu_other, hid_other)
        return moved, made, crossed, parts[len(parts) // 2 :]

    moved, (sent, kept_other), shared_crossed, shared_rest = region(back_one)

    def back_two():
        total = row_sum([grad_own[2], grad_other[2], moved])
        got = swap_inner(sent, "ctx")
        crossed = [swap_inner(v, "exp") for v in shared_rest]
        made = expert_halves(pos, rows_t, cot_t, dgu_own, hid_own)
        return ring_step(total, -1), got, made, expert_pieces(pos, kept_other, got, [0])[0], crossed

    moved_two, got_other, (sent_own, kept_own), piece, got = region(back_two)
    shared_crossed = shared_crossed + got

    def back_three():
        total = row_sum([grad_own[1], grad_other[1], moved_two])
        made = expert_pieces(pos, kept_other, got_other, [1, 2, 3])
        shared_sum = Shared(pos, shared_kept, shared_got).total(shared_moved, shared_crossed)
        out_total = row_sum([out_own[3], out_other[3]])
        middle_grads = middle_back(
            [shared_grad, grad_own[0], grad_other[0], ring_step(total, -1)],
            middle,
            cot,
            ffn_gain,
            w_out,
        )
        moved = middle_grads, swap_inner(sent_own, "ctx"), swap_inner(piece, "exp")
        shared_z = [z_take(shared_sum, d) for d in range(levels)]
        return *moved, made, shared_z, out_total

    middle_grads, got_own, piece, made, shared_z, out_total = region(back_three)
    mgrad, mgrad_low, ffn_gain_grad, att_grad = middle_grads
    pieces = [piece, *made]

    def attention_back():
        dq, same, across = attend_back(pos, span_order, queries, att_grad, lse, kv_blocks)
        got = ring_step(out_total, -1), swap_inner(pieces[1], "exp"), shift_outer(shared_z[1], "exp", 1)
        mgrad_parts = mgrad_low, over_core(mgrad_low), outer_blocks(mgrad_low)
        return mgrad_parts, dq, same, across, *got

    mgrad_parts, dq, same, across, out_moved, piece, got = region(attention_back)
    pieces[1] = piece
    shared_parts = [shared_z[0], got]

    def dense_one():
        got = over_core(across)
        made = []
        for k in reversed(range(ring)):
            part = slice(k * tokens, (k + 1) * tokens)
            made = row_sum([same[part], got[part]] + made)
            if k:
                made = [shift_outer(made, "ctx", -1)]
        total = row_sum([out_own[2], out_other[2], out_moved])
        mgrad_blocks = paired_blocks(*mgrad_parts, spread_inner(mgrad_parts[2]))
        total_out = rows_product(pos, attended_blocks, mgrad_blocks)
        sent = expert_send(pos, kept_own, got_own, pieces, 0)
        total = row_sum([out_own[1], out_other[1], ring_step(total, -1)])
        return made, outer_blocks(dq), total_out, sent, total, swap_inner(pieces[2], "exp")

    dkv, dq_moved, total_out, sent, out_total_two, piece = region(dense_one)
    pieces[2] = piece

    def dense_two():
        dkv_moved = outer_blocks(dkv)
        dkv_blocks = all_blocks(dkv, dkv_moved, inner_blocks(dkv, dkv_moved))
        dq_blocks = all_blocks(dq, dq_moved, inner_blocks(dq, dq_moved))
        total_query = rows_product(pos, normed_blocks, dq_blocks)
        total_kv = rows_product(pos, normed_blocks, dkv_blocks)
        back = input_back(dq, dkv, w_query, w_key, w_value, x, attn_gain, mgrad)
        moved = ring_step(out_total_two, -1), swap_inner(pieces[3], "exp"), expert_move(sent)
        return total_query, total_kv, back, *moved

    total_query, total_kv, (input_grad, attn_gain_grad), out_moved_three, piece, got = region(dense_two)
    pieces[3] = piece
    arrived = [got]

    def dense_three():
        devices = n_ctx * n_exp
        total = jnp.concatenate([total_out, total_query, total_kv], axis=2)
        got = expert_move(expert_send(pos, kept_own, got_own, pieces, 1))
        layer_out = row_sum([middle, shared_out, out_own[0], out_other[0], out_moved_three])
        more = [shift_outer(shared_z[d], "exp", d) for d in range(2, levels)]
        gains = jnp.stack(
            [attn_gain_grad.reshape(devices, -1), ffn_gain_grad.reshape(devices, -1)], axis=1
        )
        gains = lax.all_to_all(gains, BOTH, split_axis=0, concat_axis=0, tiled=True)
        return mine_x(total), over_x(total), got, layer_out, more, gains

    total, total_x, got, layer_out, more, gains = region(dense_three)
    shared_parts += more
    arrived.append(got)

    def dense_four():
        grads = expert_out(expert_total(pos, kept_own, got_own, pieces, arrived), inner)
        shape = lambda v: (v.shape[0] // (n_ctx * n_exp), v.shape[1])
        shared = shared_grads(
            shared_parts, shape(shared_gate), shape(shared_down)
        )
        dense = dense_out(over_z(pos, total, total_x), x.shape[1])
        return jnp.sum(gains, axis=0), shared, dense, grads

    gains, (sum_gate, sum_up, sum_down), dense, expert_grads = region(dense_four)
    sum_out, sum_query, sum_key, sum_value = dense
    return (
        layer_out[None],
        input_grad[None],
        gains[0],
        sum_query,
        sum_key,
        sum_value,
        sum_out,
        gains[1],
        sum_gate,
        sum_up,
        sum_down,
        *expert_grads,
    )


def solution(mesh):
    return jax.shard_map(
        shards,
        mesh=mesh,
        in_specs=(
            P("exp", "ctx", None),
            P(),
            P(),
            P(),
            P(),
            P(),
            P(),
            P(),
            P(),
            P(),
            P("exp", None, None),
            P("exp", None, None),
            P("exp", None, None),
            P("exp", "ctx", None),
            P("exp", "ctx", None),
            P(),
            P("exp", "ctx", None),
        ),
        out_specs=(
            P("exp", "ctx", None),
            P("exp", "ctx", None),
            P(("ctx", "exp")),
            P(("ctx", "exp"), None),
            P(("ctx", "exp"), None),
            P(("ctx", "exp"), None),
            P(("ctx", "exp"), None),
            P(("ctx", "exp")),
            P(("ctx", "exp"), None),
            P(("ctx", "exp"), None),
            P(("ctx", "exp"), None),
            P("exp", "ctx", None),
            P("exp", "ctx", None),
            P("exp", None, "ctx"),
        ),
        check_vma=False,
    )
```

```python
import functools

import jax
import jax.numpy as jnp
from jax import lax
from jax.experimental import pallas as pl
from jax.experimental.pallas import tpu as pltpu
from jax.sharding import PartitionSpec as P

H = 12
HD = 128
KVH = 4
GROUPS = H // KVH
EPSILON = 1e-06
GATE_LANES = 128
LOW_LANE = 64
NEGATIVE = -1e30
SCALE = HD ** (-0.5)
BOTH = ("ctx", "exp")
VMEM_LIMIT = 60 * 2**20
bf16 = jnp.bfloat16
f32 = jnp.float32


def dot(left_op, right_op):
    return jnp.dot(left_op, right_op, preferred_element_type=f32)


def dot_nt(left_op, right_op):
    return lax.dot_general(left_op, right_op, (((1,), (1,)), ((), ())), preferred_element_type=f32)


def dot_tn(left_op, right_op):
    return lax.dot_general(left_op, right_op, (((0,), (0,)), ((), ())), preferred_element_type=f32)


def whole(shape):
    return pl.BlockSpec(shape, lambda *_: (0,) * len(shape))


def params():
    return pltpu.CompilerParams(vmem_limit_bytes=VMEM_LIMIT)


def anywhere(count):
    return [pl.BlockSpec(memory_space=pl.ANY)] * count


def cost(flops, nbytes):
    return pl.CostEstimate(flops=flops // 4, bytes_accessed=nbytes // 4, transcendentals=0)


def keyvalue_kernel(x_ref, gain_ref, wk_ref, wv_ref, normed_ref, kv_ref):
    @pl.when(pl.program_id(0) == 0)
    def _():
        x = x_ref[...].astype(f32)
        factor = lax.rsqrt(jnp.mean(x * x, axis=-1, keepdims=True) + EPSILON)
        normed_ref[...] = (x * factor * gain_ref[...]).astype(bf16)

    both = jnp.concatenate([wk_ref[...], wv_ref[...]], axis=1)
    kv_ref[...] = dot(normed_ref[...], both).astype(bf16)


def keyvalue(x, gain, wk, wv):
    rows, width = x.shape
    return pl.pallas_call(
        keyvalue_kernel,
        grid=(KVH,),
        in_specs=[
            whole((rows, width)),
            whole((1, width)),
            pl.BlockSpec((width, HD), lambda g: (0, g)),
            pl.BlockSpec((width, HD), lambda g: (0, g)),
        ],
        out_specs=[whole((rows, width)), pl.BlockSpec((rows, 2 * HD), lambda g: (0, g))],
        out_shape=[
            jax.ShapeDtypeStruct((rows, width), bf16),
            jax.ShapeDtypeStruct((rows, 2 * KVH * HD), bf16),
        ],
        compiler_params=params(),
        cost_estimate=cost(4 * rows * width * KVH * HD, 5 * 2**20),
    )(x, gain.reshape(1, width), wk, wv)


def stack_heads(ref):
    return jnp.concatenate([ref[:, r * HD : (r + 1) * HD] for r in range(GROUPS)], axis=0)


def places(pos, spans, block, shape, dim, rows):
    outer, side = (0, 0) if block is None else (block // 2, block % 2)
    ring = spans.shape[0] // 4
    owner = 2 * lax.rem(pos[0] + ring - outer, ring) + lax.rem(pos[1] + side, 2)
    row = lax.broadcasted_iota(jnp.int32, shape, dim) % rows
    half = rows // 2
    first, second = spans[2 * owner] * half, spans[2 * owner + 1] * half
    return jnp.where(row < half, first + row, second + row - half)


def attend_kernel(blocks, extra, pos, spans, q_ref, *refs):
    kv_refs = refs[:blocks]
    out_ref, lse_ref, score_ref = refs[blocks + extra :]
    rows = q_ref.shape[0]
    queries = stack_heads(q_ref)
    wanted = places(pos, spans, None, (1, GROUPS * rows), 1, rows)
    peak = jnp.full((1, GROUPS * rows), NEGATIVE, f32)
    for b in range(blocks):
        scores = dot_nt(kv_refs[b][:, :HD], queries) * SCALE
        visible = places(pos, spans, b, (rows, 1), 0, rows) <= wanted
        scores = jnp.where(visible, scores, NEGATIVE)
        score_ref[b * rows : (b + 1) * rows, :] = scores
        peak = jnp.maximum(peak, jnp.max(scores, axis=0, keepdims=True))
    total = jnp.zeros_like(peak)
    mixed = jnp.zeros((HD, GROUPS * rows), f32)
    for b in range(blocks):
        weights = jnp.exp(score_ref[b * rows : (b + 1) * rows, :] - peak)
        total = total + jnp.sum(weights, axis=0, keepdims=True)
        mixed = mixed + dot_tn(kv_refs[b][:, HD:], weights.astype(bf16))
    lse_ref[0] = peak + jnp.log(total)
    mixed = jnp.transpose(mixed / total)
    for r in range(GROUPS):
        out_ref[:, r * HD : (r + 1) * HD] = mixed[r * rows : (r + 1) * rows].astype(bf16)


def attend(pos, spans, queries, kv_blocks, after=()):
    rows = queries.shape[0]
    blocks = len(kv_blocks)
    wide = GROUPS * HD
    return pl.pallas_call(
        functools.partial(attend_kernel, blocks, len(after)),
        grid_spec=pltpu.PrefetchScalarGridSpec(
            num_scalar_prefetch=2,
            grid=(KVH,),
            in_specs=[pl.BlockSpec((rows, wide), lambda g, *_: (0, g))]
            + [pl.BlockSpec((rows, 2 * HD), lambda g, *_: (0, g))] * blocks
            + anywhere(len(after)),
            out_specs=[
                pl.BlockSpec((rows, wide), lambda g, *_: (0, g)),
                pl.BlockSpec((1, 1, GROUPS * rows), lambda g, *_: (g, 0, 0)),
            ],
            scratch_shapes=[pltpu.VMEM((blocks * rows, GROUPS * rows), f32)],
        ),
        out_shape=[
            jax.ShapeDtypeStruct((rows, H * HD), bf16),
            jax.ShapeDtypeStruct((KVH, 1, GROUPS * rows), f32),
        ],
        compiler_params=params(),
        cost_estimate=cost(8 * rows * rows * blocks * H * HD, 4 * 2**20),
    )(pos, spans, queries, *kv_blocks, *after)


def attend_back_kernel(blocks, extra, pos, spans, q_ref, grad_ref, lse_ref, *refs):
    kv_refs = refs[:blocks]
    dq_ref, same_ref, other_ref = refs[blocks + extra : -2]
    prob_ref, slope_ref = refs[-2:]
    rows = q_ref.shape[0]
    queries = stack_heads(q_ref)
    grads = stack_heads(grad_ref)
    wanted = places(pos, spans, None, (1, GROUPS * rows), 1, rows)
    lse = lse_ref[0]
    delta = jnp.zeros((1, GROUPS * rows), f32)
    for b in range(blocks):
        part = slice(b * rows, (b + 1) * rows)
        scores = dot_nt(kv_refs[b][:, :HD], queries) * SCALE - lse
        visible = places(pos, spans, b, (rows, 1), 0, rows) <= wanted
        prob = jnp.exp(jnp.where(visible, scores, NEGATIVE))
        slope = dot_nt(kv_refs[b][:, HD:], grads)
        delta = delta + jnp.sum(prob * slope, axis=0, keepdims=True)
        prob_ref[part, :] = prob
        slope_ref[part, :] = slope
        dkv_ref = other_ref if b % 2 else same_ref
        dkv_ref[rows * (b // 2) : rows * (b // 2 + 1), HD:] = dot(prob.astype(bf16), grads).astype(bf16)
    query_grad = jnp.zeros((HD, GROUPS * rows), f32)
    for b in range(blocks):
        part = slice(b * rows, (b + 1) * rows)
        dscore = (prob_ref[part, :] * (slope_ref[part, :] - delta) * SCALE).astype(bf16)
        dkv_ref = other_ref if b % 2 else same_ref
        dkv_ref[rows * (b // 2) : rows * (b // 2 + 1), :HD] = dot(dscore, queries).astype(bf16)
        query_grad = query_grad + dot_tn(kv_refs[b][:, :HD], dscore)
    query_grad = jnp.transpose(query_grad)
    for r in range(GROUPS):
        dq_ref[:, r * HD : (r + 1) * HD] = query_grad[r * rows : (r + 1) * rows].astype(bf16)


def attend_back(pos, spans, queries, grads, lse, kv_blocks, after=()):
    rows = queries.shape[0]
    blocks = len(kv_blocks)
    wide = GROUPS * HD
    by_group = pl.BlockSpec((rows, wide), lambda g, *_: (0, g))
    kv_spec = pl.BlockSpec((rows, 2 * HD), lambda g, *_: (0, g))
    return pl.pallas_call(
        functools.partial(attend_back_kernel, blocks, len(after)),
        grid_spec=pltpu.PrefetchScalarGridSpec(
            num_scalar_prefetch=2,
            grid=(KVH,),
            in_specs=[
                by_group,
                by_group,
                pl.BlockSpec((1, 1, GROUPS * rows), lambda g, *_: (g, 0, 0)),
            ]
            + [kv_spec] * blocks
            + anywhere(len(after)),
            out_specs=[by_group]
            + [pl.BlockSpec((blocks // 2 * rows, 2 * HD), lambda g, *_: (0, g))] * 2,
            scratch_shapes=[pltpu.VMEM((blocks * rows, GROUPS * rows), f32)] * 2,
        ),
        out_shape=[jax.ShapeDtypeStruct((rows, H * HD), bf16)]
        + [jax.ShapeDtypeStruct((blocks // 2 * rows, 2 * KVH * HD), bf16)] * 2,
        compiler_params=params(),
        cost_estimate=cost(20 * rows * rows * blocks * H * HD, 8 * 2**20),
    )(pos, spans, queries, grads, lse, *kv_blocks, *after)


def middle_kernel(x_ref, att_ref, w_ref, gain_ref, middle_ref, rows_ref):
    step = pl.program_id(0)
    tile = w_ref.shape[1]
    columns = pl.ds(pl.multiple_of(step * tile, tile), tile)
    middle_ref[:, columns] = x_ref[...].astype(f32) + dot(att_ref[...], w_ref[...])

    @pl.when(step == pl.num_programs(0) - 1)
    def _():
        middle = middle_ref[...]
        factor = lax.rsqrt(jnp.mean(middle * middle, axis=-1, keepdims=True) + EPSILON)
        rows_ref[...] = (middle * factor * gain_ref[...]).astype(bf16)


def middle_forward(x, attended, w_out, gain, tile=512):
    rows, width = x.shape
    return pl.pallas_call(
        middle_kernel,
        grid=(width // tile,),
        in_specs=[
            pl.BlockSpec((rows, tile), lambda n: (0, n)),
            whole(attended.shape),
            pl.BlockSpec((w_out.shape[0], tile), lambda n: (0, n)),
            whole((1, width)),
        ],
        out_specs=[whole((rows, width))] * 2,
        out_shape=[
            jax.ShapeDtypeStruct((rows, width), f32),
            jax.ShapeDtypeStruct((rows, width), bf16),
        ],
        compiler_params=params(),
        cost_estimate=cost(2 * rows * width * width, 8 * 2**20),
    )(x, attended, w_out, gain.reshape(1, width))


def middle_back_kernel(parts, *refs):
    grad_refs = refs[:parts]
    middle_ref, cot_ref, gain_ref, w_ref = refs[parts : parts + 4]
    mgrad_ref, low_ref, dgain_ref, out_ref = refs[-4:]

    @pl.when(pl.program_id(0) == 0)
    def _():
        upstream = grad_refs[0][...].astype(f32)
        for ref in grad_refs[1:]:
            upstream = upstream + ref[...].astype(f32)
        middle = middle_ref[...]
        factor = lax.rsqrt(jnp.mean(middle * middle, axis=-1, keepdims=True) + EPSILON)
        scaled = upstream * gain_ref[...]
        inner = jnp.mean(scaled * middle, axis=-1, keepdims=True)
        grad = factor * scaled - middle * (factor * factor * factor * inner)
        grad = cot_ref[...].astype(f32) + grad
        mgrad_ref[...] = grad
        low_ref[...] = grad.astype(bf16)
        dgain_ref[...] = jnp.sum(upstream * middle * factor, axis=0, keepdims=True)

    out_ref[...] = dot_nt(low_ref[...], w_ref[...]).astype(bf16)


def middle_back(grads, middle, cotangent, gain, w_out, after=(), tile=512):
    rows, width = middle.shape
    inner = w_out.shape[0]
    return pl.pallas_call(
        functools.partial(middle_back_kernel, len(grads)),
        grid=(inner // tile,),
        in_specs=[whole((rows, width))] * (len(grads) + 2)
        + [whole((1, width)), pl.BlockSpec((tile, width), lambda n: (n, 0))]
        + anywhere(len(after)),
        out_specs=[
            whole((rows, width)),
            whole((rows, width)),
            whole((1, width)),
            pl.BlockSpec((rows, tile), lambda n: (0, n)),
        ],
        out_shape=[
            jax.ShapeDtypeStruct((rows, width), f32),
            jax.ShapeDtypeStruct((rows, width), bf16),
            jax.ShapeDtypeStruct((1, width), f32),
            jax.ShapeDtypeStruct((rows, inner), bf16),
        ],
        compiler_params=params(),
        cost_estimate=cost(2 * rows * width * inner, 16 * 2**20),
    )(*grads, middle, cotangent, gain.reshape(1, width), w_out, *after)


def input_back_kernel(dq_ref, dkv_ref, wq_ref, wk_ref, wv_ref, x_ref, gain_ref, mgrad_ref, *refs):
    out_ref, dgain_ref = refs[-2:]
    step = pl.program_id(0)
    term = dot_nt(dq_ref[...], wq_ref[...])
    term = term + dot_nt(dkv_ref[:, :HD], wk_ref[...]) + dot_nt(dkv_ref[:, HD:], wv_ref[...])

    @pl.when(step == 0)
    def _():
        out_ref[...] = term

    @pl.when(step > 0)
    def _():
        out_ref[...] += term

    @pl.when(step == pl.num_programs(0) - 1)
    def _():
        upstream = out_ref[...]
        x = x_ref[...].astype(f32)
        factor = lax.rsqrt(jnp.mean(x * x, axis=-1, keepdims=True) + EPSILON)
        scaled = upstream * gain_ref[...]
        inner = jnp.mean(scaled * x, axis=-1, keepdims=True)
        out_ref[...] = mgrad_ref[...] + factor * scaled - x * (factor * factor * factor * inner)
        dgain_ref[...] = jnp.sum(upstream * x * factor, axis=0, keepdims=True)


def input_back(dq, dkv, wq, wk, wv, x, gain, mgrad, after=()):
    rows, width = x.shape
    wide = GROUPS * HD
    return pl.pallas_call(
        input_back_kernel,
        grid=(KVH,),
        in_specs=[
            pl.BlockSpec((rows, wide), lambda g: (0, g)),
            pl.BlockSpec((rows, 2 * HD), lambda g: (0, g)),
            pl.BlockSpec((width, wide), lambda g: (0, g)),
            pl.BlockSpec((width, HD), lambda g: (0, g)),
            pl.BlockSpec((width, HD), lambda g: (0, g)),
            whole((rows, width)),
            whole((1, width)),
            whole((rows, width)),
        ]
        + anywhere(len(after)),
        out_specs=[whole((rows, width)), whole((1, width))],
        out_shape=[
            jax.ShapeDtypeStruct((rows, width), f32),
            jax.ShapeDtypeStruct((1, width), f32),
        ],
        compiler_params=params(),
        cost_estimate=cost(2 * rows * width * (H + 2 * KVH) * HD, 14 * 2**20),
    )(dq, dkv, wq, wk, wv, x, gain.reshape(1, width), mgrad, *after)


def gate_column(expert, gates):
    lanes = lax.broadcasted_iota(jnp.int32, gates.shape, 1)
    chosen = (lanes == expert) | (lanes == expert + LOW_LANE)
    return jnp.sum(jnp.where(chosen, gates.astype(f32), 0.0), axis=1, keepdims=True)


def experts_kernel(count, per, gated, extra, pos, *refs):
    x_refs, c_refs, weights = refs[:count], refs[count : 2 * count], refs[2 * count : 2 * count + 3]
    *outs, acc_o, acc_g = refs[2 * count + 3 + extra :]
    out_refs, grad_refs, kept_refs = outs[:count], outs[count : 2 * count], outs[2 * count :]
    wg_ref, wu_ref, wd_ref = weights
    hid_ref, dgu_ref = kept_refs[-2:]
    step = pl.program_id(0)
    last = pl.num_programs(0) - 1
    rows, width = x_refs[0].shape
    chunk = wg_ref.shape[1]
    parts = [slice(b * rows, (b + 1) * rows) for b in range(count)]
    if gated:

        @pl.when(step == 0)
        def _():
            for part, x_ref, c_ref in zip(parts, x_refs, c_refs):
                kept_refs[0][part, :] = x_ref[...]
                kept_refs[1][part, :] = c_ref[...]

    for part, x_ref, c_ref in zip(parts, x_refs, c_refs):
        x = x_ref[...]
        gate = dot(x, wg_ref[...])
        up = dot(x, wu_ref[...])
        slope = dot_nt(c_ref[:, :width], wd_ref[...])
        sigmoid = 1.0 / (1.0 + jnp.exp(-gate))
        act = gate * sigmoid
        hidden = act * up
        if gated:
            held = pl.num_programs(0) // per
            expert = (2 * pos[2] + pos[3]) * held + step // per
            weight = gate_column(expert, c_ref[:, width:])
            hidden = hidden * weight
            slope = slope * weight
        hidden = hidden.astype(bf16)
        dg = (slope * up * (sigmoid * (1.0 + gate * (1.0 - sigmoid)))).astype(bf16)
        du = (slope * act).astype(bf16)
        hid_ref[part, :] = hidden
        dgu_ref[part, :chunk] = dg
        dgu_ref[part, chunk:] = du
        out_term = dot(hidden, wd_ref[...])
        grad_term = dot_nt(dg, wg_ref[...]) + dot_nt(du, wu_ref[...])

        @pl.when(step == 0)
        def _():
            acc_o[part, :] = out_term
            acc_g[part, :] = grad_term

        @pl.when(step > 0)
        def _():
            acc_o[part, :] += out_term
            acc_g[part, :] += grad_term

    @pl.when(step == last)
    def _():
        for part, out_ref, grad_ref in zip(parts, out_refs, grad_refs):
            out_ref[...] = acc_o[part, :].astype(out_ref.dtype)
            grad_ref[...] = acc_g[part, :].astype(grad_ref.dtype)


def experts(pos, xs, cs, weights, part, parts, kept, gated, kind, chunk=256):
    count = len(xs)
    rows, width = xs[0].shape
    taken = count * rows
    inner = weights[2].shape[1]
    per = inner // chunk
    steps = weights[0].shape[0] * per
    specs = [
        pl.BlockSpec((None, width, chunk), lambda i, _: (i // per, 0, i % per)),
        pl.BlockSpec((None, width, chunk), lambda i, _: (i // per, 0, i % per)),
        pl.BlockSpec((None, chunk, width), lambda i, _: (i // per, i % per, 0)),
    ]
    all_rows = parts * taken
    collected = [
        jax.ShapeDtypeStruct((all_rows, steps * chunk), bf16),
        jax.ShapeDtypeStruct((all_rows, 2 * steps * chunk), bf16),
    ]
    collected_specs = [
        pl.BlockSpec((taken, chunk), lambda i, _: (part, i)),
        pl.BlockSpec((taken, 2 * chunk), lambda i, _: (part, i)),
    ]
    if gated:
        collected = [
            jax.ShapeDtypeStruct((all_rows, width), bf16),
            jax.ShapeDtypeStruct((all_rows, cs[0].shape[1]), bf16),
        ] + collected
        collected_specs = [
            pl.BlockSpec((taken, width), lambda i, _: (part, 0)),
            pl.BlockSpec((taken, cs[0].shape[1]), lambda i, _: (part, 0)),
        ] + collected_specs
    operands = [pos, *xs, *cs, *weights]
    aliases = {}
    if kept is not None:
        aliases = {len(operands) + j: 2 * count + j for j in range(len(collected))}
        operands += list(kept)
    extra = 0 if kept is None else len(collected)
    result = pl.pallas_call(
        functools.partial(experts_kernel, count, per, gated, extra),
        grid_spec=pltpu.PrefetchScalarGridSpec(
            num_scalar_prefetch=1,
            grid=(steps,),
            in_specs=[whole((rows, width))] * count + [whole(cs[0].shape)] * count + specs + anywhere(extra),
            out_specs=[whole((rows, width))] * (2 * count) + collected_specs,
            scratch_shapes=[pltpu.VMEM((taken, width), f32)] * 2,
        ),
        out_shape=[jax.ShapeDtypeStruct((rows, width), kind)] * (2 * count) + collected,
        input_output_aliases=aliases,
        compiler_params=params(),
        cost_estimate=cost(26 * taken * width * steps * chunk, 12 * 2**20),
    )(*operands)
    return result[:count], result[count : 2 * count], result[2 * count :]


def others_kernel(sets, per, bands, extra, pos, x_ref, c_ref, *refs):
    each = bands + per
    weights = [refs[t * each : (t + 1) * each] for t in range(sets)]
    *result_refs, hid_ref, dgu_ref = refs[sets * each + extra :]
    out_refs, grad_refs = result_refs[: len(result_refs) // 2], result_refs[len(result_refs) // 2 :]
    step = pl.program_id(0)
    width = x_ref.shape[1]
    band = width // bands
    chunk = weights[0][bands].shape[0]
    rows = out_refs[0].shape[0]

    def places(t, n):
        at = (lax.rem(pos[1] + t, 2) * per + n) * chunk
        cut = lambda first: pl.ds(pl.multiple_of(first, chunk), chunk)
        return cut(at), cut(2 * at), cut(2 * at + chunk)

    def columns(n):
        return slice(n * chunk, (n + 1) * chunk), slice((per + n) * chunk, (per + n + 1) * chunk)

    def hidden_chunk(t, n):
        at_hidden, at_gate, at_up = places(t, n)
        gate_cut, up_cut = columns(n)
        expert = (2 * pos[2] + 1 - pos[3]) * sets + lax.rem(pos[1] + t, 2)
        gate = up = 0.0
        for k in range(bands):
            part = x_ref[:, k * band : (k + 1) * band]
            gate = gate + dot(part, weights[t][k][:, gate_cut])
            up = up + dot(part, weights[t][k][:, up_cut])
        slope = dot_nt(c_ref[:, :width], weights[t][bands + n][...])
        sigmoid = 1.0 / (1.0 + jnp.exp(-gate))
        act = gate * sigmoid
        weight = gate_column(expert, c_ref[:, width:])
        slope = slope * weight
        hid_ref[:, at_hidden] = (act * up * weight).astype(bf16)
        dgu_ref[:, at_gate] = (slope * up * (sigmoid * (1.0 + gate * (1.0 - sigmoid)))).astype(bf16)
        dgu_ref[:, at_up] = (slope * act).astype(bf16)

    def results(k):
        out = grad = 0.0
        for t in range(sets):
            for n in range(per):
                at_hidden, at_gate, at_up = places(t, n)
                gate_cut, up_cut = columns(n)
                down = weights[t][bands + n][:, k * band : (k + 1) * band]
                out = out + dot(hid_ref[:, at_hidden], down)
                grad = grad + dot_nt(dgu_ref[:, at_gate], weights[t][k][:, gate_cut])
                grad = grad + dot_nt(dgu_ref[:, at_up], weights[t][k][:, up_cut])
        for p in range(len(out_refs)):
            out_refs[p][...] = out[p * rows : (p + 1) * rows].astype(bf16)
            grad_refs[p][...] = grad[p * rows : (p + 1) * rows].astype(bf16)

    for t in range(sets):
        for n in range(per):
            pl.when(step == t * per + n)(functools.partial(hidden_chunk, t, n))
    for k in range(bands):
        pl.when(step == sets * per + k)(functools.partial(results, k))


def others(pos, x, c, weights, part, parts, count, kept):
    taken, width = x.shape[0] // parts, x.shape[1]
    sets = len(weights)
    bands, downs = weights[0]
    per = len(downs)
    inner = per * downs[0].shape[0]
    flat = [v for bands_t, downs_t in weights for v in [*bands_t, *downs_t]]
    tile = width // len(bands)
    rows_spec = lambda v: pl.BlockSpec(
        (taken, v.shape[1]), lambda *_: (part, 0), pipeline_mode=pl.Buffered(1)
    )
    resident = lambda v: pl.BlockSpec(v.shape, lambda *_: (0, 0), pipeline_mode=pl.Buffered(1))
    late = lambda i: jnp.maximum(i - sets * per, 0)
    operands = [pos, x, c] + flat
    extra = 0 if kept is None else 2
    aliases = {len(operands) + j: 2 * count + j for j in range(extra)}
    collected = [sets * inner, 2 * sets * inner]
    result = pl.pallas_call(
        functools.partial(others_kernel, sets, per, len(bands), extra),
        grid_spec=pltpu.PrefetchScalarGridSpec(
            num_scalar_prefetch=1,
            grid=(sets * per + len(bands),),
            in_specs=[rows_spec(x), rows_spec(c)] + [resident(v) for v in flat] + anywhere(extra),
            out_specs=[pl.BlockSpec((taken // count, tile), lambda i, _: (0, late(i)))] * (2 * count)
            + [pl.BlockSpec((taken, n), lambda *_: (part, 0)) for n in collected],
        ),
        out_shape=[jax.ShapeDtypeStruct((taken // count, width), bf16)] * (2 * count)
        + [jax.ShapeDtypeStruct((parts * taken, n), bf16) for n in collected],
        input_output_aliases=aliases,
        compiler_params=params(),
        cost_estimate=cost(26 * taken * width * sets * inner, 12 * 2**20),
    )(*operands, *(kept or []))
    return result[:count], result[count : 2 * count], result[2 * count :]


def side_of(outer, s, pos):
    return 2 * lax.rem(s, outer) + lax.rem(pos[1] + 1 - s // outer, 2)


def halves_kernel(shape, outer, pos, *refs):
    sent_ref, kept_ref = refs[-2:]

    def write(out_ref):
        first = 0
        for i, rows in enumerate(shape):
            total = dot_tn(refs[2 * i][...], refs[2 * i + 1][...]).astype(bf16)
            blank = out_ref.shape[2] - total.shape[1]
            if blank:
                out_ref[:, first : first + rows, total.shape[1] :] = jnp.zeros(
                    (out_ref.shape[0], rows, blank), bf16
                )
            for e in range(out_ref.shape[0]):
                part = total[e * rows : (e + 1) * rows]
                out_ref[e, first : first + rows, : total.shape[1]] = part
            first += rows

    pl.when(pl.program_id(0) < outer)(lambda: write(sent_ref))
    pl.when(pl.program_id(0) >= outer)(lambda: write(kept_ref))


def halves(pos, pairs, after=()):
    n_ctx, n_exp = lax.axis_size("ctx"), lax.axis_size("exp")
    outer = n_ctx // 2
    shape = [left.shape[1] // (n_ctx * n_exp) for left, _ in pairs]
    wide = max(right.shape[1] for _, right in pairs)
    full = (outer * n_exp, sum(shape), wide)
    if any((left.shape[1] // n_ctx) % 128 for left, _ in pairs):
        out = []
        for side in (1, 0):
            parts = []
            for left, right in pairs:
                split = left.reshape(left.shape[0], outer, 2, -1)
                mine = lax.dynamic_index_in_dim(split, (pos[1] + side) % 2, 2, keepdims=False)
                total = dot_tn(mine.reshape(left.shape[0], -1), right).astype(bf16)
                total = total.reshape(outer * n_exp, -1, right.shape[1])
                parts.append(jnp.pad(total, ((0, 0), (0, 0), (0, wide - right.shape[1]))))
            joined = jnp.concatenate(parts, axis=1)
            out.append(jnp.pad(joined, ((0, 0), (0, -joined.shape[1] % 16), (0, 0))))
        return out
    in_specs, operands = [], []
    for left, right in pairs:
        columns = left.shape[1] // n_ctx
        in_specs.append(
            pl.BlockSpec((left.shape[0], columns), lambda s, pos: (0, side_of(outer, s, pos)))
        )
        in_specs.append(whole(right.shape))
        operands += [left, right]
    block = (n_exp,) + full[1:]
    flops = sum(2 * left.size * right.shape[1] for left, right in pairs)
    return pl.pallas_call(
        functools.partial(halves_kernel, shape, outer),
        grid_spec=pltpu.PrefetchScalarGridSpec(
            num_scalar_prefetch=1,
            grid=(2 * outer,),
            in_specs=in_specs + anywhere(len(after)),
            out_specs=[
                pl.BlockSpec(block, lambda s, pos: (jnp.minimum(s, outer - 1), 0, 0)),
                pl.BlockSpec(block, lambda s, pos: (jnp.maximum(s - outer, 0), 0, 0)),
            ],
        ),
        out_shape=[jax.ShapeDtypeStruct(full, bf16)] * 2,
        compiler_params=params(),
        cost_estimate=cost(2 * flops, 8 * 2**20),
    )(pos, *operands, *after)


def rows_product_kernel(blocks, pos, *refs):
    total = dot_tn(refs[0][...], refs[blocks][...])
    for b in range(1, blocks):
        total = total + dot_tn(refs[b][...], refs[blocks + b][...])
    refs[-1][...] = total.astype(bf16)


def rows_product(pos, lefts, rights, tile=512):
    n_ctx, n_exp = lax.axis_size("ctx"), lax.axis_size("exp")
    depth, height = lefts[0][0].shape
    high, wide = height // n_ctx, rights[0][0].shape[1]
    if high % 128:
        place = lax.axis_index("ctx") * high
        cut = lambda v: lax.slice_in_dim(v[0], v[1] * depth, (v[1] + 1) * depth, axis=0)
        total = sum(
            dot_tn(lax.dynamic_slice_in_dim(cut(a), place, high, 1), cut(b))
            for a, b in zip(lefts, rights)
        )
        return total.astype(bf16).reshape(n_exp, -1, wide)
    blocks = len(lefts)
    left_specs = [
        pl.BlockSpec((depth, high), functools.partial(lambda k, n, pos: (k, 2 * pos[0] + pos[1]), k))
        for _, k in lefts
    ]
    right_specs = [
        pl.BlockSpec((depth, tile), functools.partial(lambda k, n, pos: (k, n), k)) for _, k in rights
    ]
    total = pl.pallas_call(
        functools.partial(rows_product_kernel, blocks),
        grid_spec=pltpu.PrefetchScalarGridSpec(
            num_scalar_prefetch=1,
            grid=(wide // tile,),
            in_specs=left_specs + right_specs,
            out_specs=pl.BlockSpec((high, tile), lambda n, pos: (0, n)),
        ),
        out_shape=jax.ShapeDtypeStruct((high, wide), bf16),
        compiler_params=params(),
        cost_estimate=cost(4 * blocks * depth * high * wide, 4 * 2**20),
    )(pos, *[v for v, _ in lefts], *[v for v, _ in rights])
    return total.reshape(n_exp, -1, wide)


def expert_halves_kernel(blocks, tiles, pos, *refs):
    rows_refs, cot_refs = refs[:blocks], refs[blocks : 2 * blocks]
    dgu_ref, hid_ref, sent_ref, kept_ref = refs[2 * blocks :]
    n = pl.program_id(0)
    high = sent_ref.shape[1]

    def write(left_refs, right_ref):
        left = jnp.concatenate([ref[...] for ref in left_refs], axis=1)
        total = dot_tn(left, right_ref[...]).astype(bf16)
        count = sent_ref.shape[0]
        for i in range(count):
            sent_ref[i] = total[i * high : (i + 1) * high]
            kept_ref[i] = total[(count + i) * high : (count + i + 1) * high]

    pl.when(n < tiles)(lambda: write(rows_refs, dgu_ref))
    pl.when(n >= tiles)(lambda: write(cot_refs, hid_ref))


def expert_steps(width):
    high = width // lax.axis_size("ctx")
    return high // 128 if high % 128 == 0 else 1


def expert_halves(pos, rows_all, cot_all, dgu, hid, tile=512):
    n_ctx = lax.axis_size("ctx")
    depth, width = rows_all.shape
    high = width // n_ctx
    wide = dgu.shape[1] + hid.shape[1]
    steps = expert_steps(width)
    if high % 128:
        out = []
        for side in (1, 0):
            place = lambda y: (2 * y + (pos[1] + side) % 2) * high
            pick = lambda v: jnp.concatenate(
                [lax.dynamic_slice_in_dim(v, place(y), high, 1) for y in range(n_ctx // 2)], axis=1
            )
            parts = [dot_tn(pick(v), w).astype(bf16) for v, w in ((rows_all, dgu), (cot_all, hid))]
            out.append(jnp.concatenate(parts, axis=1).reshape(n_ctx // 2 * steps, -1, wide))
        return out
    tiles, down = dgu.shape[1] // tile, hid.shape[1] // tile
    left_specs = [
        pl.BlockSpec((depth, high), functools.partial(lambda s, n, pos: (0, side_of(n_ctx // 2, s, pos)), s))
        for s in range(n_ctx)
    ]
    block = (n_ctx // 2 * steps, high // steps, tile)
    return pl.pallas_call(
        functools.partial(expert_halves_kernel, n_ctx, tiles),
        grid_spec=pltpu.PrefetchScalarGridSpec(
            num_scalar_prefetch=1,
            grid=(tiles + down,),
            in_specs=left_specs * 2
            + [
                pl.BlockSpec((depth, tile), lambda n, pos: (0, jnp.minimum(n, tiles - 1))),
                pl.BlockSpec((depth, tile), lambda n, pos: (0, jnp.maximum(n - tiles, 0))),
            ],
            out_specs=[pl.BlockSpec(block, lambda n, pos: (0, 0, n))] * 2,
        ),
        out_shape=[jax.ShapeDtypeStruct(block[:2] + (wide,), bf16)] * 2,
        compiler_params=params(),
        cost_estimate=cost(4 * depth * width * wide, 16 * 2**20),
    )(pos, *[rows_all] * n_ctx, *[cot_all] * n_ctx, dgu, hid)


def sums_kernel(shape, only, extra, pos, *refs):
    ins, outs = refs[: sum(shape)], refs[sum(shape) + extra :]
    at = 0
    for count, out in zip(shape, outs):
        total = ins[at][...].astype(f32)
        for k in range(at + 1, at + count):
            term = ins[k][...].astype(f32)
            if only[k] is not None:
                term = jnp.where(pl.program_id(0) == only[k], term, 0.0)
            total = total + term
        out[...] = total.astype(out.dtype)
        at += count


def sums(pos, steps, outputs, after=()):
    operands, in_specs, out_specs, out_shape, only = [], [], [], [], []
    for kind, block, terms in outputs:
        for array, index, *step in terms:
            operands.append(array)
            only.append(step[0] if step else None)
            in_specs.append(pl.BlockSpec(block, functools.partial(place_of, index)))
        out_specs.append(pl.BlockSpec(block, lambda i, pos: (i, 0, 0)))
        out_shape.append(jax.ShapeDtypeStruct((steps * block[0],) + tuple(block[1:]), kind))
    return pl.pallas_call(
        functools.partial(sums_kernel, [len(terms) for _, _, terms in outputs], only, len(after)),
        grid_spec=pltpu.PrefetchScalarGridSpec(
            num_scalar_prefetch=1,
            grid=(steps,),
            in_specs=in_specs + anywhere(len(after)),
            out_specs=out_specs,
        ),
        out_shape=out_shape,
        compiler_params=params(),
        cost_estimate=cost(0, 8 * 2**20),
    )(pos, *operands, *after)


def place_of(index, i, pos):
    at = index(i, pos)
    return at if isinstance(at, tuple) else (at, 0, 0)


def straight(i, pos):
    return i


def row_sum(terms, kind=bf16):
    total = terms[0].astype(f32)
    for term in terms[1:]:
        total = total + term.astype(f32)
    return total.astype(kind)


def expert_out_kernel(gates, each, *refs):
    in_refs, (gate_ref, up_ref, down_ref) = refs[:4], refs[4:]
    n = pl.program_id(0)

    def write(ref):
        @pl.when((n < gates) & (lax.rem(n, 2) == 0))
        def _():
            gate_ref[0] = ref[...].astype(f32)

        @pl.when((n < gates) & (lax.rem(n, 2) == 1))
        def _():
            up_ref[0] = ref[...].astype(f32)

        @pl.when(n >= gates)
        def _():
            down_ref[0] = jnp.transpose(ref[...].astype(f32))

    for q in range(4):
        pl.when(n // each == q)(functools.partial(write, in_refs[q]))


def expert_out(quarters, inner, chunk=256):
    rows, wide = quarters[0].shape
    each = wide // chunk
    held = 4 * wide // (3 * inner)
    per = inner // chunk
    gates = 2 * held * per
    tile = lambda n: jnp.minimum(n, gates - 1) // 2
    spec = pl.BlockSpec((1, rows, chunk), lambda n: (tile(n) // per, 0, lax.rem(tile(n), per)))
    at = lambda n: jnp.maximum(n - gates, 0)
    return pl.pallas_call(
        functools.partial(expert_out_kernel, gates, each),
        grid=(4 * each,),
        in_specs=[
            pl.BlockSpec(
                (rows, chunk),
                functools.partial(lambda q, n: (0, jnp.clip(n - q * each, 0, each - 1)), q),
            )
            for q in range(4)
        ],
        out_specs=[
            spec,
            spec,
            pl.BlockSpec((1, chunk, rows), lambda n: (at(n) // per, lax.rem(at(n), per), 0)),
        ],
        out_shape=[jax.ShapeDtypeStruct((held, rows, inner), f32)] * 2
        + [jax.ShapeDtypeStruct((held, inner, rows), f32)],
        compiler_params=params(),
        cost_estimate=cost(0, 8 * 2**20),
    )(*quarters)


def last_sum(refs):
    total = refs[0][...].astype(f32)
    for ref in refs[1:]:
        total = total + ref[...].astype(f32)
    return total


def dense_out_kernel(count, *refs):
    total = last_sum(refs[:count])
    out_ref, query_ref, key_ref, value_ref = refs[count:]
    wide = out_ref.shape[1]
    out_ref[...] = total[:, :wide]
    query_ref[...] = total[:, wide : 2 * wide]
    for g in range(KVH):
        first = 2 * wide + 2 * g * HD
        key_ref[:, g * HD : (g + 1) * HD] = total[:, first : first + HD]
        value_ref[:, g * HD : (g + 1) * HD] = total[:, first + HD : first + 2 * HD]


def dense_out(terms, wide):
    rows = terms[0].shape[0]
    shapes = [wide, wide, KVH * HD, KVH * HD]
    return pl.pallas_call(
        functools.partial(dense_out_kernel, len(terms)),
        out_shape=[jax.ShapeDtypeStruct((rows, n), f32) for n in shapes],
        compiler_params=params(),
        cost_estimate=cost(0, 2**20),
    )(*terms)


def shared_out_kernel(count, chunk, *refs):
    total = last_sum(refs[:count])
    gate_ref, up_ref, down_ref = refs[count:]
    rows = gate_ref.shape[0]
    for n in range(gate_ref.shape[1] // chunk):
        cut = slice(n * chunk, (n + 1) * chunk)
        gate_ref[:, cut] = total[:rows, 2 * n * chunk : (2 * n + 1) * chunk]
        up_ref[:, cut] = total[:rows, (2 * n + 1) * chunk : (2 * n + 2) * chunk]
    down_ref[...] = total[rows : rows + down_ref.shape[0], : down_ref.shape[1]]


def shared_grads(terms, gate, down, chunk=256):
    return pl.pallas_call(
        functools.partial(shared_out_kernel, len(terms), chunk),
        out_shape=[jax.ShapeDtypeStruct(v, f32) for v in (gate, gate, down)],
        compiler_params=params(),
        cost_estimate=cost(0, 2**20),
    )(*terms)


def hold(values, after):
    count = len(values)
    return pl.pallas_call(
        lambda *_: None,
        in_specs=[pl.BlockSpec(memory_space=pl.ANY)] * (count + len(after)),
        out_specs=[pl.BlockSpec(memory_space=pl.ANY)] * count,
        out_shape=[jax.ShapeDtypeStruct(v.shape, v.dtype) for v in values],
        input_output_aliases={i: i for i in range(count)},
        compiler_params=params(),
        cost_estimate=cost(0, 0),
    )(*values, *after)


def swap_inner(value, axis):
    size = lax.axis_size(axis)
    return lax.ppermute(value, axis, [(i, i ^ 1) for i in range(size)])


def shift_outer(value, axis, by):
    outer = lax.axis_size(axis) // 2
    perm = [(o * 2 + i, ((o + by) % outer) * 2 + i) for o in range(outer) for i in range(2)]
    return lax.ppermute(value, axis, perm)


def ring_step(value, by):
    n_ctx, n_exp = lax.axis_size("ctx"), lax.axis_size("exp")
    outer = n_exp // 2
    perm = []
    for c in range(n_ctx):
        way = by if c % 2 == 0 else -by
        for o in range(outer):
            for i in range(2):
                perm.append((c * n_exp + o * 2 + i, c * n_exp + ((o + way) % outer) * 2 + i))
    return lax.ppermute(value, BOTH, perm)


def by_blocks(value, together):
    return value.reshape(-1, together * value.shape[1], value.shape[2])


def spread_outer(value):
    moved, out = value, []
    for _ in range(1, lax.axis_size("ctx") // 2):
        moved = shift_outer(moved, "ctx", 1)
        out.append(moved)
    return out, swap_inner(value, "ctx")


def spread_inner(moved):
    return [swap_inner(v, "ctx") for v in moved]


def outer_blocks(value):
    moved, out = value, []
    for _ in range(1, lax.axis_size("ctx") // 2):
        moved = shift_outer(moved, "ctx", 1)
        out.append(moved)
    return out


def inner_blocks(value, moved):
    return swap_inner(jnp.concatenate([value] + moved, axis=0), "ctx")


def all_blocks(value, moved, across):
    out = []
    for k, v in enumerate([value] + moved):
        out += [(v, 0), (across, k)]
    return out


def spread_all(value, moved, across, moved_across):
    blocks = [value, across]
    for a, b in zip(moved, moved_across):
        blocks += [a, b]
    return blocks


def paired_blocks(value, across, moved, moved_across):
    out = [(value, 0), (across, 0)]
    for a, b in zip(moved, moved_across):
        out += [(a, 0), (b, 0)]
    return out


class Shared:
    def __init__(self, pos, kept, got):
        self.pos = pos
        self.outer, self.levels = lax.axis_size("ctx") // 2, lax.axis_size("exp") // 2
        self.rows, self.wide = kept.shape[1:]
        self.pair = lambda v: v.reshape(-1, 2 * self.rows, self.wide)
        self.terms = [self.pair(v) for v in (kept, got)]
        self.together = 1
        self.steps = self.levels

    def _sum(self, d, rows, inner, moved=()):
        at = lambda i, pos: lax.rem(pos[0] + d, self.outer) * self.steps + i
        terms = [(v, lambda i, pos: (at(i, pos), inner(pos), 0)) for v in self.terms]
        for parts in moved:
            for k, v in enumerate(parts):
                terms.append((self.pair(v), lambda i, pos: (0, inner(pos), 0), k))
        return terms, (self.together, rows, self.wide)

    def first(self):
        out = []
        for d in range(1, self.outer):
            terms, block = self._sum(d, 2 * self.rows, lambda pos: 0)
            outputs = []
            for k in range(self.steps):
                part = [(v, functools.partial(lambda f, k, i, pos: f(k, pos), f, k)) for v, f in terms]
                outputs.append((bf16, block, part))
            out.append(sums(self.pos, 1, outputs))
        return out

    def second(self, moved, first, last):
        moved = [v[first:last] for v in moved]
        terms, block = self._sum(0, self.rows, lambda pos: 1 - pos[3], moved)
        later = lambda f: lambda i, pos: f(first + i, pos)
        terms = [(v, f, *o) if o else (v, later(f)) for v, f, *o in terms]
        return sums(self.pos, last - first, [(bf16, block, terms)])

    def total(self, moved, crossed):
        terms, block = self._sum(0, self.rows, lambda pos: pos[3], moved)
        at = 0
        for v in crossed:
            for k in range(v.shape[0]):
                terms.append((v, functools.partial(lambda k, i, pos: k, k), at))
                at += 1
        return sums(self.pos, self.steps, [(bf16, block, terms)])[0]


def z_take(total, d):
    levels = total.shape[0]
    return lax.dynamic_index_in_dim(total, (lax.axis_index("exp") // 2 + d) % levels, 0, False)


def z_send(total, d):
    return shift_outer(z_take(total, d), "exp", d)


def over_x(total):
    pairs = total.reshape((-1, 2) + total.shape[1:])
    return swap_inner(lax.dynamic_index_in_dim(pairs, 1 - lax.axis_index("exp") % 2, 1, False), "exp")


def mine_x(total):
    pairs = total.reshape((-1, 2) + total.shape[1:])
    return lax.dynamic_index_in_dim(pairs, lax.axis_index("exp") % 2, 1, False)


def over_z(pos, mine, arrived):
    levels, rows, wide = mine.shape
    outputs = []
    for d in range(levels):
        at = functools.partial(lambda d, i, pos: lax.rem(pos[2] + d, levels), d)
        outputs.append((bf16 if d else f32, (1, rows, wide), [(mine, at), (arrived, at)]))
    own, *sent = [v[0] for v in sums(pos, 1, outputs)]
    return [own] + [shift_outer(v, "exp", d + 1) for d, v in enumerate(sent)]


def expert_quarter(kept, got, q, row):
    steps = kept.shape[0] // (lax.axis_size("ctx") // 2)
    block = (steps, kept.shape[1], kept.shape[2] // 4)
    return block, [(v, lambda i, pos: (row(i, pos), 0, q)) for v in (kept, got)]


def expert_pieces(pos, kept, got, quarters):
    outputs = []
    for q in quarters:
        block, terms = expert_quarter(kept, got, q, straight)
        outputs.append((bf16, block, terms))
    return sums(pos, lax.axis_size("ctx") // 2, outputs)


def expert_row(d):
    outer = lax.axis_size("ctx") // 2
    return lambda i, pos: lax.rem(pos[0] + d, outer)


def expert_send(pos, kept, got, pieces, half):
    sent = []
    for d in range(1, lax.axis_size("ctx") // 2):
        row = expert_row(d)
        block, terms = expert_quarter(kept, got, 0, row)
        terms = [(v, lambda i, pos: (row(i, pos), 0, 2 * half + i)) for v, _ in terms]
        terms += [(pieces[2 * half + k], lambda i, pos: row(0, pos), k) for k in range(2)]
        sent += sums(pos, 2, [(bf16, block, terms)])
    return sent


def expert_move(sent):
    return [shift_outer(v, "ctx", d + 1) for d, v in enumerate(sent)]


def expert_total(pos, kept, got, pieces, arrived):
    row = expert_row(0)
    outputs = []
    for q in range(4):
        block, terms = expert_quarter(kept, got, q, row)
        at = functools.partial(lambda k, i, pos: k, q % 2)
        terms = terms + [(pieces[q], row)] + [(v, at) for v in arrived[q // 2]]
        outputs.append((bf16, block, terms))
    return [v.reshape(-1, v.shape[2]) for v in sums(pos, 1, outputs)]


def shards(
    layer_input,
    attn_gain,
    w_query,
    w_key,
    w_value,
    w_out,
    ffn_gain,
    shared_gate,
    shared_up,
    shared_down,
    expert_gate,
    expert_up,
    expert_down,
    routes,
    gate_logits,
    span_order,
    cotangent,
):
    x = layer_input[0]
    cot = cotangent[0]
    tokens, width = x.shape
    span_rows = tokens // 2
    n_ctx, n_exp = lax.axis_size("ctx"), lax.axis_size("exp")
    ctx_id, exp_id = lax.axis_index("ctx"), lax.axis_index("exp")
    local_experts, _, inner = expert_gate.shape
    expert_count = local_experts * n_exp

    levels = n_exp // 2
    pos = jnp.stack([ctx_id // 2, ctx_id % 2, exp_id // 2, exp_id % 2]).astype(jnp.int32)

    always = pos[0] < n_ctx
    ring = n_ctx // 2

    def region(work):
        made = jax.eval_shape(work)
        return lax.cond(always, work, lambda: jax.tree.map(lambda v: jnp.zeros(v.shape, v.dtype), made))

    gate_vals = jax.nn.softmax(gate_logits[0], axis=-1)
    named = routes[0][:, None, :] == jnp.arange(expert_count, dtype=jnp.int32)[None, :, None]
    row_gates = jnp.sum(jnp.where(named, gate_vals[:, None, :], 0.0), axis=-1)
    high = row_gates.astype(bf16)
    low = (row_gates - high.astype(f32)).astype(bf16)
    fill = lambda width: ((0, 0), (0, width - expert_count))
    cot_ring = [
        jnp.concatenate(
            [cot, jnp.pad(high, fill(LOW_LANE)), jnp.pad(low, fill(GATE_LANES - LOW_LANE))], axis=1
        )
    ]

    chunk, bands = 256, 3
    mine = lambda v: lax.dynamic_index_in_dim(v, pos[1], 0, keepdims=False)
    over_core = lambda v: swap_inner(v, "ctx")

    def fetch(k):
        return swap_inner(asked[k], "exp")

    def arranged(parts):
        return parts[inner // chunk :], parts[: inner // chunk]

    def ask():
        down = mine(expert_down)
        out = [down[n * chunk : (n + 1) * chunk] for n in range(inner // chunk)]
        gate, up = mine(expert_gate), mine(expert_up)
        band = width // bands
        for k in range(bands):
            cut = slice(k * band, (k + 1) * band)
            out.append(jnp.concatenate([gate[cut], up[cut]], axis=1))
        return out

    def gather_keys():
        normed, kv = keyvalue(x, attn_gain, w_key, w_value)
        moved, across = spread_outer(kv)
        queries = dot(normed, w_query).astype(bf16)
        asked = ask()
        keys = kv, moved, across, spread_inner(moved)
        return normed, keys, queries, ring_step(cot_ring[0], 1), asked, swap_inner(asked[0], "exp")

    normed, keys, queries, cot_next, asked, got = region(gather_keys)
    kv_blocks = spread_all(*keys)
    cot_ring.append(cot_next)
    fetched, crossed = [got], []

    def attention():
        attended, lse = attend(pos, span_order, queries, kv_blocks)
        middle, rows = middle_forward(x, attended, w_out, ffn_gain)
        moved = outer_blocks(normed), ring_step(cot_ring[1], 1), fetch(1), over_core(fetched[0])
        return attended, lse, middle, rows, over_core(normed), *moved

    attended, lse, middle, rows_low, across, normed_moved, cot_next, got, crossing = region(attention)
    normed_across = across
    cot_ring.append(cot_next)
    fetched.append(got)
    crossed.append(crossing)

    own_weights = (expert_gate, expert_up, expert_down)

    def own_part(ks, rows, part, parts, kept):
        return experts(pos, rows, [cot_ring[k] for k in ks], own_weights, part, parts, kept, True, bf16)

    def first():
        weights = (shared_gate[None], shared_up[None], shared_down[None])
        shared = experts(pos, [rows_low], [cot], weights, 0, 1, None, False, f32)
        more = spread_inner(normed_moved), fetch(2), over_core(fetched[1]), outer_blocks(attended)
        return ring_step(rows_low, 1), shared, *more

    rows_one, shared, across, got, crossing, attended_moved = region(first)
    fetched.append(got)
    crossed.append(crossing)
    normed_blocks = paired_blocks(normed, normed_across, normed_moved, across)
    (shared_out,), (shared_grad,), (shared_hidden, shared_dgu) = shared
    shared_pairs = [(rows_low, shared_dgu), (shared_hidden, cot)]

    def second():
        result = own_part([0], [rows_low], 2, 4, None)
        more = fetch(3), over_core(fetched[2]), [over_core(attended), *spread_inner(attended_moved)]
        return ring_step(rows_one, 1), result, halves(pos, shared_pairs), *more

    rows_two, (out_k, grad_k, kept), (shared_sent, shared_kept), got, crossing, across = region(second)
    attended_blocks = paired_blocks(attended, across[0], attended_moved, across[1:])
    fetched.append(got)
    crossed.append(crossing)
    out_own, grad_own = list(out_k), list(grad_k)

    def third():
        more = over_core(shared_sent), fetch(4), over_core(fetched[3])
        pair = own_part([1, 2], [rows_one, rows_two], 0, 2, kept)
        sent = Shared(pos, shared_kept, more[0]).first()
        return ring_step(rows_two, 1), pair, sent, *more

    rows_k, (out_k, grad_k, kept), shared_sent, shared_got, got, crossing = region(third)
    fetched.append(got)
    crossed.append(crossing)
    out_own += out_k
    grad_own += grad_k

    def over_y(parts, k):
        return [shift_outer(v[k], "ctx", d + 1) for d, v in enumerate(parts)]

    def fourth():
        moved = ring_step(cot_ring[2], 1)
        weights = [arranged(fetched), arranged(crossed + [over_core(fetched[4])])]
        half = levels // 2
        arrived = [over_y(shared_sent, k) for k in range(levels - 1)]
        out_a, grad_a, new = others(pos, kept[0], kept[1], weights, 0, 2, half, None)
        last = experts(pos, [rows_k], [moved], own_weights, 3, 4, kept, True, bf16)
        out_b, grad_b, new = others(pos, last[2][0], last[2][1], weights, 1, 2, half, new)
        return last, [out_b[0], *out_a, out_b[1]], [grad_b[0], *grad_a, grad_b[1]], new, arrived

    (out_k, grad_k, kept), out_other, grad_other, kept_other, got = region(fourth)
    shared_moved = [list(v) for v in zip(*got)]
    out_own += out_k
    grad_own += grad_k
    rows_all, cot_all, hid_own, dgu_own = kept
    hid_other, dgu_other = kept_other

    def back_one():
        moved = ring_step(row_sum([grad_own[3], grad_other[3]]), -1)
        (part,) = Shared(pos, shared_kept, shared_got).second(shared_moved, 0, levels // 2)
        made = expert_halves(pos, rows_all, cot_all, dgu_other, hid_other)
        return moved, made, swap_inner(part, "exp"), over_y(shared_sent, levels - 1)

    moved, (sent, kept_other), crossed, got = region(back_one)
    shared_moved = [v + [w] for v, w in zip(shared_moved, got)]
    shared_crossed = [crossed]

    def back_two():
        total = row_sum([grad_own[2], grad_other[2], moved])
        got = swap_inner(sent, "ctx")
        (part,) = Shared(pos, shared_kept, shared_got).second(shared_moved, levels // 2, levels)
        made = expert_halves(pos, rows_all, cot_all, dgu_own, hid_own)
        piece = expert_pieces(pos, kept_other, got, [0])[0]
        return ring_step(total, -1), got, made, piece, swap_inner(part, "exp")

    moved_two, got_other, (sent_own, kept_own), piece, crossed = region(back_two)
    shared_crossed.append(crossed)

    def back_three():
        total = row_sum([grad_own[1], grad_other[1], moved_two])
        made = expert_pieces(pos, kept_other, got_other, [1, 2, 3])
        shared_sum = Shared(pos, shared_kept, shared_got).total(shared_moved, shared_crossed)
        out_total = row_sum([out_own[3], out_other[3]])
        middle_grads = middle_back(
            [shared_grad, grad_own[0], grad_other[0], ring_step(total, -1)],
            middle,
            cot,
            ffn_gain,
            w_out,
        )
        moved = middle_grads, swap_inner(sent_own, "ctx"), swap_inner(piece, "exp")
        shared_z = [z_take(shared_sum, d) for d in range(levels)]
        return *moved, made, shared_z, out_total

    middle_grads, got_own, piece, made, shared_z, out_total = region(back_three)
    mgrad, mgrad_low, ffn_gain_grad, att_grad = middle_grads
    pieces = [piece, *made]

    def attention_back():
        dq, same, across = attend_back(pos, span_order, queries, att_grad, lse, kv_blocks)
        got = ring_step(out_total, -1), swap_inner(pieces[1], "exp"), shift_outer(shared_z[1], "exp", 1)
        mgrad_parts = mgrad_low, over_core(mgrad_low), outer_blocks(mgrad_low)
        return mgrad_parts, dq, same, across, *got

    mgrad_parts, dq, same, across, out_moved, piece, got = region(attention_back)
    pieces[1] = piece
    shared_parts = [shared_z[0], got]

    def dense_one():
        got = over_core(across)
        made = []
        for k in reversed(range(ring)):
            part = slice(k * tokens, (k + 1) * tokens)
            made = row_sum([same[part], got[part]] + made)
            if k:
                made = [shift_outer(made, "ctx", -1)]
        total = row_sum([out_own[2], out_other[2], out_moved])
        mgrad_blocks = paired_blocks(*mgrad_parts, spread_inner(mgrad_parts[2]))
        total_out = rows_product(pos, attended_blocks, mgrad_blocks)
        sent = expert_send(pos, kept_own, got_own, pieces, 0)
        total = row_sum([out_own[1], out_other[1], ring_step(total, -1)])
        return made, outer_blocks(dq), total_out, sent, total, swap_inner(pieces[2], "exp")

    dkv, dq_moved, total_out, sent, out_total_two, piece = region(dense_one)
    pieces[2] = piece

    def dense_two():
        dkv_moved = outer_blocks(dkv)
        dkv_blocks = all_blocks(dkv, dkv_moved, inner_blocks(dkv, dkv_moved))
        dq_blocks = all_blocks(dq, dq_moved, inner_blocks(dq, dq_moved))
        total_query = rows_product(pos, normed_blocks, dq_blocks)
        total_kv = rows_product(pos, normed_blocks, dkv_blocks)
        back = input_back(dq, dkv, w_query, w_key, w_value, x, attn_gain, mgrad)
        moved = ring_step(out_total_two, -1), swap_inner(pieces[3], "exp"), expert_move(sent)
        return total_query, total_kv, back, *moved

    total_query, total_kv, (input_grad, attn_gain_grad), out_moved_three, piece, got = region(dense_two)
    pieces[3] = piece
    arrived = [got]

    def dense_three():
        devices = n_ctx * n_exp
        total = jnp.concatenate([total_out, total_query, total_kv], axis=2)
        got = expert_move(expert_send(pos, kept_own, got_own, pieces, 1))
        layer_out = row_sum([middle, shared_out, out_own[0], out_other[0], out_moved_three])
        more = [shift_outer(shared_z[d], "exp", d) for d in range(2, levels)]
        gains = jnp.stack(
            [attn_gain_grad.reshape(devices, -1), ffn_gain_grad.reshape(devices, -1)], axis=1
        )
        gains = lax.all_to_all(gains, BOTH, split_axis=0, concat_axis=0, tiled=True)
        return mine_x(total), over_x(total), got, layer_out, more, gains

    total, total_x, got, layer_out, more, gains = region(dense_three)
    shared_parts += more
    arrived.append(got)

    def dense_four():
        grads = expert_out(expert_total(pos, kept_own, got_own, pieces, arrived), inner)
        shape = lambda v: (v.shape[0] // (n_ctx * n_exp), v.shape[1])
        shared = shared_grads(
            shared_parts, shape(shared_gate), shape(shared_down)
        )
        dense = dense_out(over_z(pos, total, total_x), x.shape[1])
        return jnp.sum(gains, axis=0), shared, dense, grads

    gains, (sum_gate, sum_up, sum_down), dense, expert_grads = region(dense_four)
    sum_out, sum_query, sum_key, sum_value = dense
    return (
        layer_out[None],
        input_grad[None],
        gains[0],
        sum_query,
        sum_key,
        sum_value,
        sum_out,
        gains[1],
        sum_gate,
        sum_up,
        sum_down,
        *expert_grads,
    )


def solution(mesh):
    return jax.shard_map(
        shards,
        mesh=mesh,
        in_specs=(
            P("exp", "ctx", None),
            P(),
            P(),
            P(),
            P(),
            P(),
            P(),
            P(),
            P(),
            P(),
            P("exp", None, None),
            P("exp", None, None),
            P("exp", None, None),
            P("exp", "ctx", None),
            P("exp", "ctx", None),
            P(),
            P("exp", "ctx", None),
        ),
        out_specs=(
            P("exp", "ctx", None),
            P("exp", "ctx", None),
            P(("ctx", "exp")),
            P(("ctx", "exp"), None),
            P(("ctx", "exp"), None),
            P(("ctx", "exp"), None),
            P(("ctx", "exp"), None),
            P(("ctx", "exp")),
            P(("ctx", "exp"), None),
            P(("ctx", "exp"), None),
            P(("ctx", "exp"), None),
            P("exp", "ctx", None),
            P("exp", "ctx", None),
            P("exp", None, "ctx"),
        ),
        check_vma=False,
    )
```

```python
import functools

import jax
import jax.numpy as jnp
from jax import lax
from jax.experimental import pallas as pl
from jax.experimental.pallas import tpu as pltpu
from jax.sharding import PartitionSpec as P

H = 12
HD = 128
KVH = 4
GROUPS = H // KVH
EPSILON = 1e-06
GATE_LANES = 128
LOW_LANE = 64
NEGATIVE = -1e30
SCALE = HD ** (-0.5)
BOTH = ("ctx", "exp")
VMEM_LIMIT = 60 * 2**20
bf16 = jnp.bfloat16
f32 = jnp.float32


def dot(left_op, right_op):
    return jnp.dot(left_op, right_op, preferred_element_type=f32)


def dot_nt(left_op, right_op):
    return lax.dot_general(left_op, right_op, (((1,), (1,)), ((), ())), preferred_element_type=f32)


def dot_tn(left_op, right_op):
    return lax.dot_general(left_op, right_op, (((0,), (0,)), ((), ())), preferred_element_type=f32)


def whole(shape):
    return pl.BlockSpec(shape, lambda *_: (0,) * len(shape))


def params():
    return pltpu.CompilerParams(vmem_limit_bytes=VMEM_LIMIT)


def anywhere(count):
    return [pl.BlockSpec(memory_space=pl.ANY)] * count


def cost(flops, nbytes):
    return pl.CostEstimate(flops=flops // 4, bytes_accessed=nbytes // 4, transcendentals=0)


def keyvalue_kernel(x_ref, gain_ref, wk_ref, wv_ref, normed_ref, kv_ref):
    @pl.when(pl.program_id(0) == 0)
    def _():
        x = x_ref[...].astype(f32)
        factor = lax.rsqrt(jnp.mean(x * x, axis=-1, keepdims=True) + EPSILON)
        normed_ref[...] = (x * factor * gain_ref[...]).astype(bf16)

    both = jnp.concatenate([wk_ref[...], wv_ref[...]], axis=1)
    kv_ref[...] = dot(normed_ref[...], both).astype(bf16)


def keyvalue(x, gain, wk, wv):
    rows, width = x.shape
    return pl.pallas_call(
        keyvalue_kernel,
        grid=(KVH,),
        in_specs=[
            whole((rows, width)),
            whole((1, width)),
            pl.BlockSpec((width, HD), lambda g: (0, g)),
            pl.BlockSpec((width, HD), lambda g: (0, g)),
        ],
        out_specs=[whole((rows, width)), pl.BlockSpec((rows, 2 * HD), lambda g: (0, g))],
        out_shape=[
            jax.ShapeDtypeStruct((rows, width), bf16),
            jax.ShapeDtypeStruct((rows, 2 * KVH * HD), bf16),
        ],
        compiler_params=params(),
        cost_estimate=cost(4 * rows * width * KVH * HD, 5 * 2**20),
    )(x, gain.reshape(1, width), wk, wv)


def stack_heads(ref):
    return jnp.concatenate([ref[:, r * HD : (r + 1) * HD] for r in range(GROUPS)], axis=0)


def places(pos, spans, block, shape, dim, rows):
    outer, side = (0, 0) if block is None else (block // 2, block % 2)
    ring = spans.shape[0] // 4
    owner = 2 * lax.rem(pos[0] + ring - outer, ring) + lax.rem(pos[1] + side, 2)
    row = lax.broadcasted_iota(jnp.int32, shape, dim) % rows
    half = rows // 2
    first, second = spans[2 * owner] * half, spans[2 * owner + 1] * half
    return jnp.where(row < half, first + row, second + row - half)


def attend_kernel(blocks, extra, pos, spans, q_ref, *refs):
    kv_refs = refs[:blocks]
    out_ref, lse_ref, score_ref = refs[blocks + extra :]
    rows = q_ref.shape[0]
    queries = stack_heads(q_ref)
    wanted = places(pos, spans, None, (1, GROUPS * rows), 1, rows)
    peak = jnp.full((1, GROUPS * rows), NEGATIVE, f32)
    for b in range(blocks):
        scores = dot_nt(kv_refs[b][:, :HD], queries) * SCALE
        visible = places(pos, spans, b, (rows, 1), 0, rows) <= wanted
        scores = jnp.where(visible, scores, NEGATIVE)
        score_ref[b * rows : (b + 1) * rows, :] = scores
        peak = jnp.maximum(peak, jnp.max(scores, axis=0, keepdims=True))
    total = jnp.zeros_like(peak)
    mixed = jnp.zeros((HD, GROUPS * rows), f32)
    for b in range(blocks):
        weights = jnp.exp(score_ref[b * rows : (b + 1) * rows, :] - peak)
        total = total + jnp.sum(weights, axis=0, keepdims=True)
        mixed = mixed + dot_tn(kv_refs[b][:, HD:], weights.astype(bf16))
    lse_ref[0] = peak + jnp.log(total)
    mixed = jnp.transpose(mixed / total)
    for r in range(GROUPS):
        out_ref[:, r * HD : (r + 1) * HD] = mixed[r * rows : (r + 1) * rows].astype(bf16)


def attend(pos, spans, queries, kv_blocks, after=()):
    rows = queries.shape[0]
    blocks = len(kv_blocks)
    wide = GROUPS * HD
    return pl.pallas_call(
        functools.partial(attend_kernel, blocks, len(after)),
        grid_spec=pltpu.PrefetchScalarGridSpec(
            num_scalar_prefetch=2,
            grid=(KVH,),
            in_specs=[pl.BlockSpec((rows, wide), lambda g, *_: (0, g))]
            + [pl.BlockSpec((rows, 2 * HD), lambda g, *_: (0, g))] * blocks
            + anywhere(len(after)),
            out_specs=[
                pl.BlockSpec((rows, wide), lambda g, *_: (0, g)),
                pl.BlockSpec((1, 1, GROUPS * rows), lambda g, *_: (g, 0, 0)),
            ],
            scratch_shapes=[pltpu.VMEM((blocks * rows, GROUPS * rows), f32)],
        ),
        out_shape=[
            jax.ShapeDtypeStruct((rows, H * HD), bf16),
            jax.ShapeDtypeStruct((KVH, 1, GROUPS * rows), f32),
        ],
        compiler_params=params(),
        cost_estimate=cost(8 * rows * rows * blocks * H * HD, 4 * 2**20),
    )(pos, spans, queries, *kv_blocks, *after)


def attend_back_kernel(blocks, extra, pos, spans, q_ref, grad_ref, lse_ref, *refs):
    kv_refs = refs[:blocks]
    dq_ref, same_ref, other_ref = refs[blocks + extra : -2]
    prob_ref, slope_ref = refs[-2:]
    rows = q_ref.shape[0]
    queries = stack_heads(q_ref)
    grads = stack_heads(grad_ref)
    wanted = places(pos, spans, None, (1, GROUPS * rows), 1, rows)
    lse = lse_ref[0]
    delta = jnp.zeros((1, GROUPS * rows), f32)
    for b in range(blocks):
        part = slice(b * rows, (b + 1) * rows)
        scores = dot_nt(kv_refs[b][:, :HD], queries) * SCALE - lse
        visible = places(pos, spans, b, (rows, 1), 0, rows) <= wanted
        prob = jnp.exp(jnp.where(visible, scores, NEGATIVE))
        slope = dot_nt(kv_refs[b][:, HD:], grads)
        delta = delta + jnp.sum(prob * slope, axis=0, keepdims=True)
        prob_ref[part, :] = prob
        slope_ref[part, :] = slope
        dkv_ref = other_ref if b % 2 else same_ref
        dkv_ref[rows * (b // 2) : rows * (b // 2 + 1), HD:] = dot(prob.astype(bf16), grads).astype(bf16)
    query_grad = jnp.zeros((HD, GROUPS * rows), f32)
    for b in range(blocks):
        part = slice(b * rows, (b + 1) * rows)
        dscore = (prob_ref[part, :] * (slope_ref[part, :] - delta) * SCALE).astype(bf16)
        dkv_ref = other_ref if b % 2 else same_ref
        dkv_ref[rows * (b // 2) : rows * (b // 2 + 1), :HD] = dot(dscore, queries).astype(bf16)
        query_grad = query_grad + dot_tn(kv_refs[b][:, :HD], dscore)
    query_grad = jnp.transpose(query_grad)
    for r in range(GROUPS):
        dq_ref[:, r * HD : (r + 1) * HD] = query_grad[r * rows : (r + 1) * rows].astype(bf16)


def attend_back(pos, spans, queries, grads, lse, kv_blocks, after=()):
    rows = queries.shape[0]
    blocks = len(kv_blocks)
    wide = GROUPS * HD
    by_group = pl.BlockSpec((rows, wide), lambda g, *_: (0, g))
    kv_spec = pl.BlockSpec((rows, 2 * HD), lambda g, *_: (0, g))
    return pl.pallas_call(
        functools.partial(attend_back_kernel, blocks, len(after)),
        grid_spec=pltpu.PrefetchScalarGridSpec(
            num_scalar_prefetch=2,
            grid=(KVH,),
            in_specs=[
                by_group,
                by_group,
                pl.BlockSpec((1, 1, GROUPS * rows), lambda g, *_: (g, 0, 0)),
            ]
            + [kv_spec] * blocks
            + anywhere(len(after)),
            out_specs=[by_group]
            + [pl.BlockSpec((blocks // 2 * rows, 2 * HD), lambda g, *_: (0, g))] * 2,
            scratch_shapes=[pltpu.VMEM((blocks * rows, GROUPS * rows), f32)] * 2,
        ),
        out_shape=[jax.ShapeDtypeStruct((rows, H * HD), bf16)]
        + [jax.ShapeDtypeStruct((blocks // 2 * rows, 2 * KVH * HD), bf16)] * 2,
        compiler_params=params(),
        cost_estimate=cost(20 * rows * rows * blocks * H * HD, 8 * 2**20),
    )(pos, spans, queries, grads, lse, *kv_blocks, *after)


def middle_kernel(x_ref, att_ref, w_ref, gain_ref, middle_ref, rows_ref):
    step = pl.program_id(0)
    tile = w_ref.shape[1]
    columns = pl.ds(pl.multiple_of(step * tile, tile), tile)
    middle_ref[:, columns] = x_ref[...].astype(f32) + dot(att_ref[...], w_ref[...])

    @pl.when(step == pl.num_programs(0) - 1)
    def _():
        middle = middle_ref[...]
        factor = lax.rsqrt(jnp.mean(middle * middle, axis=-1, keepdims=True) + EPSILON)
        rows_ref[...] = (middle * factor * gain_ref[...]).astype(bf16)


def middle_forward(x, attended, w_out, gain, tile=512):
    rows, width = x.shape
    return pl.pallas_call(
        middle_kernel,
        grid=(width // tile,),
        in_specs=[
            pl.BlockSpec((rows, tile), lambda n: (0, n)),
            whole(attended.shape),
            pl.BlockSpec((w_out.shape[0], tile), lambda n: (0, n)),
            whole((1, width)),
        ],
        out_specs=[whole((rows, width))] * 2,
        out_shape=[
            jax.ShapeDtypeStruct((rows, width), f32),
            jax.ShapeDtypeStruct((rows, width), bf16),
        ],
        compiler_params=params(),
        cost_estimate=cost(2 * rows * width * width, 8 * 2**20),
    )(x, attended, w_out, gain.reshape(1, width))


def middle_back_kernel(parts, *refs):
    grad_refs = refs[:parts]
    middle_ref, cot_ref, gain_ref, w_ref = refs[parts : parts + 4]
    mgrad_ref, low_ref, dgain_ref, out_ref = refs[-4:]

    @pl.when(pl.program_id(0) == 0)
    def _():
        upstream = grad_refs[0][...].astype(f32)
        for ref in grad_refs[1:]:
            upstream = upstream + ref[...].astype(f32)
        middle = middle_ref[...]
        factor = lax.rsqrt(jnp.mean(middle * middle, axis=-1, keepdims=True) + EPSILON)
        scaled = upstream * gain_ref[...]
        inner = jnp.mean(scaled * middle, axis=-1, keepdims=True)
        grad = factor * scaled - middle * (factor * factor * factor * inner)
        grad = cot_ref[...].astype(f32) + grad
        mgrad_ref[...] = grad
        low_ref[...] = grad.astype(bf16)
        dgain_ref[...] = jnp.sum(upstream * middle * factor, axis=0, keepdims=True)

    out_ref[...] = dot_nt(low_ref[...], w_ref[...]).astype(bf16)


def middle_back(grads, middle, cotangent, gain, w_out, after=(), tile=512):
    rows, width = middle.shape
    inner = w_out.shape[0]
    return pl.pallas_call(
        functools.partial(middle_back_kernel, len(grads)),
        grid=(inner // tile,),
        in_specs=[whole((rows, width))] * (len(grads) + 2)
        + [whole((1, width)), pl.BlockSpec((tile, width), lambda n: (n, 0))]
        + anywhere(len(after)),
        out_specs=[
            whole((rows, width)),
            whole((rows, width)),
            whole((1, width)),
            pl.BlockSpec((rows, tile), lambda n: (0, n)),
        ],
        out_shape=[
            jax.ShapeDtypeStruct((rows, width), f32),
            jax.ShapeDtypeStruct((rows, width), bf16),
            jax.ShapeDtypeStruct((1, width), f32),
            jax.ShapeDtypeStruct((rows, inner), bf16),
        ],
        compiler_params=params(),
        cost_estimate=cost(2 * rows * width * inner, 16 * 2**20),
    )(*grads, middle, cotangent, gain.reshape(1, width), w_out, *after)


def input_back_kernel(dq_ref, dkv_ref, wq_ref, wk_ref, wv_ref, x_ref, gain_ref, mgrad_ref, *refs):
    out_ref, dgain_ref = refs[-2:]
    step = pl.program_id(0)
    term = dot_nt(dq_ref[...], wq_ref[...])
    term = term + dot_nt(dkv_ref[:, :HD], wk_ref[...]) + dot_nt(dkv_ref[:, HD:], wv_ref[...])

    @pl.when(step == 0)
    def _():
        out_ref[...] = term

    @pl.when(step > 0)
    def _():
        out_ref[...] += term

    @pl.when(step == pl.num_programs(0) - 1)
    def _():
        upstream = out_ref[...]
        x = x_ref[...].astype(f32)
        factor = lax.rsqrt(jnp.mean(x * x, axis=-1, keepdims=True) + EPSILON)
        scaled = upstream * gain_ref[...]
        inner = jnp.mean(scaled * x, axis=-1, keepdims=True)
        out_ref[...] = mgrad_ref[...] + factor * scaled - x * (factor * factor * factor * inner)
        dgain_ref[...] = jnp.sum(upstream * x * factor, axis=0, keepdims=True)


def input_back(dq, dkv, wq, wk, wv, x, gain, mgrad, after=()):
    rows, width = x.shape
    wide = GROUPS * HD
    return pl.pallas_call(
        input_back_kernel,
        grid=(KVH,),
        in_specs=[
            pl.BlockSpec((rows, wide), lambda g: (0, g)),
            pl.BlockSpec((rows, 2 * HD), lambda g: (0, g)),
            pl.BlockSpec((width, wide), lambda g: (0, g)),
            pl.BlockSpec((width, HD), lambda g: (0, g)),
            pl.BlockSpec((width, HD), lambda g: (0, g)),
            whole((rows, width)),
            whole((1, width)),
            whole((rows, width)),
        ]
        + anywhere(len(after)),
        out_specs=[whole((rows, width)), whole((1, width))],
        out_shape=[
            jax.ShapeDtypeStruct((rows, width), f32),
            jax.ShapeDtypeStruct((1, width), f32),
        ],
        compiler_params=params(),
        cost_estimate=cost(2 * rows * width * (H + 2 * KVH) * HD, 14 * 2**20),
    )(dq, dkv, wq, wk, wv, x, gain.reshape(1, width), mgrad, *after)


def gate_column(expert, gates):
    lanes = lax.broadcasted_iota(jnp.int32, gates.shape, 1)
    chosen = (lanes == expert) | (lanes == expert + LOW_LANE)
    return jnp.sum(jnp.where(chosen, gates.astype(f32), 0.0), axis=1, keepdims=True)


def experts_kernel(count, per, gated, extra, pos, *refs):
    x_refs, c_refs, weights = refs[:count], refs[count : 2 * count], refs[2 * count : 2 * count + 3]
    *outs, acc_o, acc_g = refs[2 * count + 3 + extra :]
    out_refs, grad_refs, kept_refs = outs[:count], outs[count : 2 * count], outs[2 * count :]
    wg_ref, wu_ref, wd_ref = weights
    hid_ref, dgu_ref = kept_refs[-2:]
    step = pl.program_id(0)
    last = pl.num_programs(0) - 1
    rows, width = x_refs[0].shape
    chunk = wg_ref.shape[1]
    parts = [slice(b * rows, (b + 1) * rows) for b in range(count)]
    if gated:

        @pl.when(step == 0)
        def _():
            for part, x_ref, c_ref in zip(parts, x_refs, c_refs):
                kept_refs[0][part, :] = x_ref[...]
                kept_refs[1][part, :] = c_ref[...]

    for part, x_ref, c_ref in zip(parts, x_refs, c_refs):
        x = x_ref[...]
        gate = dot(x, wg_ref[...])
        up = dot(x, wu_ref[...])
        slope = dot_nt(c_ref[:, :width], wd_ref[...])
        sigmoid = 1.0 / (1.0 + jnp.exp(-gate))
        act = gate * sigmoid
        hidden = act * up
        if gated:
            held = pl.num_programs(0) // per
            expert = (2 * pos[2] + pos[3]) * held + step // per
            weight = gate_column(expert, c_ref[:, width:])
            hidden = hidden * weight
            slope = slope * weight
        hidden = hidden.astype(bf16)
        dg = (slope * up * (sigmoid * (1.0 + gate * (1.0 - sigmoid)))).astype(bf16)
        du = (slope * act).astype(bf16)
        hid_ref[part, :] = hidden
        dgu_ref[part, :chunk] = dg
        dgu_ref[part, chunk:] = du
        out_term = dot(hidden, wd_ref[...])
        both = jnp.concatenate([wg_ref[...], wu_ref[...]], axis=1)
        grad_term = dot_nt(jnp.concatenate([dg, du], axis=1), both)

        @pl.when(step == 0)
        def _():
            acc_o[part, :] = out_term
            acc_g[part, :] = grad_term

        @pl.when(step > 0)
        def _():
            acc_o[part, :] += out_term
            acc_g[part, :] += grad_term

    @pl.when(step == last)
    def _():
        for part, out_ref, grad_ref in zip(parts, out_refs, grad_refs):
            out_ref[...] = acc_o[part, :].astype(out_ref.dtype)
            grad_ref[...] = acc_g[part, :].astype(grad_ref.dtype)


def experts(pos, xs, cs, weights, part, parts, kept, gated, kind, chunk=256):
    count = len(xs)
    rows, width = xs[0].shape
    taken = count * rows
    inner = weights[2].shape[1]
    per = inner // chunk
    steps = weights[0].shape[0] * per
    specs = [
        pl.BlockSpec((None, width, chunk), lambda i, _: (i // per, 0, i % per)),
        pl.BlockSpec((None, width, chunk), lambda i, _: (i // per, 0, i % per)),
        pl.BlockSpec((None, chunk, width), lambda i, _: (i // per, i % per, 0)),
    ]
    all_rows = parts * taken
    collected = [
        jax.ShapeDtypeStruct((all_rows, steps * chunk), bf16),
        jax.ShapeDtypeStruct((all_rows, 2 * steps * chunk), bf16),
    ]
    collected_specs = [
        pl.BlockSpec((taken, chunk), lambda i, _: (part, i)),
        pl.BlockSpec((taken, 2 * chunk), lambda i, _: (part, i)),
    ]
    if gated:
        collected = [
            jax.ShapeDtypeStruct((all_rows, width), bf16),
            jax.ShapeDtypeStruct((all_rows, cs[0].shape[1]), bf16),
        ] + collected
        collected_specs = [
            pl.BlockSpec((taken, width), lambda i, _: (part, 0)),
            pl.BlockSpec((taken, cs[0].shape[1]), lambda i, _: (part, 0)),
        ] + collected_specs
    operands = [pos, *xs, *cs, *weights]
    aliases = {}
    if kept is not None:
        aliases = {len(operands) + j: 2 * count + j for j in range(len(collected))}
        operands += list(kept)
    extra = 0 if kept is None else len(collected)
    result = pl.pallas_call(
        functools.partial(experts_kernel, count, per, gated, extra),
        grid_spec=pltpu.PrefetchScalarGridSpec(
            num_scalar_prefetch=1,
            grid=(steps,),
            in_specs=[whole((rows, width))] * count + [whole(cs[0].shape)] * count + specs + anywhere(extra),
            out_specs=[whole((rows, width))] * (2 * count) + collected_specs,
            scratch_shapes=[pltpu.VMEM((taken, width), f32)] * 2,
        ),
        out_shape=[jax.ShapeDtypeStruct((rows, width), kind)] * (2 * count) + collected,
        input_output_aliases=aliases,
        compiler_params=params(),
        cost_estimate=cost(26 * taken * width * steps * chunk, 12 * 2**20),
    )(*operands)
    return result[:count], result[count : 2 * count], result[2 * count :]


def others_kernel(sets, per, bands, extra, pos, x_ref, c_ref, *refs):
    each = bands + per
    weights = [refs[t * each : (t + 1) * each] for t in range(sets)]
    *result_refs, hid_ref, dgu_ref = refs[sets * each + extra :]
    out_refs, grad_refs = result_refs[: len(result_refs) // 2], result_refs[len(result_refs) // 2 :]
    step = pl.program_id(0)
    width = x_ref.shape[1]
    band = width // bands
    chunk = weights[0][bands].shape[0]
    rows = out_refs[0].shape[0]

    def places(t, n):
        at = (lax.rem(pos[1] + t, 2) * per + n) * chunk
        cut = lambda first: pl.ds(pl.multiple_of(first, chunk), chunk)
        return cut(at), cut(2 * at), cut(2 * at + chunk)

    def columns(n):
        return slice(n * chunk, (n + 1) * chunk), slice((per + n) * chunk, (per + n + 1) * chunk)

    def hidden_chunk(t, n):
        at_hidden, at_gate, at_up = places(t, n)
        gate_cut, up_cut = columns(n)
        expert = (2 * pos[2] + 1 - pos[3]) * sets + lax.rem(pos[1] + t, 2)
        joined = lambda cut: jnp.concatenate([weights[t][k][:, cut] for k in range(bands)], axis=0)
        x = x_ref[...]
        gate = dot(x, joined(gate_cut))
        up = dot(x, joined(up_cut))
        slope = dot_nt(c_ref[:, :width], weights[t][bands + n][...])
        sigmoid = 1.0 / (1.0 + jnp.exp(-gate))
        act = gate * sigmoid
        weight = gate_column(expert, c_ref[:, width:])
        slope = slope * weight
        hid_ref[:, at_hidden] = (act * up * weight).astype(bf16)
        dgu_ref[:, at_gate] = (slope * up * (sigmoid * (1.0 + gate * (1.0 - sigmoid)))).astype(bf16)
        dgu_ref[:, at_up] = (slope * act).astype(bf16)

    def results(k):
        out = grad = 0.0
        for t in range(sets):
            inner = per * chunk
            first = lax.rem(pos[1] + t, 2) * inner
            own = lambda ref, by: ref[:, pl.ds(pl.multiple_of(by * first, by * inner), by * inner)]
            down = [weights[t][bands + n][:, k * band : (k + 1) * band] for n in range(per)]
            both = [weights[t][k][:, cut] for n in range(per) for cut in columns(n)]
            out = out + dot(own(hid_ref, 1), jnp.concatenate(down, axis=0))
            grad = grad + dot_nt(own(dgu_ref, 2), jnp.concatenate(both, axis=1))
        for p in range(len(out_refs)):
            out_refs[p][...] = out[p * rows : (p + 1) * rows].astype(bf16)
            grad_refs[p][...] = grad[p * rows : (p + 1) * rows].astype(bf16)

    for t in range(sets):
        for n in range(per):
            pl.when(step == t * per + n)(functools.partial(hidden_chunk, t, n))
    for k in range(bands):
        pl.when(step == sets * per + k)(functools.partial(results, k))


def others(pos, x, c, weights, part, parts, count, kept):
    taken, width = x.shape[0] // parts, x.shape[1]
    sets = len(weights)
    bands, downs = weights[0]
    per = len(downs)
    inner = per * downs[0].shape[0]
    flat = [v for bands_t, downs_t in weights for v in [*bands_t, *downs_t]]
    tile = width // len(bands)
    rows_spec = lambda v: pl.BlockSpec(
        (taken, v.shape[1]), lambda *_: (part, 0), pipeline_mode=pl.Buffered(1)
    )
    resident = lambda v: pl.BlockSpec(v.shape, lambda *_: (0, 0), pipeline_mode=pl.Buffered(1))
    late = lambda i: jnp.maximum(i - sets * per, 0)
    operands = [pos, x, c] + flat
    extra = 0 if kept is None else 2
    aliases = {len(operands) + j: 2 * count + j for j in range(extra)}
    collected = [sets * inner, 2 * sets * inner]
    result = pl.pallas_call(
        functools.partial(others_kernel, sets, per, len(bands), extra),
        grid_spec=pltpu.PrefetchScalarGridSpec(
            num_scalar_prefetch=1,
            grid=(sets * per + len(bands),),
            in_specs=[rows_spec(x), rows_spec(c)] + [resident(v) for v in flat] + anywhere(extra),
            out_specs=[pl.BlockSpec((taken // count, tile), lambda i, _: (0, late(i)))] * (2 * count)
            + [pl.BlockSpec((taken, n), lambda *_: (part, 0)) for n in collected],
        ),
        out_shape=[jax.ShapeDtypeStruct((taken // count, width), bf16)] * (2 * count)
        + [jax.ShapeDtypeStruct((parts * taken, n), bf16) for n in collected],
        input_output_aliases=aliases,
        compiler_params=params(),
        cost_estimate=cost(26 * taken * width * sets * inner, 12 * 2**20),
    )(*operands, *(kept or []))
    return result[:count], result[count : 2 * count], result[2 * count :]


def side_of(outer, s, pos):
    return 2 * lax.rem(s, outer) + lax.rem(pos[1] + 1 - s // outer, 2)


def halves_kernel(shape, outer, pos, *refs):
    sent_ref, kept_ref = refs[-2:]

    def write(out_ref):
        first = 0
        for i, rows in enumerate(shape):
            total = dot_tn(refs[2 * i][...], refs[2 * i + 1][...]).astype(bf16)
            blank = out_ref.shape[2] - total.shape[1]
            if blank:
                out_ref[:, first : first + rows, total.shape[1] :] = jnp.zeros(
                    (out_ref.shape[0], rows, blank), bf16
                )
            for e in range(out_ref.shape[0]):
                part = total[e * rows : (e + 1) * rows]
                out_ref[e, first : first + rows, : total.shape[1]] = part
            first += rows

    pl.when(pl.program_id(0) < outer)(lambda: write(sent_ref))
    pl.when(pl.program_id(0) >= outer)(lambda: write(kept_ref))


def halves(pos, pairs, after=()):
    n_ctx, n_exp = lax.axis_size("ctx"), lax.axis_size("exp")
    outer = n_ctx // 2
    shape = [left.shape[1] // (n_ctx * n_exp) for left, _ in pairs]
    wide = max(right.shape[1] for _, right in pairs)
    full = (outer * n_exp, sum(shape), wide)
    if any((left.shape[1] // n_ctx) % 128 for left, _ in pairs):
        out = []
        for side in (1, 0):
            parts = []
            for left, right in pairs:
                split = left.reshape(left.shape[0], outer, 2, -1)
                mine = lax.dynamic_index_in_dim(split, (pos[1] + side) % 2, 2, keepdims=False)
                total = dot_tn(mine.reshape(left.shape[0], -1), right).astype(bf16)
                total = total.reshape(outer * n_exp, -1, right.shape[1])
                parts.append(jnp.pad(total, ((0, 0), (0, 0), (0, wide - right.shape[1]))))
            joined = jnp.concatenate(parts, axis=1)
            out.append(jnp.pad(joined, ((0, 0), (0, -joined.shape[1] % 16), (0, 0))))
        return out
    in_specs, operands = [], []
    for left, right in pairs:
        columns = left.shape[1] // n_ctx
        in_specs.append(
            pl.BlockSpec((left.shape[0], columns), lambda s, pos: (0, side_of(outer, s, pos)))
        )
        in_specs.append(whole(right.shape))
        operands += [left, right]
    block = (n_exp,) + full[1:]
    flops = sum(2 * left.size * right.shape[1] for left, right in pairs)
    return pl.pallas_call(
        functools.partial(halves_kernel, shape, outer),
        grid_spec=pltpu.PrefetchScalarGridSpec(
            num_scalar_prefetch=1,
            grid=(2 * outer,),
            in_specs=in_specs + anywhere(len(after)),
            out_specs=[
                pl.BlockSpec(block, lambda s, pos: (jnp.minimum(s, outer - 1), 0, 0)),
                pl.BlockSpec(block, lambda s, pos: (jnp.maximum(s - outer, 0), 0, 0)),
            ],
        ),
        out_shape=[jax.ShapeDtypeStruct(full, bf16)] * 2,
        compiler_params=params(),
        cost_estimate=cost(2 * flops, 8 * 2**20),
    )(pos, *operands, *after)


def rows_product_kernel(blocks, pos, *refs):
    left = jnp.concatenate([ref[...] for ref in refs[:blocks]], axis=0)
    right = jnp.concatenate([ref[...] for ref in refs[blocks : 2 * blocks]], axis=0)
    refs[-1][...] = dot_tn(left, right).astype(bf16)


def rows_product(pos, lefts, rights, tile=512):
    n_ctx, n_exp = lax.axis_size("ctx"), lax.axis_size("exp")
    depth, height = lefts[0][0].shape
    high, wide = height // n_ctx, rights[0][0].shape[1]
    if high % 128:
        place = lax.axis_index("ctx") * high
        cut = lambda v: lax.slice_in_dim(v[0], v[1] * depth, (v[1] + 1) * depth, axis=0)
        total = sum(
            dot_tn(lax.dynamic_slice_in_dim(cut(a), place, high, 1), cut(b))
            for a, b in zip(lefts, rights)
        )
        return total.astype(bf16).reshape(n_exp, -1, wide)
    blocks = len(lefts)
    left_specs = [
        pl.BlockSpec((depth, high), functools.partial(lambda k, n, pos: (k, 2 * pos[0] + pos[1]), k))
        for _, k in lefts
    ]
    right_specs = [
        pl.BlockSpec((depth, tile), functools.partial(lambda k, n, pos: (k, n), k)) for _, k in rights
    ]
    total = pl.pallas_call(
        functools.partial(rows_product_kernel, blocks),
        grid_spec=pltpu.PrefetchScalarGridSpec(
            num_scalar_prefetch=1,
            grid=(wide // tile,),
            in_specs=left_specs + right_specs,
            out_specs=pl.BlockSpec((high, tile), lambda n, pos: (0, n)),
        ),
        out_shape=jax.ShapeDtypeStruct((high, wide), bf16),
        compiler_params=params(),
        cost_estimate=cost(4 * blocks * depth * high * wide, 4 * 2**20),
    )(pos, *[v for v, _ in lefts], *[v for v, _ in rights])
    return total.reshape(n_exp, -1, wide)


def expert_halves_kernel(blocks, tiles, pos, *refs):
    rows_refs, cot_refs = refs[:blocks], refs[blocks : 2 * blocks]
    dgu_ref, hid_ref, sent_ref, kept_ref = refs[2 * blocks :]
    n = pl.program_id(0)
    high = sent_ref.shape[1]

    def write(left_refs, right_ref):
        left = jnp.concatenate([ref[...] for ref in left_refs], axis=1)
        total = dot_tn(left, right_ref[...]).astype(bf16)
        count = sent_ref.shape[0]
        for i in range(count):
            sent_ref[i] = total[i * high : (i + 1) * high]
            kept_ref[i] = total[(count + i) * high : (count + i + 1) * high]

    pl.when(n < tiles)(lambda: write(rows_refs, dgu_ref))
    pl.when(n >= tiles)(lambda: write(cot_refs, hid_ref))


def expert_steps(width):
    high = width // lax.axis_size("ctx")
    return high // 128 if high % 128 == 0 else 1


def expert_halves(pos, rows_all, cot_all, dgu, hid, tile=512):
    n_ctx = lax.axis_size("ctx")
    depth, width = rows_all.shape
    high = width // n_ctx
    wide = dgu.shape[1] + hid.shape[1]
    steps = expert_steps(width)
    if high % 128:
        out = []
        for side in (1, 0):
            place = lambda y: (2 * y + (pos[1] + side) % 2) * high
            pick = lambda v: jnp.concatenate(
                [lax.dynamic_slice_in_dim(v, place(y), high, 1) for y in range(n_ctx // 2)], axis=1
            )
            parts = [dot_tn(pick(v), w).astype(bf16) for v, w in ((rows_all, dgu), (cot_all, hid))]
            out.append(jnp.concatenate(parts, axis=1).reshape(n_ctx // 2 * steps, -1, wide))
        return out
    tiles, down = dgu.shape[1] // tile, hid.shape[1] // tile
    left_specs = [
        pl.BlockSpec((depth, high), functools.partial(lambda s, n, pos: (0, side_of(n_ctx // 2, s, pos)), s))
        for s in range(n_ctx)
    ]
    block = (n_ctx // 2 * steps, high // steps, tile)
    return pl.pallas_call(
        functools.partial(expert_halves_kernel, n_ctx, tiles),
        grid_spec=pltpu.PrefetchScalarGridSpec(
            num_scalar_prefetch=1,
            grid=(tiles + down,),
            in_specs=left_specs * 2
            + [
                pl.BlockSpec((depth, tile), lambda n, pos: (0, jnp.minimum(n, tiles - 1))),
                pl.BlockSpec((depth, tile), lambda n, pos: (0, jnp.maximum(n - tiles, 0))),
            ],
            out_specs=[pl.BlockSpec(block, lambda n, pos: (0, 0, n))] * 2,
        ),
        out_shape=[jax.ShapeDtypeStruct(block[:2] + (wide,), bf16)] * 2,
        compiler_params=params(),
        cost_estimate=cost(4 * depth * width * wide, 16 * 2**20),
    )(pos, *[rows_all] * n_ctx, *[cot_all] * n_ctx, dgu, hid)


def sums_kernel(shape, only, extra, pos, *refs):
    ins, outs = refs[: sum(shape)], refs[sum(shape) + extra :]
    at = 0
    for count, out in zip(shape, outs):
        total = ins[at][...].astype(f32)
        for k in range(at + 1, at + count):
            term = ins[k][...].astype(f32)
            if only[k] is not None:
                term = jnp.where(pl.program_id(0) == only[k], term, 0.0)
            total = total + term
        out[...] = total.astype(out.dtype)
        at += count


def sums(pos, steps, outputs, after=()):
    operands, in_specs, out_specs, out_shape, only = [], [], [], [], []
    for kind, block, terms in outputs:
        for array, index, *step in terms:
            operands.append(array)
            only.append(step[0] if step else None)
            in_specs.append(pl.BlockSpec(block, functools.partial(place_of, index)))
        out_specs.append(pl.BlockSpec(block, lambda i, pos: (i, 0, 0)))
        out_shape.append(jax.ShapeDtypeStruct((steps * block[0],) + tuple(block[1:]), kind))
    return pl.pallas_call(
        functools.partial(sums_kernel, [len(terms) for _, _, terms in outputs], only, len(after)),
        grid_spec=pltpu.PrefetchScalarGridSpec(
            num_scalar_prefetch=1,
            grid=(steps,),
            in_specs=in_specs + anywhere(len(after)),
            out_specs=out_specs,
        ),
        out_shape=out_shape,
        compiler_params=params(),
        cost_estimate=cost(0, 8 * 2**20),
    )(pos, *operands, *after)


def place_of(index, i, pos):
    at = index(i, pos)
    return at if isinstance(at, tuple) else (at, 0, 0)


def straight(i, pos):
    return i


def row_sum(terms, kind=bf16):
    total = terms[0].astype(f32)
    for term in terms[1:]:
        total = total + term.astype(f32)
    return total.astype(kind)


def expert_out_kernel(gates, each, *refs):
    in_refs, (gate_ref, up_ref, down_ref) = refs[:4], refs[4:]
    n = pl.program_id(0)

    def write(ref):
        @pl.when((n < gates) & (lax.rem(n, 2) == 0))
        def _():
            gate_ref[0] = ref[...].astype(f32)

        @pl.when((n < gates) & (lax.rem(n, 2) == 1))
        def _():
            up_ref[0] = ref[...].astype(f32)

        @pl.when(n >= gates)
        def _():
            down_ref[0] = jnp.transpose(ref[...].astype(f32))

    for q in range(4):
        pl.when(n // each == q)(functools.partial(write, in_refs[q]))


def expert_out(quarters, inner, chunk=256):
    rows, wide = quarters[0].shape
    each = wide // chunk
    held = 4 * wide // (3 * inner)
    per = inner // chunk
    gates = 2 * held * per
    tile = lambda n: jnp.minimum(n, gates - 1) // 2
    spec = pl.BlockSpec((1, rows, chunk), lambda n: (tile(n) // per, 0, lax.rem(tile(n), per)))
    at = lambda n: jnp.maximum(n - gates, 0)
    return pl.pallas_call(
        functools.partial(expert_out_kernel, gates, each),
        grid=(4 * each,),
        in_specs=[
            pl.BlockSpec(
                (rows, chunk),
                functools.partial(lambda q, n: (0, jnp.clip(n - q * each, 0, each - 1)), q),
            )
            for q in range(4)
        ],
        out_specs=[
            spec,
            spec,
            pl.BlockSpec((1, chunk, rows), lambda n: (at(n) // per, lax.rem(at(n), per), 0)),
        ],
        out_shape=[jax.ShapeDtypeStruct((held, rows, inner), f32)] * 2
        + [jax.ShapeDtypeStruct((held, inner, rows), f32)],
        compiler_params=params(),
        cost_estimate=cost(0, 8 * 2**20),
    )(*quarters)


def last_sum(refs):
    total = refs[0][...].astype(f32)
    for ref in refs[1:]:
        total = total + ref[...].astype(f32)
    return total


def dense_out_kernel(count, *refs):
    total = last_sum(refs[:count])
    out_ref, query_ref, key_ref, value_ref = refs[count:]
    wide = out_ref.shape[1]
    out_ref[...] = total[:, :wide]
    query_ref[...] = total[:, wide : 2 * wide]
    for g in range(KVH):
        first = 2 * wide + 2 * g * HD
        key_ref[:, g * HD : (g + 1) * HD] = total[:, first : first + HD]
        value_ref[:, g * HD : (g + 1) * HD] = total[:, first + HD : first + 2 * HD]


def dense_out(terms, wide):
    rows = terms[0].shape[0]
    shapes = [wide, wide, KVH * HD, KVH * HD]
    return pl.pallas_call(
        functools.partial(dense_out_kernel, len(terms)),
        out_shape=[jax.ShapeDtypeStruct((rows, n), f32) for n in shapes],
        compiler_params=params(),
        cost_estimate=cost(0, 2**20),
    )(*terms)


def shared_out_kernel(count, chunk, *refs):
    total = last_sum(refs[:count])
    gate_ref, up_ref, down_ref = refs[count:]
    rows = gate_ref.shape[0]
    for n in range(gate_ref.shape[1] // chunk):
        cut = slice(n * chunk, (n + 1) * chunk)
        gate_ref[:, cut] = total[:rows, 2 * n * chunk : (2 * n + 1) * chunk]
        up_ref[:, cut] = total[:rows, (2 * n + 1) * chunk : (2 * n + 2) * chunk]
    down_ref[...] = total[rows : rows + down_ref.shape[0], : down_ref.shape[1]]


def shared_grads(terms, gate, down, chunk=256):
    return pl.pallas_call(
        functools.partial(shared_out_kernel, len(terms), chunk),
        out_shape=[jax.ShapeDtypeStruct(v, f32) for v in (gate, gate, down)],
        compiler_params=params(),
        cost_estimate=cost(0, 2**20),
    )(*terms)


def hold(values, after):
    count = len(values)
    return pl.pallas_call(
        lambda *_: None,
        in_specs=[pl.BlockSpec(memory_space=pl.ANY)] * (count + len(after)),
        out_specs=[pl.BlockSpec(memory_space=pl.ANY)] * count,
        out_shape=[jax.ShapeDtypeStruct(v.shape, v.dtype) for v in values],
        input_output_aliases={i: i for i in range(count)},
        compiler_params=params(),
        cost_estimate=cost(0, 0),
    )(*values, *after)


def swap_inner(value, axis):
    size = lax.axis_size(axis)
    return lax.ppermute(value, axis, [(i, i ^ 1) for i in range(size)])


def shift_outer(value, axis, by):
    outer = lax.axis_size(axis) // 2
    perm = [(o * 2 + i, ((o + by) % outer) * 2 + i) for o in range(outer) for i in range(2)]
    return lax.ppermute(value, axis, perm)


def ring_step(value, by):
    n_ctx, n_exp = lax.axis_size("ctx"), lax.axis_size("exp")
    outer = n_exp // 2
    perm = []
    for c in range(n_ctx):
        way = by if c % 2 == 0 else -by
        for o in range(outer):
            for i in range(2):
                perm.append((c * n_exp + o * 2 + i, c * n_exp + ((o + way) % outer) * 2 + i))
    return lax.ppermute(value, BOTH, perm)


def by_blocks(value, together):
    return value.reshape(-1, together * value.shape[1], value.shape[2])


def spread_outer(value):
    moved, out = value, []
    for _ in range(1, lax.axis_size("ctx") // 2):
        moved = shift_outer(moved, "ctx", 1)
        out.append(moved)
    return out, swap_inner(value, "ctx")


def spread_inner(moved):
    return [swap_inner(v, "ctx") for v in moved]


def outer_blocks(value):
    moved, out = value, []
    for _ in range(1, lax.axis_size("ctx") // 2):
        moved = shift_outer(moved, "ctx", 1)
        out.append(moved)
    return out


def inner_blocks(value, moved):
    return swap_inner(jnp.concatenate([value] + moved, axis=0), "ctx")


def all_blocks(value, moved, across):
    out = []
    for k, v in enumerate([value] + moved):
        out += [(v, 0), (across, k)]
    return out


def spread_all(value, moved, across, moved_across):
    blocks = [value, across]
    for a, b in zip(moved, moved_across):
        blocks += [a, b]
    return blocks


def paired_blocks(value, across, moved, moved_across):
    out = [(value, 0), (across, 0)]
    for a, b in zip(moved, moved_across):
        out += [(a, 0), (b, 0)]
    return out


class Shared:
    def __init__(self, pos, kept, got):
        self.pos = pos
        self.outer, self.levels = lax.axis_size("ctx") // 2, lax.axis_size("exp") // 2
        self.rows, self.wide = kept.shape[1:]
        self.pair = lambda v: v.reshape(-1, 2 * self.rows, self.wide)
        self.terms = [self.pair(v) for v in (kept, got)]
        self.together = 1
        self.steps = self.levels

    def _sum(self, d, rows, inner, moved=()):
        at = lambda i, pos: lax.rem(pos[0] + d, self.outer) * self.steps + i
        terms = [(v, lambda i, pos: (at(i, pos), inner(pos), 0)) for v in self.terms]
        for parts in moved:
            for k, v in enumerate(parts):
                terms.append((self.pair(v), lambda i, pos: (0, inner(pos), 0), k))
        return terms, (self.together, rows, self.wide)

    def first(self):
        out = []
        for d in range(1, self.outer):
            terms, block = self._sum(d, 2 * self.rows, lambda pos: 0)
            outputs = []
            for k in range(self.steps):
                part = [(v, functools.partial(lambda f, k, i, pos: f(k, pos), f, k)) for v, f in terms]
                outputs.append((bf16, block, part))
            out.append(sums(self.pos, 1, outputs))
        return out

    def second(self, moved, first, last):
        moved = [v[first:last] for v in moved]
        terms, block = self._sum(0, self.rows, lambda pos: 1 - pos[3], moved)
        later = lambda f: lambda i, pos: f(first + i, pos)
        terms = [(v, f, *o) if o else (v, later(f)) for v, f, *o in terms]
        return sums(self.pos, last - first, [(bf16, block, terms)])

    def total(self, moved, crossed):
        terms, block = self._sum(0, self.rows, lambda pos: pos[3], moved)
        at = 0
        for v in crossed:
            for k in range(v.shape[0]):
                terms.append((v, functools.partial(lambda k, i, pos: k, k), at))
                at += 1
        return sums(self.pos, self.steps, [(bf16, block, terms)])[0]


def z_take(total, d):
    levels = total.shape[0]
    return lax.dynamic_index_in_dim(total, (lax.axis_index("exp") // 2 + d) % levels, 0, False)


def z_send(total, d):
    return shift_outer(z_take(total, d), "exp", d)


def over_x(total):
    pairs = total.reshape((-1, 2) + total.shape[1:])
    return swap_inner(lax.dynamic_index_in_dim(pairs, 1 - lax.axis_index("exp") % 2, 1, False), "exp")


def mine_x(total):
    pairs = total.reshape((-1, 2) + total.shape[1:])
    return lax.dynamic_index_in_dim(pairs, lax.axis_index("exp") % 2, 1, False)


def over_z(pos, mine, arrived):
    levels, rows, wide = mine.shape
    outputs = []
    for d in range(levels):
        at = functools.partial(lambda d, i, pos: lax.rem(pos[2] + d, levels), d)
        outputs.append((bf16 if d else f32, (1, rows, wide), [(mine, at), (arrived, at)]))
    own, *sent = [v[0] for v in sums(pos, 1, outputs)]
    return [own] + [shift_outer(v, "exp", d + 1) for d, v in enumerate(sent)]


def expert_quarter(kept, got, q, row):
    steps = kept.shape[0] // (lax.axis_size("ctx") // 2)
    block = (steps, kept.shape[1], kept.shape[2] // 4)
    return block, [(v, lambda i, pos: (row(i, pos), 0, q)) for v in (kept, got)]


def expert_pieces(pos, kept, got, quarters):
    outputs = []
    for q in quarters:
        block, terms = expert_quarter(kept, got, q, straight)
        outputs.append((bf16, block, terms))
    return sums(pos, lax.axis_size("ctx") // 2, outputs)


def expert_row(d):
    outer = lax.axis_size("ctx") // 2
    return lambda i, pos: lax.rem(pos[0] + d, outer)


def expert_send(pos, kept, got, pieces, half):
    sent = []
    for d in range(1, lax.axis_size("ctx") // 2):
        row = expert_row(d)
        block, terms = expert_quarter(kept, got, 0, row)
        terms = [(v, lambda i, pos: (row(i, pos), 0, 2 * half + i)) for v, _ in terms]
        terms += [(pieces[2 * half + k], lambda i, pos: row(0, pos), k) for k in range(2)]
        sent += sums(pos, 2, [(bf16, block, terms)])
    return sent


def expert_move(sent):
    return [shift_outer(v, "ctx", d + 1) for d, v in enumerate(sent)]


def expert_total(pos, kept, got, pieces, arrived):
    row = expert_row(0)
    outputs = []
    for q in range(4):
        block, terms = expert_quarter(kept, got, q, row)
        at = functools.partial(lambda k, i, pos: k, q % 2)
        terms = terms + [(pieces[q], row)] + [(v, at) for v in arrived[q // 2]]
        outputs.append((bf16, block, terms))
    return [v.reshape(-1, v.shape[2]) for v in sums(pos, 1, outputs)]


def shards(
    layer_input,
    attn_gain,
    w_query,
    w_key,
    w_value,
    w_out,
    ffn_gain,
    shared_gate,
    shared_up,
    shared_down,
    expert_gate,
    expert_up,
    expert_down,
    routes,
    gate_logits,
    span_order,
    cotangent,
):
    x = layer_input[0]
    cot = cotangent[0]
    tokens, width = x.shape
    span_rows = tokens // 2
    n_ctx, n_exp = lax.axis_size("ctx"), lax.axis_size("exp")
    ctx_id, exp_id = lax.axis_index("ctx"), lax.axis_index("exp")
    local_experts, _, inner = expert_gate.shape
    expert_count = local_experts * n_exp

    levels = n_exp // 2
    pos = jnp.stack([ctx_id // 2, ctx_id % 2, exp_id // 2, exp_id % 2]).astype(jnp.int32)

    always = pos[0] < n_ctx
    ring = n_ctx // 2

    def region(work):
        made = jax.eval_shape(work)
        return lax.cond(always, work, lambda: jax.tree.map(lambda v: jnp.zeros(v.shape, v.dtype), made))

    gate_vals = jax.nn.softmax(gate_logits[0], axis=-1)
    named = routes[0][:, None, :] == jnp.arange(expert_count, dtype=jnp.int32)[None, :, None]
    row_gates = jnp.sum(jnp.where(named, gate_vals[:, None, :], 0.0), axis=-1)
    high = row_gates.astype(bf16)
    low = (row_gates - high.astype(f32)).astype(bf16)
    fill = lambda width: ((0, 0), (0, width - expert_count))
    cot_ring = [
        jnp.concatenate(
            [cot, jnp.pad(high, fill(LOW_LANE)), jnp.pad(low, fill(GATE_LANES - LOW_LANE))], axis=1
        )
    ]

    chunk, bands = 256, 3
    mine = lambda v: lax.dynamic_index_in_dim(v, pos[1], 0, keepdims=False)
    over_core = lambda v: swap_inner(v, "ctx")

    def fetch(k):
        return swap_inner(asked[k], "exp")

    def arranged(parts):
        return parts[inner // chunk :], parts[: inner // chunk]

    def ask():
        down = mine(expert_down)
        out = [down[n * chunk : (n + 1) * chunk] for n in range(inner // chunk)]
        gate, up = mine(expert_gate), mine(expert_up)
        band = width // bands
        for k in range(bands):
            cut = slice(k * band, (k + 1) * band)
            out.append(jnp.concatenate([gate[cut], up[cut]], axis=1))
        return out

    def gather_keys():
        normed, kv = keyvalue(x, attn_gain, w_key, w_value)
        moved, across = spread_outer(kv)
        queries = dot(normed, w_query).astype(bf16)
        asked = ask()
        keys = kv, moved, across, spread_inner(moved)
        return normed, keys, queries, ring_step(cot_ring[0], 1), asked, swap_inner(asked[0], "exp")

    normed, keys, queries, cot_next, asked, got = region(gather_keys)
    kv_blocks = spread_all(*keys)
    cot_ring.append(cot_next)
    fetched, crossed = [got], []

    def attention():
        attended, lse = attend(pos, span_order, queries, kv_blocks)
        middle, rows = middle_forward(x, attended, w_out, ffn_gain)
        moved = outer_blocks(normed), ring_step(cot_ring[1], 1), fetch(1), over_core(fetched[0])
        return attended, lse, middle, rows, over_core(normed), *moved

    attended, lse, middle, rows_low, across, normed_moved, cot_next, got, crossing = region(attention)
    normed_across = across
    cot_ring.append(cot_next)
    fetched.append(got)
    crossed.append(crossing)

    own_weights = (expert_gate, expert_up, expert_down)

    def own_part(ks, rows, part, parts, kept):
        return experts(pos, rows, [cot_ring[k] for k in ks], own_weights, part, parts, kept, True, bf16)

    def first():
        weights = (shared_gate[None], shared_up[None], shared_down[None])
        shared = experts(pos, [rows_low], [cot], weights, 0, 1, None, False, f32)
        more = spread_inner(normed_moved), fetch(2), over_core(fetched[1]), outer_blocks(attended)
        return ring_step(rows_low, 1), shared, *more

    rows_one, shared, across, got, crossing, attended_moved = region(first)
    fetched.append(got)
    crossed.append(crossing)
    normed_blocks = paired_blocks(normed, normed_across, normed_moved, across)
    (shared_out,), (shared_grad,), (shared_hidden, shared_dgu) = shared
    shared_pairs = [(rows_low, shared_dgu), (shared_hidden, cot)]

    def second():
        result = own_part([0], [rows_low], 2, 4, None)
        more = fetch(3), over_core(fetched[2]), [over_core(attended), *spread_inner(attended_moved)]
        return ring_step(rows_one, 1), result, halves(pos, shared_pairs), *more

    rows_two, (out_k, grad_k, kept), (shared_sent, shared_kept), got, crossing, across = region(second)
    attended_blocks = paired_blocks(attended, across[0], attended_moved, across[1:])
    fetched.append(got)
    crossed.append(crossing)
    out_own, grad_own = list(out_k), list(grad_k)

    def third():
        more = over_core(shared_sent), fetch(4), over_core(fetched[3])
        pair = own_part([1, 2], [rows_one, rows_two], 0, 2, kept)
        sent = Shared(pos, shared_kept, more[0]).first()
        return ring_step(rows_two, 1), pair, sent, *more

    rows_k, (out_k, grad_k, kept), shared_sent, shared_got, got, crossing = region(third)
    fetched.append(got)
    crossed.append(crossing)
    out_own += out_k
    grad_own += grad_k

    def over_y(parts, k):
        return [shift_outer(v[k], "ctx", d + 1) for d, v in enumerate(parts)]

    def fourth():
        moved = ring_step(cot_ring[2], 1)
        weights = [arranged(fetched), arranged(crossed + [over_core(fetched[4])])]
        half = levels // 2
        arrived = [over_y(shared_sent, k) for k in range(levels - 1)]
        out_a, grad_a, new = others(pos, kept[0], kept[1], weights, 0, 2, half, None)
        last = experts(pos, [rows_k], [moved], own_weights, 3, 4, kept, True, bf16)
        out_b, grad_b, new = others(pos, last[2][0], last[2][1], weights, 1, 2, half, new)
        return last, [out_b[0], *out_a, out_b[1]], [grad_b[0], *grad_a, grad_b[1]], new, arrived

    (out_k, grad_k, kept), out_other, grad_other, kept_other, got = region(fourth)
    shared_moved = [list(v) for v in zip(*got)]
    out_own += out_k
    grad_own += grad_k
    rows_all, cot_all, hid_own, dgu_own = kept
    hid_other, dgu_other = kept_other

    def back_one():
        moved = ring_step(row_sum([grad_own[3], grad_other[3]]), -1)
        (part,) = Shared(pos, shared_kept, shared_got).second(shared_moved, 0, levels // 2)
        made = expert_halves(pos, rows_all, cot_all, dgu_other, hid_other)
        return moved, made, swap_inner(part, "exp"), over_y(shared_sent, levels - 1)

    moved, (sent, kept_other), crossed, got = region(back_one)
    shared_moved = [v + [w] for v, w in zip(shared_moved, got)]
    shared_crossed = [crossed]

    def back_two():
        total = row_sum([grad_own[2], grad_other[2], moved])
        got = swap_inner(sent, "ctx")
        (part,) = Shared(pos, shared_kept, shared_got).second(shared_moved, levels // 2, levels)
        made = expert_halves(pos, rows_all, cot_all, dgu_own, hid_own)
        piece = expert_pieces(pos, kept_other, got, [0])[0]
        return ring_step(total, -1), got, made, piece, swap_inner(part, "exp")

    moved_two, got_other, (sent_own, kept_own), piece, crossed = region(back_two)
    shared_crossed.append(crossed)

    def back_three():
        total = row_sum([grad_own[1], grad_other[1], moved_two])
        made = expert_pieces(pos, kept_other, got_other, [1, 2, 3])
        shared_sum = Shared(pos, shared_kept, shared_got).total(shared_moved, shared_crossed)
        out_total = row_sum([out_own[3], out_other[3]])
        middle_grads = middle_back(
            [shared_grad, grad_own[0], grad_other[0], ring_step(total, -1)],
            middle,
            cot,
            ffn_gain,
            w_out,
        )
        moved = middle_grads, swap_inner(sent_own, "ctx"), swap_inner(piece, "exp")
        shared_z = [z_take(shared_sum, d) for d in range(levels)]
        return *moved, made, shared_z, out_total

    middle_grads, got_own, piece, made, shared_z, out_total = region(back_three)
    mgrad, mgrad_low, ffn_gain_grad, att_grad = middle_grads
    pieces = [piece, *made]

    def attention_back():
        dq, same, across = attend_back(pos, span_order, queries, att_grad, lse, kv_blocks)
        got = ring_step(out_total, -1), swap_inner(pieces[1], "exp"), shift_outer(shared_z[1], "exp", 1)
        mgrad_parts = mgrad_low, over_core(mgrad_low), outer_blocks(mgrad_low)
        return mgrad_parts, dq, same, across, *got

    mgrad_parts, dq, same, across, out_moved, piece, got = region(attention_back)
    pieces[1] = piece
    shared_parts = [shared_z[0], got]

    def dense_one():
        got = over_core(across)
        made = []
        for k in reversed(range(ring)):
            part = slice(k * tokens, (k + 1) * tokens)
            made = row_sum([same[part], got[part]] + made)
            if k:
                made = [shift_outer(made, "ctx", -1)]
        total = row_sum([out_own[2], out_other[2], out_moved])
        mgrad_blocks = paired_blocks(*mgrad_parts, spread_inner(mgrad_parts[2]))
        total_out = rows_product(pos, attended_blocks, mgrad_blocks)
        sent = expert_send(pos, kept_own, got_own, pieces, 0)
        total = row_sum([out_own[1], out_other[1], ring_step(total, -1)])
        return made, outer_blocks(dq), total_out, sent, total, swap_inner(pieces[2], "exp")

    dkv, dq_moved, total_out, sent, out_total_two, piece = region(dense_one)
    pieces[2] = piece

    def dense_two():
        dkv_moved = outer_blocks(dkv)
        dkv_blocks = all_blocks(dkv, dkv_moved, inner_blocks(dkv, dkv_moved))
        dq_blocks = all_blocks(dq, dq_moved, inner_blocks(dq, dq_moved))
        total_query = rows_product(pos, normed_blocks, dq_blocks)
        total_kv = rows_product(pos, normed_blocks, dkv_blocks)
        back = input_back(dq, dkv, w_query, w_key, w_value, x, attn_gain, mgrad)
        moved = ring_step(out_total_two, -1), swap_inner(pieces[3], "exp"), expert_move(sent)
        return total_query, total_kv, back, *moved

    total_query, total_kv, (input_grad, attn_gain_grad), out_moved_three, piece, got = region(dense_two)
    pieces[3] = piece
    arrived = [got]

    def dense_three():
        devices = n_ctx * n_exp
        total = jnp.concatenate([total_out, total_query, total_kv], axis=2)
        got = expert_move(expert_send(pos, kept_own, got_own, pieces, 1))
        layer_out = row_sum([middle, shared_out, out_own[0], out_other[0], out_moved_three])
        more = [shift_outer(shared_z[d], "exp", d) for d in range(2, levels)]
        gains = jnp.stack(
            [attn_gain_grad.reshape(devices, -1), ffn_gain_grad.reshape(devices, -1)], axis=1
        )
        gains = lax.all_to_all(gains, BOTH, split_axis=0, concat_axis=0, tiled=True)
        return mine_x(total), over_x(total), got, layer_out, more, gains

    total, total_x, got, layer_out, more, gains = region(dense_three)
    shared_parts += more
    arrived.append(got)

    def dense_four():
        grads = expert_out(expert_total(pos, kept_own, got_own, pieces, arrived), inner)
        shape = lambda v: (v.shape[0] // (n_ctx * n_exp), v.shape[1])
        shared = shared_grads(
            shared_parts, shape(shared_gate), shape(shared_down)
        )
        dense = dense_out(over_z(pos, total, total_x), x.shape[1])
        return jnp.sum(gains, axis=0), shared, dense, grads

    gains, (sum_gate, sum_up, sum_down), dense, expert_grads = region(dense_four)
    sum_out, sum_query, sum_key, sum_value = dense
    return (
        layer_out[None],
        input_grad[None],
        gains[0],
        sum_query,
        sum_key,
        sum_value,
        sum_out,
        gains[1],
        sum_gate,
        sum_up,
        sum_down,
        *expert_grads,
    )


def solution(mesh):
    return jax.shard_map(
        shards,
        mesh=mesh,
        in_specs=(
            P("exp", "ctx", None),
            P(),
            P(),
            P(),
            P(),
            P(),
            P(),
            P(),
            P(),
            P(),
            P("exp", None, None),
            P("exp", None, None),
            P("exp", None, None),
            P("exp", "ctx", None),
            P("exp", "ctx", None),
            P(),
            P("exp", "ctx", None),
        ),
        out_specs=(
            P("exp", "ctx", None),
            P("exp", "ctx", None),
            P(("ctx", "exp")),
            P(("ctx", "exp"), None),
            P(("ctx", "exp"), None),
            P(("ctx", "exp"), None),
            P(("ctx", "exp"), None),
            P(("ctx", "exp")),
            P(("ctx", "exp"), None),
            P(("ctx", "exp"), None),
            P(("ctx", "exp"), None),
            P("exp", "ctx", None),
            P("exp", "ctx", None),
            P("exp", None, "ctx"),
        ),
        check_vma=False,
    )
```
